32 devices in a mesh: section: 2 (over core), rep: 2 (over x), shard: 8 (over z, y).
Axes of the slice: x: 2, y: 2, z: 4, core: 2. Of those that a mesh axis runs over, the one named last changes fastest.
Arguments:
- boundary: bfloat16 [2, 2, 1024, 768], P('section', None, ('rep', 'shard')), may hold values from -6 to 6
- seq_lengths: int32 [2, 16, 4], P(None, ('rep', 'shard')), may hold values from 1 to 32, 64 in all within a row
- routes: int32 [2, 2, 1024, 1], P('section', None, ('rep', 'shard')), may hold values from 0 to 3; in each aligned block of 64 rows (0 to 63, 64 to 127, ..., all dimensions but the last counted through in order) at most 17 rows name the same one
- qkv_proj: bfloat16 [2, 3, 768, 768], P('section', None, 'shard'), may hold values from -0.21875 to 0.21875
- out_proj: bfloat16 [2, 768, 768], P('section', 'shard'), may hold values from -0.875 to 0.875
- router: bfloat16 [2, 768, 4], P('section', 'shard'), may hold values from -0.15625 to 0.15625
- gains: bfloat16 [2, 2, 768], P('section', None, 'shard'), may hold values from 0.5 to 1.5
- rel_table: bfloat16 [2, 384], P('section', 'shard'), may hold values from -6 to 6
- expert_in: bfloat16 [2, 8, 768, 1536], P('section', 'shard', None, 'rep'), may hold values from -0.21875 to 0.21875
- expert_out: bfloat16 [2, 8, 1536, 768], P('section', 'shard', 'rep'), may hold values from -0.4375 to 0.4375
Outputs:
- boundary_out: float32 [2, 2, 1024, 768], P('section', None, ('rep', 'shard'))
- grad_qkv: float32 [2, 3, 768, 768], P('section', None, 'shard')
- grad_out_proj: float32 [2, 768, 768], P('section', 'shard')
- grad_router: float32 [2, 768, 4], P('section', 'shard')
- grad_gains: float32 [2, 2, 768], P('section', None, 'shard')
- grad_table: float32 [2, 384], P('section', 'shard')
- grad_expert_in: float32 [2, 8, 768, 1536], P('section', 'shard', None, 'rep')
- grad_expert_out: float32 [2, 8, 1536, 768], P('section', 'shard', 'rep')
The draws below stay inside these ranges and needn't reach their ends.
Inputs may be any that keep to these rules, and one draw needn't show every extreme that they name: `seq_lengths`: each device's 4 lengths of a micro-batch sum to 64. `routes`: in the 64 rows of one device in one micro-batch of one section no expert is named more than 17 times.
All inputs are finite; a program needn't handle non-finite values.
Results may differ from the reference program's by a relative error of at most 0.024.
Values may be sent and summed in bfloat16 or wider, within the bound.
No kernel may reach another device: no remote copies, remote signals or barrier semaphores. Data moves between devices by JAX's collectives and lax.ppermute only.
A program may use at most 128 MiB of HBM per device.

```python
import math
import jax
import jax.numpy as jnp
import numpy as np
from jax import lax

D = 768
HEADS = 12
HEAD = 64
FF = 3072
BUCKETS = 32
SPAN = 128
TOK_DEV = 64
SEQ_DEV = 4
MICRO = 2
SECTIONS = 2
EXPERTS = 4
CAP = 17
DATA = 16
TOKENS = 1024


def level_of(own_key, shape, shards, smallest, high):
    level = 1.0
    for axis_at, shards_of in shards:
        draws = jax.random.uniform(jax.random.fold_in(jax.random.fold_in(own_key, 6), axis_at), (shards_of,), jnp.float32, smallest / len(shards), high / len(shards))
        level = level * jnp.repeat(jnp.exp(draws), shape[axis_at] // shards_of).reshape((-1,) + (1,) * (len(shape) - 1 - axis_at))
    return level


def profile(amount, total, bound, skew):
    loads = [(1 << 20) // math.isqrt(grade ** skew) + 1 for grade in range(2, amount + 1)]
    surplus, holding = total - bound - (amount - 1), [1] * (amount - 1)
    while surplus > 0:
        movable = [i for i in range(amount - 1) if holding[i] < bound]
        whole, remaining = sum([loads[i] for i in movable]), surplus
        for i in movable:
            more = min(bound - holding[i], max(1, remaining * loads[i] // whole), surplus)
            holding[i] = holding[i] + more
            surplus = surplus - more
    return np.array([bound] + holding)


def uneven(stream_key, number_of, total, bound, slope):
    if number_of == 2:
        one = jax.random.randint(stream_key, (), max(1, total - bound), min(bound, total - 1) + 1)
        return jnp.stack([one, total - one])
    tallies = jnp.asarray(profile(number_of, total, bound, slope), jnp.int32)
    pairs = (number_of - 1) // 2
    source_of, receiver = tallies[1:1 + 2 * pairs:2], tallies[2:2 + 2 * pairs:2]
    slack = jnp.minimum(source_of - 1, bound - receiver)
    shifted = jax.random.randint(jax.random.fold_in(stream_key, 1), (pairs,), 0, 1 << 20) % (slack + 1)
    tallies = tallies.at[1:1 + 2 * pairs:2].set(source_of - shifted).at[2:2 + 2 * pairs:2].set(receiver + shifted)
    return tallies[jax.random.permutation(jax.random.fold_in(stream_key, 2), number_of)]


def routed_block(own_key, own, number, rows, amount, top, limit, lean):
    ranking = jax.random.permutation(own_key, amount)
    heavy_load, usual = shares(amount, rows * top, limit, lean, True), shares(amount, rows * top, limit, lean, False)
    places = jnp.arange(amount)

    def named(tallies, rotation):
        used = int((tallies > 0).sum())
        fixed = max(1, used // 4)
        shifted = fixed + (places - fixed + rotation * (used - fixed)) % max(1, amount - fixed)
        return jnp.zeros((amount,), jnp.int32).at[ranking[jnp.where(places < fixed, places, shifted)]].set(jnp.asarray(tallies, jnp.int32))

    tallies = jnp.where(number % 4 == 0, named(heavy_load, number // 4), named(usual, number - number // 4 - 1))
    mixed = jax.random.permutation(jax.random.fold_in(own, 3), amount)
    source_of, receiver = mixed[0:amount // 2 * 2:2], mixed[1:amount // 2 * 2:2]
    slack = jnp.minimum(tallies[source_of] - 1, limit - tallies[receiver]) // 2
    slack = jnp.where((source_of == ranking[0]) | (receiver == ranking[0]) | (tallies[receiver] == 0), 0, jnp.maximum(slack, 0))
    shifted = jax.random.randint(jax.random.fold_in(own, 4), (amount // 2,), 0, 1 << 20) % (slack + 1)
    tallies = tallies.at[source_of].add(-shifted).at[receiver].add(shifted)
    items = jnp.searchsorted(jnp.cumsum(tallies), jnp.arange(rows * top), side="right").astype(jnp.int32)
    table = items.reshape(top, rows).T
    table = table[jax.random.permutation(jax.random.fold_in(own, 1), rows)]
    rotation = jax.random.randint(jax.random.fold_in(own, 2), (rows, 1), 0, top)
    return jnp.take_along_axis(table, (jnp.arange(top)[None, :] + rotation) % top, axis=1)


def shares(number_of, total, reach, slope, full):
    portions = [(1 << 20) // math.isqrt(rank ** slope) + 1 for rank in range(1, number_of + 1)]
    largest = reach if full else min(reach, max(-(-total // number_of), total * portions[0] // sum(portions)))
    least = 1 if total - largest >= number_of - 1 else 0
    holding, rest = [largest] + [least] * (number_of - 1), total - largest - least * (number_of - 1)
    while rest > 0:
        movable = [i for i in range(1, number_of) if holding[i] < largest] or [i for i in range(1, number_of) if holding[i] < reach]
        mass, left = sum([portions[i] for i in movable]), rest
        for i in movable:
            extra = min(reach - holding[i], max(1, left * portions[i] // mass), rest)
            holding[i] = holding[i] + extra
            rest = rest - extra
    return np.array(holding)


def gaussian(key, shape, scale, reach, pieces=(), kind=jnp.bfloat16):
    array = scale * jax.random.normal(key, shape, jnp.float32)
    if pieces:
        array = array * level_of(key, shape, pieces, -0.22, 0.18)
    return jnp.clip(array, -reach, reach).astype(kind)


def setup_inputs(seed: int = 0) -> dict:
    seeds = jax.random.split(jax.random.key(seed), 11)
    boundary = gaussian(seeds[0], (2, MICRO, TOKENS, D), 1.0, 6.0, ((0, 2), (2, 16)))
    seq_lengths = jax.vmap(lambda own: uneven(own, SEQ_DEV, TOK_DEV, TOK_DEV // 2, 2))(jax.random.split(seeds[1], MICRO * DATA)).reshape((MICRO, DATA, SEQ_DEV)).astype(jnp.int32)
    routes_keys = jax.random.split(jax.random.fold_in(seeds[2], 1), SECTIONS * MICRO * TOKENS // TOK_DEV)
    routes_turns = jax.random.permutation(jax.random.fold_in(seeds[2], 3), SECTIONS * MICRO * TOKENS // TOK_DEV)
    routes = jax.vmap(lambda own, number: routed_block(jax.random.fold_in(seeds[2], 2), own, number, TOK_DEV, EXPERTS, 1, CAP, 1))(routes_keys, routes_turns).reshape((SECTIONS, MICRO, TOKENS, 1))
    qkv_proj = gaussian(seeds[3], (SECTIONS, 3, D, D), D ** -0.5, 0.21875, ((0, 2), (2, 8)))
    out_proj = gaussian(seeds[4], (SECTIONS, D, D), (D // 16) ** -0.5, 0.875, ((0, 2), (1, 8)))
    router = gaussian(seeds[5], (SECTIONS, D, EXPERTS), (2 * D) ** -0.5, 0.15625, ((0, 2), (1, 8)))
    gains = jnp.clip(1.0 + 0.1 * jax.random.normal(seeds[6], (SECTIONS, 2, D), jnp.float32), 0.5, 1.5).astype(jnp.bfloat16)
    rel_table = gaussian(seeds[7], (SECTIONS, BUCKETS * HEADS), 1.0, 6.0, ((0, 2), (1, 8)))
    expert_in = gaussian(seeds[8], (SECTIONS, 2 * EXPERTS, D, FF // 2), D ** -0.5, 0.21875, ((0, 2), (1, 8), (3, 2)))
    expert_out = gaussian(seeds[9], (SECTIONS, 2 * EXPERTS, FF // 2, D), (max(1, FF // (EXPERTS * EXPERTS))) ** -0.5, 0.4375, ((0, 2), (1, 8), (2, 2)))
    return dict(boundary=boundary, seq_lengths=seq_lengths, routes=routes, qkv_proj=qkv_proj, out_proj=out_proj, router=router, gains=gains, rel_table=rel_table, expert_in=expert_in, expert_out=expert_out)


EPSILON = 1e-06
NEGATIVE = -1e+30

@jax.custom_vjp
def low(v):
    return lax.optimization_barrier(v.astype(jnp.bfloat16)).astype(jnp.float32)

@jax.custom_vjp
def low_back(v):
    return v

def low_keep(v):
    return (low(v), None)

def low_pass(kept, grad):
    return (grad,)

def back_keep(v):
    return (v, None)

def back_low(kept, grad):
    return (low(grad),)
low.defvjp(low_keep, low_pass)
low_back.defvjp(back_keep, back_low)

def bucket_onehot(length, bucket_count, max_span):
    half_count = bucket_count // 2
    exact_count = half_count // 2
    table_rows = np.zeros((length * length, bucket_count), np.float32)
    for query_place in range(length):
        for key_place in range(length):
            offset = key_place - query_place
            base_bucket = half_count if offset > 0 else 0
            distance = abs(offset)
            if distance < exact_count:
                bucket = distance
            else:
                bucket = exact_count + int(math.log(distance / exact_count) / math.log(max_span / exact_count) * (half_count - exact_count))
                bucket = min(bucket, half_count - 1)
            table_rows[query_place * length + key_place, base_bucket + bucket] = 1.0
    return table_rows

def hdot(left_side, right_side):
    return jnp.dot(left_side, right_side, precision=lax.Precision.HIGHEST)

def rms_norm(values, gain_row):
    return values * lax.rsqrt(lax.optimization_barrier(jnp.mean(values * values, axis=-1, keepdims=True)) + EPSILON) * gain_row

def soft_max(scores):
    highest = lax.optimization_barrier(jnp.max(scores, axis=-1, keepdims=True))
    exponent = jnp.exp(scores - highest)
    return exponent / lax.optimization_barrier(jnp.sum(exponent, axis=-1, keepdims=True))

def segment_mask(seq_lengths, row_count):
    boundary_ends = jnp.cumsum(seq_lengths).astype(jnp.int32)
    position = jnp.arange(row_count, dtype=jnp.int32)
    segment = lax.optimization_barrier(jnp.sum((position[:, None] >= boundary_ends[None, :]).astype(jnp.int32), axis=1))
    return segment[:, None] == segment[None, :]

def section_layer(layer_in, weights, length_rows, route_ids):
    qkv_weight, out_weight, router_weight, gain_pair, table_flat, first_expert, second_expert = weights
    block_count = length_rows.shape[0]
    scale_factor = 1.0 / math.sqrt(HEAD)
    normed_in = low(rms_norm(layer_in, gain_pair[0]))
    projected = [low_back(low(hdot(normed_in, qkv_weight[part_slot]))) for part_slot in range(3)]
    onehot_rows = jnp.asarray(bucket_onehot(TOK_DEV, BUCKETS, SPAN))
    position_bias = hdot(onehot_rows, table_flat.reshape(BUCKETS, HEADS)).T.reshape(HEADS, TOK_DEV, TOK_DEV)
    blocked = [member_array.reshape(block_count, TOK_DEV, HEADS, HEAD) for member_array in projected]

    def attend(block_items):
        query_block, key_block, value_block, block_lengths = block_items
        same_seq = segment_mask(block_lengths, TOK_DEV)
        raw_scores = jnp.einsum('qhc,khc->hqk', query_block, key_block, precision=lax.Precision.HIGHEST) * scale_factor + position_bias
        raw_scores = low_back(raw_scores)
        scores = jnp.where(same_seq[None], raw_scores, NEGATIVE)
        attn_prob = low(soft_max(scores))
        return jnp.einsum('hqk,khc->qhc', attn_prob, value_block, precision=lax.Precision.HIGHEST).reshape(TOK_DEV, HEADS * HEAD)
    context = lax.map(jax.checkpoint(attend), (blocked[0], blocked[1], blocked[2], length_rows))
    context = low_back(low(context.reshape(-1, HEADS * HEAD)))
    middle = layer_in + low_back(hdot(context, out_weight))
    normed_mid = low(rms_norm(middle, gain_pair[1]))
    router_prob = soft_max(hdot(normed_mid, router_weight))
    member = (route_ids[:, None] == jnp.arange(EXPERTS, dtype=jnp.int32)[None, :]).astype(jnp.int32)
    gate_prob = lax.optimization_barrier(jnp.sum(router_prob * member.astype(router_prob.dtype), axis=1))
    blocked_member = member.reshape(block_count, TOK_DEV, EXPERTS)
    slot_index = lax.optimization_barrier(jnp.sum((jnp.cumsum(blocked_member, axis=1) - 1) * blocked_member, axis=2)).reshape(-1).astype(jnp.int32)
    device_slot = (jnp.arange(TOKENS, dtype=jnp.int32) // TOK_DEV).astype(jnp.int32)
    target_row = (route_ids * (block_count * CAP) + device_slot * CAP + slot_index).astype(jnp.int32)
    buffer_rows = jnp.zeros((EXPERTS * block_count * CAP, D), normed_mid.dtype).at[target_row].set(normed_mid)
    full_in = first_expert.reshape(EXPERTS, 2, D, FF // 2).transpose(0, 2, 1, 3).reshape(EXPERTS, D, FF)
    full_out = second_expert.reshape(EXPERTS, FF, D)

    def run_expert(expert_items):
        rows_in, weight_first, weight_second = expert_items
        hidden_pre = low_back(hdot(rows_in, weight_first))
        return hdot(low(jax.nn.gelu(hidden_pre)), weight_second)
    expert_rows = lax.map(jax.checkpoint(run_expert), (buffer_rows.reshape(EXPERTS, block_count * CAP, D), full_in, full_out))
    expert_out = low_back(expert_rows.reshape(-1, D)[target_row])
    return middle + gate_prob[:, None] * expert_out

def reference(boundary, seq_lengths, routes, qkv_proj, out_proj, router, gains, rel_table, expert_in, expert_out):
    inputs = boundary[0].astype(jnp.float32)
    cotangent = boundary[1].astype(jnp.float32)
    weights = tuple((weight_array.astype(jnp.float32) for weight_array in (qkv_proj, out_proj, router, gains, rel_table, expert_in, expert_out)))

    def forward(input_rows, qkv_all, out_all, router_all, gain_all, table_all, first_all, second_all):
        outputs = []
        for micro_slot in range(MICRO):
            hidden = input_rows[micro_slot]
            for section_slot in range(SECTIONS):
                section_weights = tuple((weight_array[section_slot] for weight_array in (qkv_all, out_all, router_all, gain_all, table_all, first_all, second_all)))
                hidden = section_layer(hidden, section_weights, seq_lengths[micro_slot], routes[section_slot, micro_slot, :, 0])
                if section_slot < SECTIONS - 1:
                    hidden = low_back(low(hidden))
            outputs.append(hidden)
        return jnp.stack(outputs)
    result, pull_back = jax.vjp(forward, inputs, *weights)
    grads = pull_back(cotangent)
    return (jnp.stack([grads[0], result]), grads[1], grads[2], grads[3], grads[4], grads[5], grads[6], grads[7])
```

```python
import functools
import math

import jax
import jax.numpy as jnp
import numpy as np
from jax import lax
from jax.experimental import pallas as pl
from jax.experimental.pallas import tpu as pltpu
from jax.sharding import Mesh, PartitionSpec as P

HEADS = 12
HEAD = 64
BUCKETS = 32
SPAN = 128
PAIRS = HEADS // 2
EPSILON = 1e-06
NEGATIVE = -1e30
SCALE = 1.0 / math.sqrt(HEAD)
LANES = 128
PLANE = ("rep", "half")
BF = jnp.bfloat16
F32 = jnp.float32
VM = pl.BlockSpec(memory_space=pltpu.VMEM)
SM = pl.BlockSpec(memory_space=pltpu.SMEM)
ANY = pl.BlockSpec(memory_space=pl.ANY)


def up(n, m):
    return -(-n // m) * m


def bucket_onehot(length):
    half_count = BUCKETS // 2
    exact_count = half_count // 2
    rows = np.zeros((length * length, BUCKETS), np.float32)
    for q in range(length):
        for k in range(length):
            offset = k - q
            base = half_count if offset > 0 else 0
            distance = abs(offset)
            if distance < exact_count:
                bucket = distance
            else:
                bucket = exact_count + int(
                    math.log(distance / exact_count)
                    / math.log(SPAN / exact_count)
                    * (half_count - exact_count)
                )
                bucket = min(bucket, half_count - 1)
            rows[q * length + k, base + bucket] = 1.0
    return rows


def mm(a, b):
    return jnp.dot(a, b, preferred_element_type=F32)


def mm_nt(a, b):
    return lax.dot_general(a, b, (((1,), (1,)), ((), ())), preferred_element_type=F32)


def mm_tn(a, b):
    return lax.dot_general(a, b, (((0,), (0,)), ((), ())), preferred_element_type=F32)


def inv_rms(v):
    return lax.rsqrt(jnp.mean(v * v, axis=-1, keepdims=True) + EPSILON)


def rms_back(v, gain, grad):
    r = inv_rms(v)
    scaled = grad * gain
    dv = r * scaled - v * (r * r * r) * jnp.mean(v * scaled, axis=-1, keepdims=True)
    return dv, jnp.sum(grad * v * r, axis=0, keepdims=True)


def tanh_parts(v):
    c = math.sqrt(2.0 / math.pi)
    return c, jnp.tanh(c * (v + 0.044715 * (v * v * v)))


def gelu(v):
    _, t = tanh_parts(v)
    return 0.5 * v * (1.0 + t)


def gelu_slope(v):
    c, t = tanh_parts(v)
    return 0.5 * (1.0 + t) + 0.5 * v * (1.0 - t * t) * (c * (1.0 + 3.0 * 0.044715 * (v * v)))


def stack_heads(pair, rows):
    lane = lax.broadcasted_iota(jnp.int32, (rows, LANES), 1)
    zero = jnp.zeros_like(pair)
    return jnp.concatenate(
        [jnp.where(lane < HEAD, pair, zero), jnp.where(lane < HEAD, zero, pair)], axis=0
    )


def pick_heads(stacked, rows):
    lane = lax.broadcasted_iota(jnp.int32, (rows, LANES), 1)
    return jnp.where(lane < HEAD, stacked[:rows], stacked[rows:])


def member_of(rc, rows):
    lane = lax.broadcasted_iota(jnp.int32, (rows, LANES), 1)
    return (lane == rc).astype(F32)


def put_rows(target_row, block, cap_pad, values, rows):
    slot = lax.broadcasted_iota(jnp.int32, (cap_pad, rows), 0) + block * cap_pad
    return mm((slot == target_row).astype(BF), values)


def take_rows(target_col, blocks, cap_pad, rows):
    total = None
    for i, block in enumerate(blocks):
        slot = lax.broadcasted_iota(jnp.int32, (rows, cap_pad), 1) + i * cap_pad
        part = mm((slot == target_col).astype(BF), block)
        total = part if total is None else total + part
    return total


class Weights:
    def __init__(self, refs, experts, slab, layer):
        self.refs, self.experts, self.slab, self.layer = refs, experts, slab, layer
        self.big = len(refs) == 1

    @staticmethod
    def scratch(count, experts, width):
        return [
            pltpu.VMEM((4, width, width), BF),
            pltpu.SemaphoreType.DMA((1 if count == 1 else count * experts,)),
        ]

    def copies(self, meta, scr, sem):
        if self.big:
            return [pltpu.make_async_copy(self.refs[0], scr, sem.at[0])]
        s, x, z, y = meta[0], meta[1], meta[2], meta[3]
        made = []
        for c in range(2):
            for m in range(4):
                for i in range(self.experts):
                    matrix = 2 * (x ^ (m >> 1)) + (s ^ c ^ self.layer)
                    source_z = lax.rem(z - i + self.experts, self.experts)
                    row = (source_z * 2 + (y ^ (m & 1))) * self.slab
                    made.append(
                        pltpu.make_async_copy(
                            self.refs[c * 4 + m].at[i],
                            scr.at[matrix, pl.ds(pl.multiple_of(row, self.slab), self.slab)],
                            sem.at[len(made)],
                        )
                    )
        return made


def forward_kernel(layer, experts, slab, cap_pad, n_ret, n_w, *refs):
    it = iter(refs)
    meta = next(it)
    if layer == 0:
        x_ref = next(it)
    else:
        mid0, probs0, rc0, tc0, g_ref = (next(it) for _ in range(5))
        ret = [next(it) for _ in range(n_ret)]
    gains, router, bm, rc, tr = (next(it) for _ in range(5))
    w = Weights([next(it) for _ in range(n_w)], experts, slab, layer)
    h1_ref, qkv_ref, p_ref, ctx_ref, mid_ref, h2_ref, probs_ref = (next(it) for _ in range(7))
    if layer == 1:
        x1_ref, y0_ref = next(it), next(it)
    rest = list(it)
    scr, sem = rest[-2:]
    disp = rest[:-2]
    copies = w.copies(meta, scr, sem)
    for copy in copies:
        copy.start()
    rows, width = h1_ref.shape
    if layer == 0:
        x = x_ref[...].astype(F32)
    else:
        blocks = [ret[i][...] for i in range(n_ret)] if n_ret > 1 else [
            ret[0][i] for i in range(experts)
        ]
        y0 = take_rows(tc0[...], blocks, cap_pad, rows)
        y0_ref[...] = y0
        gate0 = jnp.sum(probs0[...] * member_of(rc0[...], rows), axis=-1, keepdims=True)
        x1 = (mid0[...] + gate0 * y0).astype(BF)
        x1_ref[...] = x1
        x = x1.astype(F32)
    h1 = (x * inv_rms(x) * gains[0:1]).astype(BF)
    h1_ref[...] = h1
    for copy in copies:
        copy.wait()
    q = mm(h1, scr[0]).astype(BF)
    k = mm(h1, scr[1]).astype(BF)
    v = mm(h1, scr[2]).astype(BF)
    qkv_ref[0] = q
    qkv_ref[1] = k
    qkv_ref[2] = v
    contexts = []
    for pair in range(PAIRS):
        cols = slice(pair * LANES, (pair + 1) * LANES)
        sc = mm_nt(stack_heads(q[:, cols], rows), k[:, cols]) * SCALE + bm[pair]
        e = jnp.exp(sc - jnp.max(sc, axis=-1, keepdims=True))
        p = e / jnp.sum(e, axis=-1, keepdims=True)
        p_ref[pair] = p
        contexts.append(pick_heads(mm(p.astype(BF), v[:, cols]), rows))
    ctx = jnp.concatenate(contexts, axis=1).astype(BF)
    ctx_ref[...] = ctx
    mid = x + mm(ctx, scr[3])
    mid_ref[...] = mid
    h2 = (mid * inv_rms(mid) * gains[1:2]).astype(BF)
    h2_ref[...] = h2
    logits = mm(h2, router[...])
    lane = lax.broadcasted_iota(jnp.int32, (rows, LANES), 1)
    logits = jnp.where(lane < experts, logits, NEGATIVE)
    e = jnp.exp(logits - jnp.max(logits, axis=-1, keepdims=True))
    probs = e / jnp.sum(e, axis=-1, keepdims=True)
    probs_ref[...] = probs
    sent = [h2]
    if layer == 1:
        gate = jnp.sum(probs * member_of(rc[...], rows), axis=-1, keepdims=True)
        sent.append((gate * g_ref[...].astype(F32)).astype(BF))
    for i in range(experts):
        for part, values in enumerate(sent):
            block = put_rows(tr[...], i, cap_pad, values, rows).astype(BF)
            ref = disp[i] if len(disp) > 1 else disp[0].at[i]
            if layer == 1:
                ref[part] = block
            else:
                ref[...] = block


def backward_kernel(layer, experts, slab, cap_pad, n_ret, n_w, *refs):
    it = iter(refs)
    meta, g_ref, x_ref, h1_ref, qkv_ref, p_ref, ctx_ref, mid_ref, h2_ref, probs_ref = (
        next(it) for _ in range(10)
    )
    gains, router, rc, tc = (next(it) for _ in range(4))
    if layer == 0:
        y_ref = next(it)
    else:
        probs0, rc0, tr0 = (next(it) for _ in range(3))
    ret = [next(it) for _ in range(n_ret)]
    w = Weights([next(it) for _ in range(n_w)], experts, slab, layer)
    dx_ref, ds_ref, ex_ref = (next(it) for _ in range(3))
    factors = [next(it) for _ in range(4)]
    if layer == 1:
        out_ref = next(it)
    rest = list(it)
    scr, sem, right, left = rest[-4:]
    disp = rest[:-4]
    copies = w.copies(meta, scr, sem)
    for copy in copies:
        copy.start()
    rows, width = h1_ref.shape
    g = g_ref[...].astype(F32)
    mid = mid_ref[...]
    probs = probs_ref[...]
    member = member_of(rc[...], rows)
    gate = jnp.sum(probs * member, axis=-1, keepdims=True)

    def blocks(part):
        if layer == 0:
            return [r[...] for r in ret] if n_ret > 1 else [ret[0][i] for i in range(experts)]
        return [r[part] for r in ret] if n_ret > 1 else [ret[0][i, part] for i in range(experts)]

    if layer == 0:
        y = y_ref[...]
        dh2 = take_rows(tc[...], blocks(0), cap_pad, rows)
    else:
        y = take_rows(tc[...], blocks(0), cap_pad, rows)
        dh2 = take_rows(tc[...], blocks(1), cap_pad, rows)
        out_ref[...] = mid + gate * y
    dgate = jnp.sum(g * y, axis=-1, keepdims=True)
    dlogits = probs * (dgate * (member - gate))
    high = dlogits.astype(BF)
    low = (dlogits - high.astype(F32)).astype(BF)
    dh2 = dh2 + mm_nt(high, router[...]) + mm_nt(low, router[...])
    dmid, dgain1 = rms_back(mid, gains[1:2], dh2)
    dmid = dmid + g
    h2 = h2_ref[...]
    drouter = mm_tn(high, h2) + mm_tn(low, h2)
    da = dmid.astype(BF)
    right[3] = da
    for copy in copies:
        copy.wait()
    dctx = mm_nt(da, scr[3]).astype(BF)
    grads = ([], [], [])
    for pair in range(PAIRS):
        cols = slice(pair * LANES, (pair + 1) * LANES)
        p = p_ref[pair]
        qs = stack_heads(qkv_ref[0, :, cols], rows)
        ds_heads = stack_heads(dctx[:, cols], rows)
        dp = mm_nt(ds_heads, qkv_ref[2, :, cols])
        ds = (p * (dp - jnp.sum(p * dp, axis=-1, keepdims=True))).astype(BF)
        ds_ref[pair] = ds
        grads[0].append(pick_heads(mm(ds, qkv_ref[1, :, cols]) * SCALE, rows))
        grads[1].append(mm_tn(ds, qs) * SCALE)
        grads[2].append(mm_tn(p.astype(BF), ds_heads))
    dh1 = None
    for j in range(3):
        dj = jnp.concatenate(grads[j], axis=1).astype(BF)
        right[j] = dj
        part = mm_nt(dj, scr[j])
        dh1 = part if dh1 is None else dh1 + part
    dx, dgain0 = rms_back(x_ref[...].astype(F32), gains[0:1], dh1)
    dx = dx + dmid
    dx_ref[...] = dx
    ex_ref[...] = jnp.zeros_like(ex_ref)
    ex_ref[0:experts] = drouter[0:experts]
    ex_ref[experts:experts + 1] = dgain0
    ex_ref[experts + 1:experts + 2] = dgain1
    if layer == 1:
        gate0 = jnp.sum(probs0[...] * member_of(rc0[...], rows), axis=-1, keepdims=True)
        dy0 = (gate0 * dx.astype(BF).astype(F32)).astype(BF)
        for i in range(experts):
            block = put_rows(tr0[...], i, cap_pad, dy0, rows).astype(BF)
            ref = disp[i] if len(disp) > 1 else disp[0].at[i]
            ref[...] = block
    left[0] = h1_ref[...]
    left[1] = ctx_ref[...]
    place = meta[4]
    for m in range(4):
        target = place ^ m
        factors[m][0:rows] = left[jnp.where(target == 3, 1, 0)]
        factors[m][rows:] = right[target]


def pack_kernel(n, cap, parts, *refs):
    out = refs[-1]
    blocks = refs[:-1]
    packed = out.shape[-2]
    cap_pad = blocks[0].shape[-2]
    for part in range(parts):
        total = None
        for i in range(n):
            block = blocks[i][part] if len(blocks) > 1 else blocks[0][i, part]
            row = lax.broadcasted_iota(jnp.int32, (packed, cap_pad), 0)
            slot = lax.broadcasted_iota(jnp.int32, (packed, cap_pad), 1)
            pick = ((row == slot + i * cap) & (slot < cap)).astype(BF)
            moved = mm(pick, block)
            total = moved if total is None else total + moved
        out[part] = total.astype(BF)


def unpack_kernel(n, cap, parts, *refs):
    sums, outs = refs[:4], refs[4:]
    packed = sums[0].shape[-2]
    cap_pad = outs[0].shape[-2]
    for part in range(parts):
        total = (
            sums[0][part].astype(F32)
            + sums[1][part].astype(F32)
            + sums[2][part].astype(F32)
            + sums[3][part].astype(F32)
        ).astype(BF)
        for i in range(n):
            row = lax.broadcasted_iota(jnp.int32, (cap_pad, packed), 1)
            slot = lax.broadcasted_iota(jnp.int32, (cap_pad, packed), 0)
            pick = ((row == slot + i * cap) & (slot < cap)).astype(BF)
            block = mm(pick, total).astype(BF)
            if len(outs) > 1:
                outs[i][part] = block
            else:
                outs[0][i, part] = block


def expert_weights(layer, meta, own, other, scr, sem):
    for which in range(2):
        @pl.when(meta[0] == layer)
        def _():
            pltpu.make_async_copy(own[which], scr.at[which], sem.at[which]).start()

        @pl.when(meta[0] != layer)
        def _():
            pltpu.make_async_copy(other[which], scr.at[which], sem.at[which]).start()

    def wait(which):
        pltpu.make_async_copy(own[which], scr.at[which], sem.at[which]).wait()

    return wait


def expert_forward_kernel(layer, both, *refs):
    meta, c0, c1, c2, c3, in_own, in_other, out_own, out_other = refs[:9]
    outs = refs[9:13]
    rest = list(refs[13:])
    scr, sem = rest[-2:]
    saved = rest[:-2]
    wait = expert_weights(layer, meta, (in_own, out_own), (in_other, out_other), scr, sem)
    packed = c0.shape[-2]
    rows = jnp.concatenate([c[0] for c in (c0, c1, c2, c3)], axis=0)
    wait(0)
    pre = mm(rows, scr[0])
    act = gelu(pre).astype(BF)
    saved[0][...] = rows
    saved[1][...] = act
    wait(1)
    y = mm(act, scr[1])
    for m in range(4):
        outs[m][0] = y[m * packed:(m + 1) * packed].astype(BF)
    if both:
        grad_rows = jnp.concatenate([c[1] for c in (c0, c1, c2, c3)], axis=0)
        dpre = (mm_nt(grad_rows, scr[1]) * gelu_slope(pre)).astype(BF)
        saved[2][...] = grad_rows
        saved[3][...] = dpre
        dh = mm_nt(dpre, scr[0])
        for m in range(4):
            outs[m][1] = dh[m * packed:(m + 1) * packed].astype(BF)
    else:
        saved[2][...] = pre


def expert_backward_kernel(layer, *refs):
    meta, c0, c1, c2, c3, in_own, in_other, out_own, out_other, pre_ref = refs[:10]
    outs = refs[10:14]
    rows_ref, dpre_ref, scr, sem = refs[14:]
    wait = expert_weights(layer, meta, (in_own, out_own), (in_other, out_other), scr, sem)
    packed = c0.shape[-2]
    grad_rows = jnp.concatenate([c[0] for c in (c0, c1, c2, c3)], axis=0)
    rows_ref[...] = grad_rows
    slope = gelu_slope(pre_ref[...])
    wait(1)
    dpre = (mm_nt(grad_rows, scr[1]) * slope).astype(BF)
    dpre_ref[...] = dpre
    wait(0)
    dh = mm_nt(dpre, scr[0])
    for m in range(4):
        outs[m][0] = dh[m * packed:(m + 1) * packed].astype(BF)


def expert_grads_kernel(rows, dpre, act, grad_rows, gin, gout):
    gin[...] = mm_tn(rows[...], dpre[...])
    gout[...] = mm_tn(act[...], grad_rows[...])


def factor_kernel(experts, slab, rows, meta, f0, f1, f2, f3, ex, tab, keep, send):
    factors = (f0, f1, f2, f3)
    left = jnp.concatenate([f[0:rows] for f in factors], axis=0)
    right = jnp.concatenate([f[rows:] for f in factors], axis=0)
    grad = mm_tn(left, right).astype(BF)
    s, z = meta[0], meta[2]
    extra = jnp.where(
        lax.broadcasted_iota(jnp.int32, ex.shape, 0) == experts + 2, tab[...], ex[...]
    )
    pad = jnp.zeros((16, grad.shape[1] - LANES), F32)
    for shard in range(2 * experts):
        at = lax.rem(shard // 2 - z + experts, experts)
        wide = jnp.concatenate(
            [extra[:, shard * slab:(shard + 1) * slab], jnp.zeros((16, LANES - slab), F32)], axis=1
        )
        block = jnp.concatenate([wide, pad], axis=1).astype(BF)

        @pl.when(s == shard % 2)
        def _():
            keep[at, 0:slab] = grad[shard * slab:(shard + 1) * slab]
            keep[at, slab:] = block

        @pl.when(s != shard % 2)
        def _():
            send[at, 0:slab] = grad[shard * slab:(shard + 1) * slab]
            send[at, slab:] = block


def call(kernel, out_shapes, args, specs, scratch=(), flops=0, moved=0, name=None):
    return pl.pallas_call(
        kernel,
        out_shape=[jax.ShapeDtypeStruct(shape, dtype) for shape, dtype in out_shapes],
        in_specs=specs,
        out_specs=[VM] * len(out_shapes),
        scratch_shapes=list(scratch),
        compiler_params=pltpu.CompilerParams(vmem_limit_bytes=40 * 2**20),
        cost_estimate=pl.CostEstimate(flops=flops, bytes_accessed=moved, transcendentals=0),
        name=name,
    )(*args)


def shift(v, axis, by):
    n = lax.axis_size(axis)
    return lax.ppermute(v, axis, [(i, (i + by) % n) for i in range(n)])


def swap_section(v):
    return lax.ppermute(v, "section", [(0, 1), (1, 0)])


def plane_swap(v, mask):
    return lax.ppermute(v, PLANE, [(i, i ^ mask) for i in range(4)])


def plane_gather(v):
    return [v] + [plane_swap(v, m) for m in (1, 2, 3)]


def local(
    experts,
    boundary,
    seq_lengths,
    routes,
    qkv_proj,
    out_proj,
    router,
    gains,
    rel_table,
    expert_in,
    expert_out,
):
    big = experts > 8
    s = lax.axis_index("section")
    x_at = lax.axis_index("rep")
    z_at = lax.axis_index("expert")
    y_at = lax.axis_index("half")
    shards = 2 * experts
    rows, width = boundary.shape[2:]
    slab = qkv_proj.shape[2]
    table_slab = rel_table.shape[1]
    cap = max(2, rows // experts + 1)
    cap_pad = up(cap, 8)
    packed = up(experts * cap, 16)
    ff = expert_in.shape[3]
    first = s == 0
    meta = jnp.stack([s, x_at, z_at, y_at, 2 * x_at + y_at]).astype(jnp.int32)

    own = boundary[0]
    got = swap_section(own[1 - s])
    x0 = jnp.where(first, own[0], got)
    g1 = jnp.where(first, got, own[1])
    lengths = seq_lengths[s, 0]
    own_routes = routes[0, :, :, 0]
    got_routes = swap_section(own_routes[1 - s])
    route_list = [
        jnp.where(first, own_routes[0], got_routes),
        jnp.where(first, got_routes, own_routes[1]),
    ]

    if big:
        slabs = jnp.concatenate([qkv_proj[0], out_proj], axis=0)
        whole = lax.all_gather(slabs, ("expert", "half"), axis=1, tiled=True)
        layers = lax.all_gather(whole, "section", axis=0)
        attn_w = [[layers[0]], [layers[1]]]
    else:
        def matrix(j0, j1):
            a = out_proj[0] if j0 == 3 else qkv_proj[0, j0]
            b = out_proj[0] if j1 == 3 else qkv_proj[0, j1]
            return jnp.where(x_at == 0, a, b)

        mine, other = matrix(0, 2), swap_section(matrix(1, 3))
        attn_w = []
        for layer in range(2):
            piece = jnp.where(s == layer, mine, other)
            if layer == 1:
                piece, _ = lax.optimization_barrier((piece, attn_w[0][0]))
            gathered = jnp.stack([piece] + [shift(piece, "expert", i) for i in range(1, experts)])
            in_plane = plane_gather(gathered)
            attn_w.append(in_plane + [swap_section(v) for v in in_plane])
    other_in = swap_section(expert_in[0, 0])
    other_out = swap_section(expert_out[0, 0])
    expert_w = [expert_in[0, 0], other_in, expert_out[0, 0], other_out]

    small_rows = up(experts + 3, 8)
    table_row = jnp.zeros((1, slab), BF).at[0, :table_slab].set(rel_table[0])
    small = jnp.concatenate(
        [
            router[0].T,
            gains[0],
            table_row,
            jnp.zeros((small_rows - experts - 3, slab), BF),
        ]
    )
    if big:
        small_all = lax.all_gather(
            lax.all_gather(small, ("expert", "half"), axis=0), "section", axis=0
        )
    else:
        along = jnp.stack([small] + [shift(small, "expert", i) for i in range(1, experts)])
        along = jnp.stack([along, shift(along, "half", 1)])
        along = jnp.stack([along, swap_section(along)])
        at = jnp.arange(2 * shards, dtype=jnp.int32)
        layer_i, z_i, y_i = at // shards, (at % shards) // 2, at % 2
        source = ((layer_i ^ s) * 2 + (y_i ^ y_at)) * experts + (z_at - z_i + experts) % experts
        pick = (source[:, None] == at[None, :]).astype(BF)
        small_all = jnp.dot(
            pick, along.reshape(2 * shards, -1), preferred_element_type=F32
        ).astype(BF).reshape(2, shards, small_rows, slab)
    spread = jnp.asarray(bucket_onehot(rows), dtype=BF)
    ends = jnp.cumsum(lengths).astype(jnp.int32)
    position = jnp.arange(rows, dtype=jnp.int32)
    segment = jnp.sum((position[:, None] >= ends[None, :]).astype(jnp.int32), axis=1)
    same_seq = segment[:, None] == segment[None, :]
    params = []
    for layer in range(2):
        flat = small_all[layer].transpose(1, 0, 2)
        router_w = jnp.pad(
            flat[:experts].reshape(experts, width).T, ((0, 0), (0, LANES - experts))
        )
        gain_rows = flat[experts:experts + 2].reshape(2, width).astype(F32)
        table = flat[experts + 2, :, :table_slab].reshape(BUCKETS, HEADS)
        bias = jnp.dot(table.T, spread.T, preferred_element_type=F32).reshape(HEADS, rows, rows)
        bias = jnp.where(same_seq[None], bias, NEGATIVE).reshape(PAIRS, 2 * rows, rows)
        member = (
            route_list[layer][:, None] == jnp.arange(experts, dtype=jnp.int32)[None, :]
        ).astype(jnp.int32)
        slot = jnp.sum((jnp.cumsum(member, axis=0) - 1) * member, axis=1).astype(jnp.int32)
        block_at = route_list[layer] if big else (route_list[layer] - z_at + experts) % experts
        target = block_at * cap_pad + slot
        params.append(
            dict(
                gains=gain_rows,
                router=router_w,
                bias=bias,
                rc=route_list[layer][:, None],
                tr=target[None, :],
                tc=target[:, None],
            )
        )

    n_w = len(attn_w[0])
    n_ret = 1 if big else experts

    def message_shapes(parts):
        if big:
            return [((experts,) + parts + (cap_pad, width), BF)]
        return [(parts + (cap_pad, width), BF)] * experts

    def dispatch(blocks, parts):
        if big:
            arrived = lax.all_to_all(blocks[0], "expert", 0, 0, tiled=True)
            arrived = [arrived if parts == 2 else arrived[:, None]]
        else:
            arrived = [blocks[0]] + [shift(blocks[i], "expert", i) for i in range(1, experts)]
            arrived = arrived if parts == 2 else [a[None] for a in arrived]
        (joined,) = call(
            functools.partial(pack_kernel, experts, cap, parts),
            [((parts, packed, width), BF)],
            arrived,
            [VM] * len(arrived),
            moved=4 * packed * width,
            name="pack",
        )
        return plane_gather(joined)

    def come_back(partial, parts):
        sums = [partial[0]] + [plane_swap(partial[m], m) for m in (1, 2, 3)]
        shapes = (
            [((experts, parts, cap_pad, width), BF)]
            if big
            else [((parts, cap_pad, width), BF)] * experts
        )
        blocks = call(
            functools.partial(unpack_kernel, experts, cap, parts),
            shapes,
            sums,
            [VM] * 4,
            moved=4 * packed * width,
            name="unpack",
        )
        if big:
            back = lax.all_to_all(blocks[0], "expert", 0, 0, tiled=True)
            return [back if parts == 2 else back[:, 0]]
        back = [blocks[0]] + [shift(blocks[i], "expert", -i) for i in range(1, experts)]
        return back if parts == 2 else [b[0] for b in back]

    def forward(layer, extra):
        prm = params[layer]
        args = [meta] + extra + [prm["gains"], prm["router"], prm["bias"], prm["rc"], prm["tr"]]
        specs = [SM] + [VM] * (len(args) - 1) + [ANY] * n_w
        shapes = [
            ((rows, width), BF),
            ((3, rows, width), BF),
            ((PAIRS, 2 * rows, rows), F32),
            ((rows, width), BF),
            ((rows, width), F32),
            ((rows, width), BF),
            ((rows, LANES), F32),
        ]
        if layer == 1:
            shapes += [((rows, width), BF), ((rows, width), F32)]
        fixed = len(shapes)
        shapes += message_shapes((2,) if layer == 1 else ())
        outs = call(
            functools.partial(forward_kernel, layer, experts, slab, cap_pad, n_ret, n_w),
            shapes,
            args + attn_w[layer],
            specs,
            Weights.scratch(n_w, experts, width),
            flops=8 * rows * width * width,
            moved=8 * width * width,
            name="attention_forward",
        )
        names = ["h1", "qkv", "p", "ctx", "mid", "h2", "probs", "x1", "y0"][:fixed]
        return dict(zip(names, outs[:fixed])), outs[fixed:]

    def backward(layer, kept, x_in, g, returned, extra):
        prm = params[layer]
        args = [meta, g, x_in] + [
            kept[n] for n in ("h1", "qkv", "p", "ctx", "mid", "h2", "probs")
        ]
        args += [prm["gains"], prm["router"], prm["rc"], prm["tc"]] + extra + returned
        specs = [SM] + [VM] * (len(args) - 1) + [ANY] * n_w
        shapes = [
            ((rows, width), F32),
            ((PAIRS, 2 * rows, rows), BF),
            ((up(experts + 3, 16), width), F32),
        ] + [((2 * rows, width), BF)] * 4
        if layer == 1:
            shapes += [((rows, width), F32)] + message_shapes(())
        return call(
            functools.partial(backward_kernel, layer, experts, slab, cap_pad, n_ret, n_w),
            shapes,
            args + attn_w[layer],
            specs,
            Weights.scratch(n_w, experts, width)
            + [pltpu.VMEM((4, rows, width), BF), pltpu.VMEM((2, rows, width), BF)],
            flops=16 * rows * width * width,
            moved=8 * width * width,
            name="attention_backward",
        )

    expert_scratch = [pltpu.VMEM((2, width, ff), BF), pltpu.SemaphoreType.DMA((2,))]
    expert_specs = [SM] + [VM] * 4 + [ANY] * 4
    all_rows = 4 * packed

    def expert_forward(layer, joined, both):
        parts = 2 if both else 1
        shapes = [((parts, packed, width), BF)] * 4
        shapes += [((all_rows, width), BF), ((all_rows, ff), BF)]
        shapes += (
            [((all_rows, width), BF), ((all_rows, ff), BF)] if both else [((all_rows, ff), F32)]
        )
        outs = call(
            functools.partial(expert_forward_kernel, layer, both),
            shapes,
            [meta] + joined + expert_w,
            expert_specs,
            expert_scratch,
            flops=4 * all_rows * width * ff * parts,
            moved=4 * width * ff,
            name="expert_forward",
        )
        return outs[:4], outs[4:]

    def expert_grads(rows_in, dpre, act, grad_rows):
        return call(
            expert_grads_kernel,
            [((width, ff), F32), ((ff, width), F32)],
            [rows_in, dpre, act, grad_rows],
            [VM] * 4,
            flops=4 * all_rows * width * ff,
            moved=8 * width * ff,
            name="expert_grads",
        )

    def attention_grads(factors, ex, ds):
        table = jnp.dot(
            ds.reshape(HEADS, rows * rows), spread, preferred_element_type=F32
        ).T.reshape(shards, table_slab)
        tab = jnp.pad(table, ((0, 0), (0, slab - table_slab))).reshape(1, width)
        got = [factors[0]] + [plane_swap(factors[m], m) for m in (1, 2, 3)]
        keep, send = call(
            functools.partial(factor_kernel, experts, slab, rows),
            [((experts, slab + 16, width), BF)] * 2,
            [meta] + got + [ex, tab],
            [SM] + [VM] * 6,
            flops=8 * rows * width * width,
            moved=8 * width * width,
            name="attention_grads",
        )
        both = keep.astype(F32) + swap_section(send).astype(F32)
        parts = [both[i].astype(BF) for i in range(experts)]
        total = both[0]
        for i in range(1, experts):
            total = total + shift(parts[i], "expert", i).astype(F32)
        return total.astype(BF)

    kept0, blocks = forward(0, [x0])
    joined = dispatch(blocks, 1)
    partial, (rows0, act0, pre0) = expert_forward(0, joined, False)
    returned = come_back(partial, 1)

    kept1, blocks = forward(
        1, [kept0["mid"], kept0["probs"], params[0]["rc"], params[0]["tc"], g1] + returned
    )
    joined = dispatch(blocks, 2)
    partial, (rows1, act1, grows1, dpre1) = expert_forward(1, joined, True)
    gin1, gout1 = expert_grads(rows1, dpre1, act1, grows1)
    returned = come_back(partial, 2)

    outs = backward(
        1,
        kept1,
        kept1["x1"],
        g1,
        returned,
        [kept0["probs"], params[0]["rc"], params[0]["tr"]],
    )
    dx1, ds1, ex1 = outs[:3]
    factors1, out1, blocks = outs[3:7], outs[7], outs[8:]

    joined = dispatch(blocks, 1)
    shapes = [((1, packed, width), BF)] * 4 + [((all_rows, width), BF), ((all_rows, ff), BF)]
    outs = call(
        functools.partial(expert_backward_kernel, 0),
        shapes,
        [meta] + joined + expert_w + [pre0],
        expert_specs + [VM],
        expert_scratch,
        flops=4 * all_rows * width * ff,
        moved=4 * width * ff,
        name="expert_backward",
    )
    partial, (grows0, dpre0) = outs[:4], outs[4:]
    gin0, gout0 = expert_grads(rows0, dpre0, act0, grows0)
    returned = come_back(partial, 1)
    outs = backward(0, kept0, x0, dx1.astype(BF), returned, [kept1["y0"]])
    dx0, ds0, ex0 = outs[:3]
    factors0 = outs[3:7]

    traded = swap_section(jnp.where(first, out1, dx0))
    result_rows = jnp.stack([jnp.where(first, dx0, traded), jnp.where(first, traded, out1)])

    final_experts = []
    for g0, g1_ in ((gin0, gin1), (gout0, gout1)):
        recv = swap_section(jnp.where(first, g1_, g0).astype(BF))
        final_experts.append(jnp.where(first, g0, g1_) + recv.astype(F32))

    if big:
        own_factors = []
        for layer, (kept, ds, ex, fac) in enumerate(
            ((kept0, ds0, ex0, factors0), (kept1, ds1, ex1, factors1))
        ):
            place = 2 * x_at + y_at
            right = jnp.stack([fac[m][rows:] for m in range(4)])
            pieces = [
                jnp.sum(
                    jnp.where(
                        (jnp.arange(4) ^ place == j)[:, None, None], right, jnp.zeros_like(right)
                    ),
                    axis=0,
                )
                for j in range(4)
            ]
            lefts = [kept["h1"]] * 3 + [kept["ctx"]]
            grad = jnp.stack(
                [
                    lax.dot_general(
                        a, b, (((0,), (0,)), ((), ())), preferred_element_type=F32
                    )
                    for a, b in zip(lefts, pieces)
                ]
            )
            table = jnp.dot(
                ds.reshape(HEADS, rows * rows), spread, preferred_element_type=F32
            ).T.reshape(shards, table_slab)
            tab = jnp.pad(table, ((0, 0), (0, slab - table_slab))).reshape(1, width)
            lines = jnp.concatenate([ex[:experts + 2], tab])
            own_factors.append((grad, lines))
        grad = jnp.stack([own_factors[0][0], own_factors[1][0]]).astype(BF)
        lines = jnp.stack([own_factors[0][1], own_factors[1][1]])
        grad = lax.psum_scatter(grad, "section", scatter_dimension=0)
        lines = lax.psum_scatter(lines, "section", scatter_dimension=0)
        grad = lax.psum_scatter(grad, ("expert", "half"), scatter_dimension=1, tiled=True)
        grad = lax.psum(grad, "rep").astype(F32)
        lines = lax.psum(lines, ("rep", "expert", "half"))
        shard_at = z_at * 2 + y_at
        extra = lax.dynamic_slice_in_dim(lines, shard_at * slab, slab, axis=1)
    else:
        blocks = [
            attention_grads(factors0, ex0, ds0),
            attention_grads(factors1, ex1, ds1),
        ]
        arrived = []
        trade = ("section", "rep", "half")
        for a in range(2):
            message = jnp.where((y_at ^ a) == 0, blocks[0], blocks[1])
            for b in range(2):
                pairs = []
                for i in range(8):
                    si, xi, yi = i // 4, (i // 2) % 2, i % 2
                    pairs.append((i, (yi ^ a) * 4 + (xi ^ b) * 2 + si))
                arrived.append(lax.ppermute(message, trade, pairs))
        place = 2 * x_at + s
        order = [jnp.zeros((), jnp.int32)] * 4
        stacked = jnp.stack([arrived[0], arrived[2], arrived[1], arrived[3]])
        main = stacked[:, :slab].astype(F32)
        swapped = jnp.where(s == 0, main, main[jnp.array([1, 0, 3, 2])])
        grad = jnp.where(x_at == 0, swapped, swapped[jnp.array([2, 3, 0, 1])])
        extra = jnp.sum(stacked[:, slab:, :slab].astype(F32), axis=0)
    return (
        result_rows[None],
        grad[None, :3],
        grad[3][None],
        extra[:experts].T[None],
        extra[experts:experts + 2][None],
        extra[experts + 2, :table_slab][None],
        final_experts[0][None, None],
        final_experts[1][None, None],
    )


def solution(mesh):
    sections, reps, shards = (mesh.shape[n] for n in ("section", "rep", "shard"))
    experts = shards // 2
    split = Mesh(
        mesh.devices.reshape(sections, reps, experts, 2), ("section", "rep", "expert", "half")
    )
    shard = ("expert", "half")
    in_specs = (
        P("section", None, ("rep",) + shard, None),
        P(None, ("rep",) + shard, None),
        P("section", None, ("rep",) + shard, None),
        P("section", None, shard, None),
        P("section", shard, None),
        P("section", shard, None),
        P("section", None, shard),
        P("section", shard),
        P("section", shard, None, "rep"),
        P("section", shard, "rep", None),
    )
    out_specs = (
        P("section", None, ("rep",) + shard, None),
        P("section", None, shard, None),
        P("section", shard, None),
        P("section", shard, None),
        P("section", None, shard),
        P("section", shard),
        P("section", shard, None, "rep"),
        P("section", shard, "rep", None),
    )
    return jax.shard_map(
        functools.partial(local, experts),
        mesh=split,
        in_specs=in_specs,
        out_specs=out_specs,
        check_vma=False,
    )
```

```python
import functools
import math

import jax
import jax.numpy as jnp
import numpy as np
from jax import lax
from jax.experimental import pallas as pl
from jax.experimental.pallas import tpu as pltpu
from jax.sharding import Mesh, PartitionSpec as P

HEADS = 12
HEAD = 64
BUCKETS = 32
SPAN = 128
PAIRS = HEADS // 2
EPSILON = 1e-06
NEGATIVE = -1e30
SCALE = 1.0 / math.sqrt(HEAD)
LANES = 128
PLANE = ("rep", "half")
BF = jnp.bfloat16
F32 = jnp.float32
VM = pl.BlockSpec(memory_space=pltpu.VMEM)
SM = pl.BlockSpec(memory_space=pltpu.SMEM)
ANY = pl.BlockSpec(memory_space=pl.ANY)


def up(n, m):
    return -(-n // m) * m


def bucket_of(offset):
    half_count = BUCKETS // 2
    exact_count = half_count // 2
    base = half_count if offset > 0 else 0
    distance = abs(offset)
    if distance < exact_count:
        return base + distance
    bucket = exact_count + int(
        math.log(distance / exact_count)
        / math.log(SPAN / exact_count)
        * (half_count - exact_count)
    )
    return base + min(bucket, half_count - 1)


def table_places(shards, slab, table_slab):
    head_of = np.zeros((16, shards * slab), np.float32)
    offset_of = np.zeros((LANES, shards * slab), np.float32)
    for lane in range(shards * slab):
        shard, place = divmod(lane, slab)
        if place >= table_slab:
            continue
        bucket, head = divmod(shard * table_slab + place, HEADS)
        head_of[head, lane] = 1.0
        for d in range(LANES):
            if bucket_of(d if d < HEAD else d - LANES) == bucket:
                offset_of[d, lane] = 1.0
    return jnp.asarray(head_of, BF), jnp.asarray(offset_of, BF)


def mm(a, b):
    return jnp.dot(a, b, preferred_element_type=F32)


def mm_nt(a, b):
    return lax.dot_general(a, b, (((1,), (1,)), ((), ())), preferred_element_type=F32)


def mm_tn(a, b):
    return lax.dot_general(a, b, (((0,), (0,)), ((), ())), preferred_element_type=F32)


def inv_rms(v):
    return lax.rsqrt(jnp.mean(v * v, axis=-1, keepdims=True) + EPSILON)


def rms_back(v, gain, grad):
    r = inv_rms(v)
    scaled = grad * gain
    dv = r * scaled - v * (r * r * r) * jnp.mean(v * scaled, axis=-1, keepdims=True)
    return dv, jnp.sum(grad * v * r, axis=0, keepdims=True)


def tanh_parts(v):
    c = math.sqrt(2.0 / math.pi)
    return c, jnp.tanh(c * (v + 0.044715 * (v * v * v)))


def gelu(v):
    _, t = tanh_parts(v)
    return 0.5 * v * (1.0 + t)


def gelu_slope(v):
    c, t = tanh_parts(v)
    return 0.5 * (1.0 + t) + 0.5 * v * (1.0 - t * t) * (c * (1.0 + 3.0 * 0.044715 * (v * v)))


def stack_heads(pair, rows):
    lane = lax.broadcasted_iota(jnp.int32, (rows, LANES), 1)
    zero = jnp.zeros_like(pair)
    return jnp.concatenate(
        [jnp.where(lane < HEAD, pair, zero), jnp.where(lane < HEAD, zero, pair)], axis=0
    )


def pick_heads(stacked, rows):
    lane = lax.broadcasted_iota(jnp.int32, (rows, LANES), 1)
    return jnp.where(lane < HEAD, stacked[:rows], stacked[rows:])


def member_of(rc, experts):
    lane = lax.broadcasted_iota(jnp.int32, (rc.shape[0], experts), 1)
    return (lane == rc).astype(F32)


def target_slots(rc, rr, z, experts, cap_pad, big):
    rows = rc.shape[0]
    i = lax.broadcasted_iota(jnp.int32, (rows, rows), 0)
    j = lax.broadcasted_iota(jnp.int32, (rows, rows), 1)
    same = rc == rr
    before = jnp.where(same & (j < i), 1.0, 0.0)
    after = jnp.where(same & (i < j), 1.0, 0.0)

    def place(route, slot):
        if not big:
            route = jnp.where(route < z, route - z + experts, route - z)
        return route * cap_pad + slot.astype(jnp.int32)

    return (
        place(rc, jnp.sum(before, axis=1, keepdims=True)),
        place(rr, jnp.sum(after, axis=0, keepdims=True)),
    )


def small_lines(meta, small, layer, experts, slab):
    pieces = []
    for shard in range(2 * experts):
        if small.shape[0] == 2 and len(small.shape) == 4:
            block = small[layer, shard]
        else:
            at_z = lax.rem(meta[2] - shard // 2 + experts, experts)
            block = small[meta[0] ^ layer, meta[3] ^ (shard % 2), at_z]
        pieces.append(block.astype(F32))
    return jnp.concatenate(pieces, axis=1)


def same_sequence(meta, rows):
    shape = (2 * rows, rows)
    i = lax.broadcasted_iota(jnp.int32, shape, 0)
    i = jnp.where(i < rows, i, i - rows)
    j = lax.broadcasted_iota(jnp.int32, shape, 1)
    seg_i, seg_j = jnp.zeros(shape, jnp.int32), jnp.zeros(shape, jnp.int32)
    end = 0
    for n in range(5, 9):
        end = end + meta[n]
        seg_i = seg_i + (i >= end).astype(jnp.int32)
        seg_j = seg_j + (j >= end).astype(jnp.int32)
    return seg_i == seg_j


def position_bias(by_offset, head, rows):
    line = jnp.broadcast_to(by_offset[head:head + 1], (rows, LANES))
    return pltpu.roll(line, 0, 1, stride=1, stride_axis=0)[:, :rows]


def offset_sums(ds, flip):
    turned = mm(flip, ds)
    wide = jnp.concatenate([turned, jnp.zeros_like(turned)], axis=1)
    rolled = pltpu.roll(wide, 0, 1, stride=1, stride_axis=0)
    rows = ds.shape[0] // 2
    first = jnp.sum(rolled[rows:], axis=0, keepdims=True)
    second = jnp.sum(rolled[:rows], axis=0, keepdims=True)
    return [pltpu.roll(first, 1, 1), pltpu.roll(second, 1 + rows, 1)]


def split_two(v):
    high = v.astype(BF)
    return high, (v - high.astype(F32)).astype(BF)


def put_rows(target_row, block, cap_pad, values, rows):
    slot = lax.broadcasted_iota(jnp.int32, (cap_pad, rows), 0) + block * cap_pad
    return mm((slot == target_row).astype(BF), values)


def take_rows(target_col, blocks, cap_pad, rows):
    total = None
    for i, block in enumerate(blocks):
        slot = lax.broadcasted_iota(jnp.int32, (rows, cap_pad), 1) + i * cap_pad
        part = mm((slot == target_col).astype(BF), block)
        total = part if total is None else total + part
    return total


class Weights:
    def __init__(self, refs, plan, experts, slab, layer):
        self.refs, self.plan, self.experts, self.slab, self.layer = (
            refs, plan, experts, slab, layer,
        )

    @staticmethod
    def scratch(plan, width):
        return [pltpu.VMEM((4, width, width), BF), pltpu.SemaphoreType.DMA((max(1, len(plan)),))]

    def copies(self, meta, scr, sem, which):
        if not self.plan:
            return [pltpu.make_async_copy(self.refs[0], scr, sem.at[0])]
        x, z, y = meta[1], meta[2], meta[3]
        count = len(self.plan)
        made = []
        for n, (i, flip_y, flip_x, offset, held) in enumerate(self.plan):
            at_z = lax.rem(z - i + self.experts, self.experts)
            row = pl.multiple_of((at_z * 2 + (y ^ flip_y)) * self.slab, self.slab)
            matrix = 0 if held == 4 else 2 * (x ^ flip_x) + offset
            made.append(
                pltpu.make_async_copy(
                    self.refs[which * count + n],
                    scr.at[pl.ds(matrix, held), pl.ds(row, self.slab)],
                    sem.at[n],
                )
            )
        return made

    def start(self, meta, scr, sem):
        if not self.plan:
            self.copies(meta, scr, sem, 0)[0].start()
            return

        @pl.when(meta[0] == self.layer)
        def _():
            for copy in self.copies(meta, scr, sem, 0):
                copy.start()

        @pl.when(meta[0] != self.layer)
        def _():
            for copy in self.copies(meta, scr, sem, 1):
                copy.start()

    def wait(self, meta, scr, sem):
        for copy in self.copies(meta, scr, sem, 0):
            copy.wait()


def forward_kernel(layer, experts, slab, cap_pad, n_ret, n_w, plan, *refs):
    it = iter(refs)
    meta, small, rc_ref, rr_ref, head_of, offset_of = (next(it) for _ in range(6))
    if layer == 0:
        x_ref = next(it)
    else:
        mid0, probs0, g_ref = (next(it) for _ in range(3))
        ret = [next(it) for _ in range(n_ret)]
    w = Weights([next(it) for _ in range(n_w)], plan, experts, slab, layer)
    h1_ref, qkv_ref, p_ref, ctx_ref, mid_ref, h2_ref, probs_ref = (next(it) for _ in range(7))
    if layer == 1:
        x1_ref, y0_ref = next(it), next(it)
    rest = list(it)
    scr, sem = rest[-2:]
    disp = rest[:-2]
    big = not plan
    w.start(meta, scr, sem)
    rows, width = h1_ref.shape
    z = meta[2]
    rc = rc_ref[:, layer:layer + 1]
    _, tr = target_slots(rc, rr_ref[layer:layer + 1], z, experts, cap_pad, big)
    lines = small_lines(meta, small, layer, experts, slab)
    router = lines[:experts].astype(BF)
    table = (head_of[...].astype(F32) * lines[experts + 2:experts + 3]).astype(BF)
    by_offset = mm_nt(table, offset_of[...])
    keep = same_sequence(meta, rows)
    if layer == 0:
        x = x_ref[...].astype(F32)
    else:
        blocks = [ret[i][...] for i in range(n_ret)] if n_ret > 1 else [
            ret[0][i] for i in range(experts)
        ]
        rc0 = rc_ref[:, 0:1]
        tc0, _ = target_slots(rc0, rr_ref[0:1], z, experts, cap_pad, big)
        y0 = take_rows(tc0, blocks, cap_pad, rows)
        y0_ref[...] = y0
        gate0 = jnp.sum(probs0[...] * member_of(rc0, experts), axis=-1, keepdims=True)
        x1 = (mid0[...] + gate0 * y0).astype(BF)
        x1_ref[...] = x1
        x = x1.astype(F32)
    h1 = (x * inv_rms(x) * lines[experts:experts + 1]).astype(BF)
    h1_ref[...] = h1
    w.wait(meta, scr, sem)
    q = mm(h1, scr[0]).astype(BF)
    k = mm(h1, scr[1]).astype(BF)
    v = mm(h1, scr[2]).astype(BF)
    qkv_ref[0] = q
    qkv_ref[1] = k
    qkv_ref[2] = v
    contexts = []
    for pair in range(PAIRS):
        cols = slice(pair * LANES, (pair + 1) * LANES)
        bias = jnp.concatenate(
            [position_bias(by_offset, 2 * pair + n, rows) for n in range(2)], axis=0
        )
        sc = mm_nt(stack_heads(q[:, cols], rows), k[:, cols]) * SCALE + bias
        sc = jnp.where(keep, sc, NEGATIVE)
        e = jnp.exp(sc - jnp.max(sc, axis=-1, keepdims=True))
        p = e / jnp.sum(e, axis=-1, keepdims=True)
        p_ref[pair] = p
        contexts.append(pick_heads(mm(p.astype(BF), v[:, cols]), rows))
    ctx = jnp.concatenate(contexts, axis=1).astype(BF)
    ctx_ref[...] = ctx
    mid = x + mm(ctx, scr[3])
    mid_ref[...] = mid
    h2 = (mid * inv_rms(mid) * lines[experts + 1:experts + 2]).astype(BF)
    h2_ref[...] = h2
    logits = mm_nt(h2, router)
    e = jnp.exp(logits - jnp.max(logits, axis=-1, keepdims=True))
    probs = e / jnp.sum(e, axis=-1, keepdims=True)
    probs_ref[...] = probs
    sent = [h2]
    if layer == 1:
        gate = jnp.sum(probs * member_of(rc, experts), axis=-1, keepdims=True)
        sent.append((gate * g_ref[...].astype(F32)).astype(BF))
    for i in range(experts):
        for part, values in enumerate(sent):
            block = put_rows(tr, i, cap_pad, values, rows).astype(BF)
            ref = disp[i] if len(disp) > 1 else disp[0].at[i]
            if layer == 1:
                ref[part] = block
            else:
                ref[...] = block


def backward_kernel(layer, experts, slab, cap_pad, n_ret, n_w, plan, *refs):
    it = iter(refs)
    meta, small, rc_ref, rr_ref, head_of, offset_of, flip = (next(it) for _ in range(7))
    g_ref, x_ref, h1_ref, qkv_ref, p_ref, ctx_ref, mid_ref, h2_ref, probs_ref = (
        next(it) for _ in range(9)
    )
    if layer == 0:
        y_ref = next(it)
    else:
        probs0, h1_0, ctx_0 = (next(it) for _ in range(3))
    ret = [next(it) for _ in range(n_ret)]
    w = Weights([next(it) for _ in range(n_w)], plan, experts, slab, layer)
    dx_ref, ex_ref = (next(it) for _ in range(2))
    factors = [next(it) for _ in range(4)]
    if layer == 1:
        out_ref = next(it)
    rest = list(it)
    scr, sem, right, left, sums = rest[-5:]
    disp = rest[:-5]
    big = not plan
    w.start(meta, scr, sem)
    rows, width = h1_ref.shape
    z = meta[2]
    rc = rc_ref[:, layer:layer + 1]
    tc, _ = target_slots(rc, rr_ref[layer:layer + 1], z, experts, cap_pad, big)
    lines = small_lines(meta, small, layer, experts, slab)
    router = lines[:experts].astype(BF)
    g = g_ref[...].astype(F32)
    mid = mid_ref[...]
    probs = probs_ref[...]
    member = member_of(rc, experts)
    gate = jnp.sum(probs * member, axis=-1, keepdims=True)

    def blocks(part):
        if layer == 0:
            return [r[...] for r in ret] if n_ret > 1 else [ret[0][i] for i in range(experts)]
        return [r[part] for r in ret] if n_ret > 1 else [ret[0][i, part] for i in range(experts)]

    if layer == 0:
        y = y_ref[...]
        dh2 = take_rows(tc, blocks(0), cap_pad, rows)
    else:
        y = take_rows(tc, blocks(0), cap_pad, rows)
        dh2 = take_rows(tc, blocks(1), cap_pad, rows)
        out_ref[...] = mid + gate * y
    dgate = jnp.sum(g * y, axis=-1, keepdims=True)
    high, low = split_two(probs * (dgate * (member - gate)))
    dh2 = dh2 + mm(high, router) + mm(low, router)
    dmid, dgain1 = rms_back(mid, lines[experts + 1:experts + 2], dh2)
    dmid = dmid + g
    h2 = h2_ref[...]
    drouter = mm_tn(high, h2) + mm_tn(low, h2)
    da = dmid.astype(BF)
    right[3] = da
    w.wait(meta, scr, sem)
    dctx = mm_nt(da, scr[3]).astype(BF)
    grads = ([], [], [])
    sums[...] = jnp.zeros_like(sums)
    for pair in range(PAIRS):
        cols = slice(pair * LANES, (pair + 1) * LANES)
        p = p_ref[pair]
        qs = stack_heads(qkv_ref[0, :, cols], rows)
        ds_heads = stack_heads(dctx[:, cols], rows)
        dp = mm_nt(ds_heads, qkv_ref[2, :, cols])
        ds = (p * (dp - jnp.sum(p * dp, axis=-1, keepdims=True))).astype(BF)
        for n, line in enumerate(offset_sums(ds, flip[...])):
            sums[2 * pair + n:2 * pair + n + 1] = line
        grads[0].append(pick_heads(mm(ds, qkv_ref[1, :, cols]) * SCALE, rows))
        grads[1].append(mm_tn(ds, qs) * SCALE)
        grads[2].append(mm_tn(p.astype(BF), ds_heads))
    dh1 = None
    for j in range(3):
        dj = jnp.concatenate(grads[j], axis=1).astype(BF)
        right[j] = dj
        part = mm_nt(dj, scr[j])
        dh1 = part if dh1 is None else dh1 + part
    dx, dgain0 = rms_back(x_ref[...].astype(F32), lines[experts:experts + 1], dh1)
    dx = dx + dmid
    dx_ref[...] = dx
    high, low = split_two(sums[...])
    by_place = (mm(high, offset_of[...]) + mm(low, offset_of[...])) * head_of[...].astype(F32)
    ex_ref[...] = jnp.zeros_like(ex_ref)
    ex_ref[0:experts] = drouter
    ex_ref[experts:experts + 1] = dgain0
    ex_ref[experts + 1:experts + 2] = dgain1
    ex_ref[experts + 2:experts + 3] = jnp.sum(by_place, axis=0, keepdims=True)
    if layer == 1:
        rc0 = rc_ref[:, 0:1]
        _, tr0 = target_slots(rc0, rr_ref[0:1], z, experts, cap_pad, big)
        gate0 = jnp.sum(probs0[...] * member_of(rc0, experts), axis=-1, keepdims=True)
        dy0 = (gate0 * dx.astype(BF).astype(F32)).astype(BF)
        for i in range(experts):
            block = put_rows(tr0, i, cap_pad, dy0, rows).astype(BF)
            ref = disp[i] if len(disp) > 1 else disp[0].at[i]
            ref[...] = block
    if layer == 1:
        left[0] = h1_ref[...]
        left[1] = ctx_ref[...]
        left[2] = h1_0[...]
        left[3] = ctx_0[...]
    place = meta[4]
    for m in range(4):
        target = place ^ m
        factors[m][0:rows] = right[target]
        if layer == 1:
            which = jnp.where(target == 3, 1, 0)
            factors[m][rows:2 * rows] = left[which]
            factors[m][2 * rows:] = left[2 + which]


def pack_kernel(n, cap, parts, *refs):
    out = refs[-1]
    blocks = refs[:-1]
    packed = out.shape[-2]
    cap_pad = blocks[0].shape[-2]
    for part in range(parts):
        total = None
        for i in range(n):
            block = blocks[i][part] if len(blocks) > 1 else blocks[0][i, part]
            row = lax.broadcasted_iota(jnp.int32, (packed, cap_pad), 0)
            slot = lax.broadcasted_iota(jnp.int32, (packed, cap_pad), 1)
            pick = ((row == slot + i * cap) & (slot < cap)).astype(BF)
            moved = mm(pick, block)
            total = moved if total is None else total + moved
        out[part] = total.astype(BF)


def unpack_kernel(n, cap, parts, *refs):
    sums, outs = refs[:4], refs[4:]
    packed = sums[0].shape[-2]
    cap_pad = outs[0].shape[-2]
    for part in range(parts):
        total = (
            sums[0][part].astype(F32)
            + sums[1][part].astype(F32)
            + sums[2][part].astype(F32)
            + sums[3][part].astype(F32)
        ).astype(BF)
        for i in range(n):
            row = lax.broadcasted_iota(jnp.int32, (cap_pad, packed), 1)
            slot = lax.broadcasted_iota(jnp.int32, (cap_pad, packed), 0)
            pick = ((row == slot + i * cap) & (slot < cap)).astype(BF)
            block = mm(pick, total).astype(BF)
            if len(outs) > 1:
                outs[i][part] = block
            else:
                outs[0][i, part] = block


def expert_weights(layer, meta, own, other, scr, sem):
    for which in range(2):
        @pl.when(meta[0] == layer)
        def _():
            pltpu.make_async_copy(own[which], scr.at[which], sem.at[which]).start()

        @pl.when(meta[0] != layer)
        def _():
            pltpu.make_async_copy(other[which], scr.at[which], sem.at[which]).start()

    def wait(which):
        pltpu.make_async_copy(own[which], scr.at[which], sem.at[which]).wait()

    return wait


def expert_forward_kernel(layer, both, *refs):
    meta, c0, c1, c2, c3, in_own, in_other, out_own, out_other = refs[:9]
    outs = refs[9:13]
    count = (len(refs) - 16) // 2
    kept = refs[13:13 + count]
    scr, sem = refs[13 + count:15 + count]
    saved, keep_sem = refs[15 + count:-1], refs[-1]

    def save(n, values):
        saved[n][...] = values
        pltpu.make_async_copy(saved[n], kept[n], keep_sem.at[n]).start()

    wait = expert_weights(layer, meta, (in_own, out_own), (in_other, out_other), scr, sem)
    packed = c0.shape[-2]
    rows = jnp.concatenate([c[0] for c in (c0, c1, c2, c3)], axis=0)
    wait(0)
    pre = mm(rows, scr[0])
    act = gelu(pre).astype(BF)
    save(0, rows)
    save(1, act)
    wait(1)
    y = mm(act, scr[1])
    for m in range(4):
        outs[m][0] = y[m * packed:(m + 1) * packed].astype(BF)
    if both:
        grad_rows = jnp.concatenate([c[1] for c in (c0, c1, c2, c3)], axis=0)
        dpre = (mm_nt(grad_rows, scr[1]) * gelu_slope(pre)).astype(BF)
        save(2, grad_rows)
        save(3, dpre)
        dh = mm_nt(dpre, scr[0])
        for m in range(4):
            outs[m][1] = dh[m * packed:(m + 1) * packed].astype(BF)
    else:
        save(2, pre)
    for n in range(count):
        pltpu.make_async_copy(saved[n], kept[n], keep_sem.at[n]).wait()


def expert_backward_kernel(layer, *refs):
    meta, c0, c1, c2, c3, in_own, in_other, out_own, out_other, pre_ref = refs[:10]
    outs = refs[10:14]
    kept, scr, sem, saved, keep_sem = refs[14:16], refs[16], refs[17], refs[18:20], refs[20]

    def copy_out(n):
        return pltpu.make_async_copy(saved[n], kept[n], keep_sem.at[n])

    wait = expert_weights(layer, meta, (in_own, out_own), (in_other, out_other), scr, sem)
    packed = c0.shape[-2]
    grad_rows = jnp.concatenate([c[0] for c in (c0, c1, c2, c3)], axis=0)
    saved[0][...] = grad_rows
    copy_out(0).start()
    slope = gelu_slope(pre_ref[...])
    wait(1)
    dpre = (mm_nt(grad_rows, scr[1]) * slope).astype(BF)
    saved[1][...] = dpre
    copy_out(1).start()
    wait(0)
    dh = mm_nt(dpre, scr[0])
    for m in range(4):
        outs[m][0] = dh[m * packed:(m + 1) * packed].astype(BF)
    copy_out(0).wait()
    copy_out(1).wait()


def bring_layer(layer_is, sets, scr, sem):
    for layer in range(2):
        @pl.when(layer_is == layer)
        def _():
            for n in range(4):
                pltpu.make_async_copy(sets[layer][n], scr[n], sem.at[n]).start()

    def wait(n):
        pltpu.make_async_copy(sets[0][n], scr[n], sem.at[n]).wait()

    return wait


def expert_send_kernel(meta, *refs):
    sets, out, scr, sem = (refs[0:4], refs[4:8]), refs[8], refs[9:13], refs[13]
    wait = bring_layer(1 - meta[0], sets, scr, sem)
    wait(0)
    wait(1)
    out[0] = mm_tn(scr[0][...], scr[1][...]).astype(BF)
    wait(2)
    wait(3)
    out[1] = mm_tn(scr[2][...], scr[3][...]).astype(BF)


def expert_own_kernel(meta, *refs):
    sets, got, gin, gout, scr, sem = (
        (refs[0:4], refs[4:8]), refs[8], refs[9], refs[10], refs[11:15], refs[15],
    )
    wait = bring_layer(meta[0], sets, scr, sem)
    wait(0)
    wait(1)
    gin[...] = mm_tn(scr[0][...], scr[1][...]) + got[0].astype(F32)
    wait(2)
    wait(3)
    gout[...] = mm_tn(scr[2][...], scr[3][...]) + got[1].astype(F32)


def factor_kernel(experts, slab, rows, split, meta, *refs):
    rights, lefts, ex, keep, send = refs[0:4], refs[4:8], refs[8], refs[9], refs[10]
    right = jnp.concatenate([f[0:rows] for f in rights], axis=0)
    left = jnp.concatenate([f[split:split + rows] for f in lefts], axis=0)
    grad = mm_tn(left, right).astype(BF)
    s, z = meta[0], meta[2]
    extra = ex[...]
    pad = jnp.zeros((16, grad.shape[1] - LANES), F32)
    for shard in range(2 * experts):
        at = lax.rem(shard // 2 - z + experts, experts)
        wide = jnp.concatenate(
            [extra[:, shard * slab:(shard + 1) * slab], jnp.zeros((16, LANES - slab), F32)], axis=1
        )
        block = jnp.concatenate([wide, pad], axis=1).astype(BF)

        @pl.when(s == shard % 2)
        def _():
            keep[at, 0:slab] = grad[shard * slab:(shard + 1) * slab]
            keep[at, slab:] = block

        @pl.when(s != shard % 2)
        def _():
            send[at, 0:slab] = grad[shard * slab:(shard + 1) * slab]
            send[at, slab:] = block


def finish_kernel(experts, slab, table_slab, meta, *refs):
    arrived, (qkv, out, router, gains, table) = refs[:4], refs[4:]
    s, x = meta[0], meta[1]
    extra = None
    for a in range(2):
        for b in range(2):
            block = arrived[2 * a + b]
            matrix = 2 * (x ^ b) + (s ^ a)
            main = block[0:slab].astype(F32)

            @pl.when(matrix == 3)
            def _():
                out[0] = main

            @pl.when(matrix != 3)
            def _():
                qkv[0, matrix] = main

            small = block[slab:, 0:LANES].astype(F32)
            extra = small if extra is None else extra + small
    router[0] = extra[0:experts, 0:slab]
    gains[0] = extra[experts:experts + 2, 0:slab]
    table[...] = extra[experts + 2:experts + 3, 0:table_slab]


def call(
    kernel, out_shapes, args, specs, scratch=(), flops=0, moved=0, name=None, vmem=62, hbm=0
):
    return pl.pallas_call(
        kernel,
        out_shape=[jax.ShapeDtypeStruct(shape, dtype) for shape, dtype in out_shapes],
        in_specs=specs,
        out_specs=[VM] * (len(out_shapes) - hbm) + [ANY] * hbm,
        scratch_shapes=list(scratch),
        compiler_params=pltpu.CompilerParams(vmem_limit_bytes=vmem * 2**20),
        cost_estimate=pl.CostEstimate(flops=flops, bytes_accessed=moved, transcendentals=0),
        name=name,
    )(*args)


def shift(v, axis, by):
    n = lax.axis_size(axis)
    return lax.ppermute(v, axis, [(i, (i + by) % n) for i in range(n)])


def after(values, *events):
    values = tuple(values)
    return list(lax.optimization_barrier(values + events)[: len(values)])


def swap_section(v):
    return lax.ppermute(v, "section", [(0, 1), (1, 0)])


def plane_swap(v, mask):
    return lax.ppermute(v, PLANE, [(i, i ^ mask) for i in range(4)])


def plane_gather(v):
    return [v] + [plane_swap(v, m) for m in (1, 2, 3)]


def local(
    experts,
    boundary,
    seq_lengths,
    routes,
    qkv_proj,
    out_proj,
    router,
    gains,
    rel_table,
    expert_in,
    expert_out,
):
    big = experts > 8
    s = lax.axis_index("section")
    x_at = lax.axis_index("rep")
    z_at = lax.axis_index("expert")
    y_at = lax.axis_index("half")
    shards = 2 * experts
    rows, width = boundary.shape[2:]
    slab = qkv_proj.shape[2]
    table_slab = rel_table.shape[1]
    cap = max(2, rows // experts + 1)
    cap_pad = up(cap, 8)
    packed = up(experts * cap, 16)
    ff = expert_in.shape[3]
    first = s == 0

    own = boundary[0]
    got = swap_section(own[1 - s])
    x0 = jnp.where(first, own[0], got)
    g1 = jnp.where(first, got, own[1])
    lengths = seq_lengths[s, 0]
    place = jnp.stack([s, x_at, z_at, y_at, 2 * x_at + y_at]).astype(jnp.int32)
    meta = jnp.concatenate([place, lengths])
    own_routes = routes[0, :, :, 0]
    got_routes = swap_section(own_routes[1 - s])
    route_list = [
        jnp.where(first, own_routes[0], got_routes),
        jnp.where(first, got_routes, own_routes[1]),
    ]

    early = ()
    if big:
        slabs = jnp.concatenate([qkv_proj[0], out_proj], axis=0)
        whole = lax.all_gather(slabs, ("expert", "half"), axis=1, tiled=True)
        layers = lax.all_gather(whole, "section", axis=0)
        attn_w = [[layers[0]], [layers[1]]]
        plan = []
    else:
        slabs = jnp.concatenate([qkv_proj[0], out_proj], axis=0)
        piece = lax.dynamic_slice_in_dim(slabs, 2 * x_at, 2, axis=0)
        along = {1: shift(piece, "expert", 1), 3: shift(piece, "expert", 3)}
        over_y0 = plane_swap(piece, 1)
        along[2] = shift(after([piece], along[1])[0], "expert", 2)
        early = (over_y0,)

    small_rows = up(experts + 3, 8)
    table_row = jnp.pad(rel_table, ((0, 0), (0, slab - table_slab)))
    small = jnp.concatenate(
        [
            router[0].T,
            gains[0],
            table_row,
            jnp.zeros((small_rows - experts - 3, slab), BF),
        ]
    )
    (small,) = after([small], *early)
    if big:
        small_all = lax.all_gather(
            lax.all_gather(small, ("expert", "half"), axis=0), "section", axis=0
        )
    else:
        lines = jnp.stack([small] + [shift(small, "expert", i) for i in range(1, experts)])
        lines = jnp.stack([lines, shift(lines, "half", 1)])
        small_all = jnp.stack([lines, swap_section(lines)])
    head_of, offset_of = table_places(shards, slab, table_slab)
    flip = jnp.asarray(np.eye(2 * rows)[::-1], BF)
    rr = jnp.stack(route_list)
    common = [meta, small_all, rr.T, rr, head_of, offset_of]

    if not big:
        pieces, plan = [slabs], [(0, 0, 0, 0, 4)]
        pieces += [over_y0, plane_swap(over_y0, 2)]
        plan += [(0, 1, 0, 0, 2), (0, 1, 1, 0, 2)]
        for i in (1, 3, 2):
            got = along[i]
            if i == 2:
                got, x0, g1, *common = after([got, x0, g1] + common)
            over_y, over_x = plane_swap(got, 1), plane_swap(got, 2)
            pieces += [got, over_y, over_x]
            plan += [(i, 0, 0, 0, 2), (i, 1, 0, 0, 2), (i, 0, 1, 0, 2)]
            if i == 1:
                pieces.append(plane_swap(over_y, 2))
                plan.append((i, 1, 1, 0, 2))
            elif i == 3:
                pieces.append(plane_swap(over_x, 1))
                plan.append((i, 1, 1, 0, 2))
            else:
                pieces += [plane_swap(over_y[:1], 2), plane_swap(over_x[1:], 1)]
                plan += [(i, 1, 1, 0, 1), (i, 1, 1, 1, 1)]
        copied = [swap_section(v) for v in pieces]
        attn_w = [pieces + copied] * 2
    other_in = swap_section(expert_in[0, 0])
    other_out = swap_section(expert_out[0, 0])
    expert_w = [expert_in[0, 0], other_in, expert_out[0, 0], other_out]

    n_w = len(attn_w[0])
    n_ret = 1 if big else experts

    def message_shapes(parts):
        if big:
            return [((experts,) + parts + (cap_pad, width), BF)]
        return [(parts + (cap_pad, width), BF)] * experts

    def dispatch(blocks, parts):
        if big:
            arrived = lax.all_to_all(blocks[0], "expert", 0, 0, tiled=True)
            arrived = [arrived if parts == 2 else arrived[:, None]]
        else:
            arrived = [blocks[0]] + [shift(blocks[i], "expert", i) for i in range(1, experts)]
            arrived = arrived if parts == 2 else [a[None] for a in arrived]
        (joined,) = call(
            functools.partial(pack_kernel, experts, cap, parts),
            [((parts, packed, width), BF)],
            arrived,
            [VM] * len(arrived),
            moved=4 * packed * width,
            name="pack",
            vmem=8,
        )
        return plane_gather(joined)

    def come_back(partial, parts, events=()):
        sums = [partial[0]] + [plane_swap(partial[m], m) for m in (1, 2, 3)]
        if events:
            sums = after(sums, *events)
        shapes = (
            [((experts, parts, cap_pad, width), BF)]
            if big
            else [((parts, cap_pad, width), BF)] * experts
        )
        blocks = call(
            functools.partial(unpack_kernel, experts, cap, parts),
            shapes,
            sums,
            [VM] * 4,
            moved=4 * packed * width,
            name="unpack",
            vmem=8,
        )
        if big:
            back = lax.all_to_all(blocks[0], "expert", 0, 0, tiled=True)
            return [back if parts == 2 else back[:, 0]]
        back = [blocks[0]] + [shift(blocks[i], "expert", -i) for i in range(1, experts)]
        return back if parts == 2 else [b[0] for b in back]

    def forward(layer, extra):
        args = common + extra
        specs = [SM] + [VM] * (len(args) - 1) + [ANY] * n_w
        shapes = [
            ((rows, width), BF),
            ((3, rows, width), BF),
            ((PAIRS, 2 * rows, rows), F32),
            ((rows, width), BF),
            ((rows, width), F32),
            ((rows, width), BF),
            ((rows, experts), F32),
        ]
        if layer == 1:
            shapes += [((rows, width), BF), ((rows, width), F32)]
        fixed = len(shapes)
        shapes += message_shapes((2,) if layer == 1 else ())
        outs = call(
            functools.partial(forward_kernel, layer, experts, slab, cap_pad, n_ret, n_w, plan),
            shapes,
            args + attn_w[layer],
            specs,
            Weights.scratch(plan, width),
            flops=8 * rows * width * width,
            moved=8 * width * width,
            name="attention_forward",
        )
        names = ["h1", "qkv", "p", "ctx", "mid", "h2", "probs", "x1", "y0"][:fixed]
        return dict(zip(names, outs[:fixed])), outs[fixed:]

    def backward(layer, kept, x_in, g, returned, extra):
        args = common + [flip, g, x_in] + [
            kept[n] for n in ("h1", "qkv", "p", "ctx", "mid", "h2", "probs")
        ]
        args += extra + returned
        specs = [SM] + [VM] * (len(args) - 1) + [ANY] * n_w
        shapes = [
            ((rows, width), F32),
            ((up(experts + 3, 16), width), F32),
        ] + [(((3 if layer == 1 else 1) * rows, width), BF)] * 4
        if layer == 1:
            shapes += [((rows, width), F32)] + message_shapes(())
        return call(
            functools.partial(backward_kernel, layer, experts, slab, cap_pad, n_ret, n_w, plan),
            shapes,
            args + attn_w[layer],
            specs,
            Weights.scratch(plan, width)
            + [
                pltpu.VMEM((4, rows, width), BF),
                pltpu.VMEM((4, rows, width), BF),
                pltpu.VMEM((16, LANES), F32),
            ],
            flops=16 * rows * width * width,
            moved=8 * width * width,
            name="attention_backward",
        )

    expert_scratch = [pltpu.VMEM((2, width, ff), BF), pltpu.SemaphoreType.DMA((2,))]
    expert_specs = [SM] + [VM] * 4 + [ANY] * 4
    all_rows = 4 * packed

    def expert_forward(layer, joined, both):
        parts = 2 if both else 1
        shapes = [((parts, packed, width), BF)] * 4
        shapes += [((all_rows, width), BF), ((all_rows, ff), BF)]
        shapes += (
            [((all_rows, width), BF), ((all_rows, ff), BF)] if both else [((all_rows, ff), F32)]
        )
        outs = call(
            functools.partial(expert_forward_kernel, layer, both),
            shapes,
            [meta] + joined + expert_w,
            expert_specs,
            expert_scratch
            + [pltpu.VMEM(*shape) for shape in shapes[4:]]
            + [pltpu.SemaphoreType.DMA((len(shapes) - 4,))],
            hbm=len(shapes) - 4,
            flops=4 * all_rows * width * ff * parts,
            moved=4 * width * ff,
            name="expert_forward",
            vmem=20,
        )
        return outs[:4], outs[4:]

    def plane_factors(factors):
        return [factors[0]] + [plane_swap(factors[m], m) for m in (1, 2, 3)]

    def attention_grads(rights, lefts, split, ex):
        keep, send = call(
            functools.partial(factor_kernel, experts, slab, rows, split),
            [((experts, slab + 16, width), BF)] * 2,
            [meta] + rights + lefts + [ex],
            [SM] + [VM] * 9,
            flops=8 * rows * width * width,
            moved=8 * width * width,
            name="attention_grads",
        )
        return keep, send

    def sum_cores(keep, send):
        both = keep.astype(F32) + swap_section(send).astype(F32)
        return [both[i].astype(BF) for i in range(experts)]

    def along_z(parts):
        return [parts[0]] + [shift(parts[i], "expert", i) for i in range(1, experts)]

    def add_up(parts):
        total = parts[0].astype(F32)
        for part in parts[1:]:
            total = total + part.astype(F32)
        return total.astype(BF)

    kept0, blocks = forward(0, [x0])
    joined = dispatch(blocks, 1)
    partial, (rows0, act0, pre0) = expert_forward(0, joined, False)
    returned = come_back(partial, 1)

    kept1, blocks = forward(1, [kept0["mid"], kept0["probs"], g1] + returned)
    joined = dispatch(blocks, 2)
    partial, (rows1, act1, grows1, dpre1) = expert_forward(1, joined, True)
    returned = come_back(partial, 2)

    outs = backward(
        1, kept1, kept1["x1"], g1, returned, [kept0["probs"], kept0["h1"], kept0["ctx"]]
    )
    dx1, ex1 = outs[:2]
    factors1, out1, blocks = outs[2:6], outs[6], outs[7:]

    joined = dispatch(blocks, 1)
    shapes = [((1, packed, width), BF)] * 4 + [((all_rows, width), BF), ((all_rows, ff), BF)]
    outs = call(
        functools.partial(expert_backward_kernel, 0),
        shapes,
        [meta] + joined + expert_w + [pre0],
        expert_specs + [VM],
        expert_scratch
        + [pltpu.VMEM(*shape) for shape in shapes[4:]]
        + [pltpu.SemaphoreType.DMA((2,))],
        hbm=2,
        flops=4 * all_rows * width * ff,
        moved=4 * width * ff,
        name="expert_backward",
            vmem=20,
    )
    partial, (grows0, dpre0) = outs[:4], outs[4:]
    if not big:
        beside = plane_factors(factors1)
        beside = after(beside, partial[3])
        halves1 = attention_grads(beside, beside, rows, ex1)
        returned = come_back(partial, 1, halves1)
        moved1 = along_z(after(sum_cores(*halves1), *returned))
    else:
        returned = come_back(partial, 1)
    outs = backward(0, kept0, x0, dx1.astype(BF), returned, [kept1["y0"]])
    dx0, ex0 = outs[:2]
    factors0 = outs[2:6]
    if not big:
        factors0 = after(factors0, *moved1)
        rights0 = plane_factors(factors0)
        halves0 = attention_grads(rights0, beside, 2 * rows, ex0)
        parts0 = sum_cores(*halves0)
        moved0 = along_z(parts0)

    traded = swap_section(jnp.where(first, out1, dx0))
    result_rows = jnp.stack([jnp.where(first, dx0, traded), jnp.where(first, traded, out1)])

    sets = [rows0, dpre0, act0, grows0, rows1, dpre1, act1, grows1]
    if not big:
        sets = after(sets, rights0[1])
    bring_scratch = [
        pltpu.VMEM((all_rows, width), BF),
        pltpu.VMEM((all_rows, ff), BF),
        pltpu.VMEM((all_rows, ff), BF),
        pltpu.VMEM((all_rows, width), BF),
        pltpu.SemaphoreType.DMA((4,)),
    ]
    (sent,) = call(
        expert_send_kernel,
        [((2, width, ff), BF)],
        [meta] + sets,
        [SM] + [ANY] * 8,
        bring_scratch,
        flops=4 * all_rows * width * ff,
        moved=8 * width * ff,
        name="expert_gradients_sent",
    )
    got = swap_section(sent)

    def own_experts(sets, got):
        return call(
            expert_own_kernel,
            [((width, ff), F32), ((ff, width), F32)],
            [meta] + sets + [got],
            [SM] + [ANY] * 8 + [VM],
            bring_scratch,
            flops=4 * all_rows * width * ff,
            moved=8 * width * ff,
            name="expert_gradients_own",
        )

    traded = swap_section(jnp.where(first, out1, dx0))
    result_rows = jnp.stack([jnp.where(first, dx0, traded), jnp.where(first, traded, out1)])

    if big:
        own_factors = []
        for kept, ex, fac in ((kept0, ex0, factors0), (kept1, ex1, factors1)):
            spot = 2 * x_at + y_at
            right = jnp.stack([fac[m][:rows] for m in range(4)])
            pieces = [
                jnp.sum(
                    jnp.where(
                        (jnp.arange(4) ^ spot == j)[:, None, None], right, jnp.zeros_like(right)
                    ),
                    axis=0,
                )
                for j in range(4)
            ]
            lefts = [kept["h1"]] * 3 + [kept["ctx"]]
            grad = jnp.stack(
                [
                    lax.dot_general(
                        a, b, (((0,), (0,)), ((), ())), preferred_element_type=F32
                    )
                    for a, b in zip(lefts, pieces)
                ]
            )
            own_factors.append((grad, ex[:experts + 3]))
        grad = jnp.stack([own_factors[0][0], own_factors[1][0]]).astype(BF)
        lines = jnp.stack([own_factors[0][1], own_factors[1][1]])
        grad = lax.psum_scatter(grad, "section", scatter_dimension=0)
        lines = lax.psum_scatter(lines, "section", scatter_dimension=0)
        grad = lax.psum_scatter(grad, ("expert", "half"), scatter_dimension=1, tiled=True)
        grad = lax.psum(grad, "rep").astype(F32)
        lines = lax.psum(lines, ("rep", "expert", "half"))
        shard_at = z_at * 2 + y_at
        extra = lax.dynamic_slice_in_dim(lines, shard_at * slab, slab, axis=1)
        smalls = (
            grad[None, :3],
            grad[3][None],
            extra[:experts].T[None],
            extra[experts:experts + 2][None],
            extra[experts + 2, :table_slab][None],
        )
        final_in, final_out = own_experts(sets, got)
    else:
        blocks = [add_up(moved0), add_up(moved1)]
        arrived = []
        trade = ("section", "rep", "half")
        for a in range(2):
            message = jnp.where((y_at ^ a) == 0, blocks[0], blocks[1])
            for b in range(2):
                pairs = []
                for i in range(8):
                    si, xi, yi = i // 4, (i // 2) % 2, i % 2
                    pairs.append((i, (yi ^ a) * 4 + (xi ^ b) * 2 + si))
                arrived.append(lax.ppermute(message, trade, pairs))
        final_in, final_out = own_experts(after(sets, arrived[0]), got)
        arrived = after(arrived, final_in)
        smalls = list(call(
            functools.partial(finish_kernel, experts, slab, table_slab),
            [
                ((1, 3, slab, width), F32),
                ((1, slab, width), F32),
                ((1, experts, slab), F32),
                ((1, 2, slab), F32),
                ((1, table_slab), F32),
            ],
            [meta] + arrived,
            [SM] + [VM] * 4,
            moved=16 * slab * width,
            name="finish",
        ))
        smalls[2] = smalls[2].transpose(0, 2, 1)
    return (result_rows[None], *smalls, final_in[None, None], final_out[None, None])


def solution(mesh):
    sections, reps, shards = (mesh.shape[n] for n in ("section", "rep", "shard"))
    experts = shards // 2
    split = Mesh(
        mesh.devices.reshape(sections, reps, experts, 2), ("section", "rep", "expert", "half")
    )
    shard = ("expert", "half")
    in_specs = (
        P("section", None, ("rep",) + shard, None),
        P(None, ("rep",) + shard, None),
        P("section", None, ("rep",) + shard, None),
        P("section", None, shard, None),
        P("section", shard, None),
        P("section", shard, None),
        P("section", None, shard),
        P("section", shard),
        P("section", shard, None, "rep"),
        P("section", shard, "rep", None),
    )
    out_specs = (
        P("section", None, ("rep",) + shard, None),
        P("section", None, shard, None),
        P("section", shard, None),
        P("section", shard, None),
        P("section", None, shard),
        P("section", shard),
        P("section", shard, None, "rep"),
        P("section", shard, "rep", None),
    )
    return jax.shard_map(
        functools.partial(local, experts),
        mesh=split,
        in_specs=in_specs,
        out_specs=out_specs,
        check_vma=False,
    )
```

```python
import functools
import math

import jax
import jax.numpy as jnp
import numpy as np
from jax import lax
from jax.experimental import pallas as pl
from jax.experimental.pallas import tpu as pltpu
from jax.sharding import Mesh, PartitionSpec as P

HEADS = 12
HEAD = 64
BUCKETS = 32
SPAN = 128
PAIRS = HEADS // 2
EPSILON = 1e-06
NEGATIVE = -1e30
SCALE = 1.0 / math.sqrt(HEAD)
LANES = 128
PLANE = ("rep", "half")
BF = jnp.bfloat16
F32 = jnp.float32
VM = pl.BlockSpec(memory_space=pltpu.VMEM)
SM = pl.BlockSpec(memory_space=pltpu.SMEM)
ANY = pl.BlockSpec(memory_space=pl.ANY)
HBM = pl.BlockSpec(memory_space=pltpu.HBM)


def up(n, m):
    return -(-n // m) * m


def bucket_of(offset):
    half_count = BUCKETS // 2
    exact_count = half_count // 2
    base = half_count if offset > 0 else 0
    distance = abs(offset)
    if distance < exact_count:
        return base + distance
    bucket = exact_count + int(
        math.log(distance / exact_count)
        / math.log(SPAN / exact_count)
        * (half_count - exact_count)
    )
    return base + min(bucket, half_count - 1)


def table_places(shards, slab, table_slab):
    head_of = np.zeros((16, shards * slab), np.float32)
    offset_of = np.zeros((LANES, shards * slab), np.float32)
    for lane in range(shards * slab):
        shard, place = divmod(lane, slab)
        if place >= table_slab:
            continue
        bucket, head = divmod(shard * table_slab + place, HEADS)
        head_of[head, lane] = 1.0
        for d in range(LANES):
            if bucket_of(d if d < HEAD else d - LANES) == bucket:
                offset_of[d, lane] = 1.0
    return jnp.asarray(head_of, BF), jnp.asarray(offset_of, BF)


def mm(a, b):
    return jnp.dot(a, b, preferred_element_type=F32)


def mm_nt(a, b):
    return lax.dot_general(a, b, (((1,), (1,)), ((), ())), preferred_element_type=F32)


def mm_tn(a, b):
    return lax.dot_general(a, b, (((0,), (0,)), ((), ())), preferred_element_type=F32)


def inv_rms(v):
    return lax.rsqrt(jnp.mean(v * v, axis=-1, keepdims=True) + EPSILON)


def rms_back(v, gain, grad):
    r = inv_rms(v)
    scaled = grad * gain
    dv = r * scaled - v * (r * r * r) * jnp.mean(v * scaled, axis=-1, keepdims=True)
    return dv, jnp.sum(grad * v * r, axis=0, keepdims=True)


def tanh_parts(v):
    c = math.sqrt(2.0 / math.pi)
    return c, jnp.tanh(c * (v + 0.044715 * (v * v * v)))


def gelu(v):
    _, t = tanh_parts(v)
    return 0.5 * v * (1.0 + t)


def gelu_slope(v):
    c, t = tanh_parts(v)
    return 0.5 * (1.0 + t) + 0.5 * v * (1.0 - t * t) * (c * (1.0 + 3.0 * 0.044715 * (v * v)))


def stack_heads(pair, rows):
    lane = lax.broadcasted_iota(jnp.int32, (rows, LANES), 1)
    zero = jnp.zeros_like(pair)
    return jnp.concatenate(
        [jnp.where(lane < HEAD, pair, zero), jnp.where(lane < HEAD, zero, pair)], axis=0
    )


def pick_heads(stacked, rows):
    lane = lax.broadcasted_iota(jnp.int32, (rows, LANES), 1)
    return jnp.where(lane < HEAD, stacked[:rows], stacked[rows:])


def member_of(rc, experts):
    lane = lax.broadcasted_iota(jnp.int32, (rc.shape[0], experts), 1)
    return (lane == rc).astype(F32)


def target_slots(rc, rr, z, experts, cap_pad, big):
    rows = rc.shape[0]
    i = lax.broadcasted_iota(jnp.int32, (rows, rows), 0)
    j = lax.broadcasted_iota(jnp.int32, (rows, rows), 1)
    same = rc == rr
    before = jnp.where(same & (j < i), 1.0, 0.0)
    after = jnp.where(same & (i < j), 1.0, 0.0)

    def place(route, slot):
        if not big:
            route = jnp.where(route < z, route - z + experts, route - z)
        return route * cap_pad + slot.astype(jnp.int32)

    return (
        place(rc, jnp.sum(before, axis=1, keepdims=True)),
        place(rr, jnp.sum(after, axis=0, keepdims=True)),
    )


def small_lines(meta, small, layer, experts, slab):
    pieces = []
    for shard in range(2 * experts):
        if small.shape[0] == 2 and len(small.shape) == 4:
            block = small[layer, shard]
        else:
            at_z = lax.rem(meta[2] - shard // 2 + experts, experts)
            block = small[meta[0] ^ layer, meta[3] ^ (shard % 2), at_z]
        pieces.append(block.astype(F32))
    return jnp.concatenate(pieces, axis=1)


def same_sequence(meta, rows):
    shape = (2 * rows, rows)
    i = lax.broadcasted_iota(jnp.int32, shape, 0)
    i = jnp.where(i < rows, i, i - rows)
    j = lax.broadcasted_iota(jnp.int32, shape, 1)
    seg_i, seg_j = jnp.zeros(shape, jnp.int32), jnp.zeros(shape, jnp.int32)
    end = 0
    for n in range(5, 9):
        end = end + meta[n]
        seg_i = seg_i + (i >= end).astype(jnp.int32)
        seg_j = seg_j + (j >= end).astype(jnp.int32)
    return seg_i == seg_j


def position_bias(by_offset, head, rows):
    line = jnp.broadcast_to(by_offset[head:head + 1], (rows, LANES))
    return pltpu.roll(line, 0, 1, stride=1, stride_axis=0)[:, :rows]


def offset_sums(ds, flip):
    turned = mm(flip, ds)
    wide = jnp.concatenate([turned, jnp.zeros_like(turned)], axis=1)
    rolled = pltpu.roll(wide, 0, 1, stride=1, stride_axis=0)
    rows = ds.shape[0] // 2
    first = jnp.sum(rolled[rows:], axis=0, keepdims=True)
    second = jnp.sum(rolled[:rows], axis=0, keepdims=True)
    return [pltpu.roll(first, 1, 1), pltpu.roll(second, 1 + rows, 1)]


def split_two(v):
    high = v.astype(BF)
    return high, (v - high.astype(F32)).astype(BF)


def put_rows(target_row, block, cap_pad, values, rows):
    slot = lax.broadcasted_iota(jnp.int32, (cap_pad, rows), 0) + block * cap_pad
    return mm((slot == target_row).astype(BF), values)


def take_rows(target_col, blocks, cap_pad, rows):
    total = None
    for i, block in enumerate(blocks):
        slot = lax.broadcasted_iota(jnp.int32, (rows, cap_pad), 1) + i * cap_pad
        part = mm((slot == target_col).astype(BF), block)
        total = part if total is None else total + part
    return total


class Weights:
    def __init__(self, refs, plan, experts, slab, layer):
        self.refs, self.plan, self.experts, self.slab, self.layer = (
            refs, plan, experts, slab, layer,
        )

    @staticmethod
    def scratch(plan, width):
        return [pltpu.VMEM((4, width, width), BF), pltpu.SemaphoreType.DMA((max(1, len(plan)),))]

    def copies(self, meta, scr, sem, which):
        if not self.plan:
            return [pltpu.make_async_copy(self.refs[0], scr, sem.at[0])]
        x, z, y = meta[1], meta[2], meta[3]
        count = len(self.plan)
        made = []
        for n, (i, flip_y, flip_x, offset, held) in enumerate(self.plan):
            at_z = lax.rem(z - i + self.experts, self.experts)
            row = pl.multiple_of((at_z * 2 + (y ^ flip_y)) * self.slab, self.slab)
            matrix = 0 if held == 4 else 2 * (x ^ flip_x) + offset
            made.append(
                pltpu.make_async_copy(
                    self.refs[which * count + n],
                    scr.at[pl.ds(matrix, held), pl.ds(row, self.slab)],
                    sem.at[n],
                )
            )
        return made

    def start(self, meta, scr, sem):
        if not self.plan:
            self.copies(meta, scr, sem, 0)[0].start()
            return

        @pl.when(meta[0] == self.layer)
        def _():
            for copy in self.copies(meta, scr, sem, 0):
                copy.start()

        @pl.when(meta[0] != self.layer)
        def _():
            for copy in self.copies(meta, scr, sem, 1):
                copy.start()

    def wait(self, meta, scr, sem):
        for copy in self.copies(meta, scr, sem, 0):
            copy.wait()


def forward_kernel(layer, experts, slab, cap_pad, n_ret, n_w, plan, *refs):
    it = iter(refs)
    meta, small, rc_ref, rr_ref, head_of, offset_of = (next(it) for _ in range(6))
    if layer == 0:
        x_ref = next(it)
    else:
        mid0, probs0, g_ref = (next(it) for _ in range(3))
        ret = [next(it) for _ in range(n_ret)]
    w = Weights([next(it) for _ in range(n_w)], plan, experts, slab, layer)
    h1_ref, qkv_ref, p_ref, ctx_ref, mid_ref, h2_ref, probs_ref = (next(it) for _ in range(7))
    if layer == 1:
        x1_ref, y0_ref = next(it), next(it)
    rest = list(it)
    scr, sem = rest[-2:]
    disp = rest[:-2]
    big = not plan
    w.start(meta, scr, sem)
    rows, width = h1_ref.shape
    z = meta[2]
    rc = rc_ref[:, layer:layer + 1]
    _, tr = target_slots(rc, rr_ref[layer:layer + 1], z, experts, cap_pad, big)
    lines = small_lines(meta, small, layer, experts, slab)
    router = lines[:experts].astype(BF)
    table = (head_of[...].astype(F32) * lines[experts + 2:experts + 3]).astype(BF)
    by_offset = mm_nt(table, offset_of[...])
    keep = same_sequence(meta, rows)
    if layer == 0:
        x = x_ref[...].astype(F32)
    else:
        blocks = [ret[i][...] for i in range(n_ret)] if n_ret > 1 else [
            ret[0][i] for i in range(experts)
        ]
        rc0 = rc_ref[:, 0:1]
        tc0, _ = target_slots(rc0, rr_ref[0:1], z, experts, cap_pad, big)
        y0 = take_rows(tc0, blocks, cap_pad, rows)
        y0_ref[...] = y0
        gate0 = jnp.sum(probs0[...] * member_of(rc0, experts), axis=-1, keepdims=True)
        x1 = (mid0[...] + gate0 * y0).astype(BF)
        x1_ref[...] = x1
        x = x1.astype(F32)
    h1 = (x * inv_rms(x) * lines[experts:experts + 1]).astype(BF)
    h1_ref[...] = h1
    w.wait(meta, scr, sem)
    q = mm(h1, scr[0]).astype(BF)
    k = mm(h1, scr[1]).astype(BF)
    v = mm(h1, scr[2]).astype(BF)
    qkv_ref[0] = q
    qkv_ref[1] = k
    qkv_ref[2] = v
    pairs = range(PAIRS)
    cols = [slice(pair * LANES, (pair + 1) * LANES) for pair in pairs]
    sc = [mm_nt(stack_heads(q[:, c], rows), k[:, c]) for c in cols]
    bias = [
        jnp.concatenate([position_bias(by_offset, 2 * pair + n, rows) for n in range(2)], axis=0)
        for pair in pairs
    ]
    sc = [jnp.where(keep, sc[pair] * SCALE + bias[pair], NEGATIVE) for pair in pairs]
    top = [jnp.max(v, axis=-1, keepdims=True) for v in sc]
    e = [jnp.exp(sc[pair] - top[pair]) for pair in pairs]
    total = [jnp.sum(v, axis=-1, keepdims=True) for v in e]
    p = [e[pair] / total[pair] for pair in pairs]
    for pair in pairs:
        p_ref[pair] = p[pair]
    contexts = [mm(p[pair].astype(BF), v[:, cols[pair]]) for pair in pairs]
    contexts = [pick_heads(both, rows) for both in contexts]
    ctx = jnp.concatenate(contexts, axis=1).astype(BF)
    ctx_ref[...] = ctx
    mid = x + mm(ctx, scr[3])
    mid_ref[...] = mid
    h2 = (mid * inv_rms(mid) * lines[experts + 1:experts + 2]).astype(BF)
    h2_ref[...] = h2
    logits = mm_nt(h2, router)
    e = jnp.exp(logits - jnp.max(logits, axis=-1, keepdims=True))
    probs = e / jnp.sum(e, axis=-1, keepdims=True)
    probs_ref[...] = probs
    sent = [h2]
    if layer == 1:
        gate = jnp.sum(probs * member_of(rc, experts), axis=-1, keepdims=True)
        sent.append((gate * g_ref[...].astype(F32)).astype(BF))
    for i in range(experts):
        for part, values in enumerate(sent):
            block = put_rows(tr, i, cap_pad, values, rows).astype(BF)
            ref = disp[i] if len(disp) > 1 else disp[0].at[i]
            if layer == 1:
                ref[part] = block
            else:
                ref[...] = block


def backward_kernel(layer, experts, slab, cap_pad, n_ret, n_w, plan, *refs):
    it = iter(refs)
    meta, small, rc_ref, rr_ref, head_of, offset_of, flip = (next(it) for _ in range(7))
    g_ref, x_ref, h1_ref, qkv_ref, p_ref, ctx_ref, mid_ref, h2_ref, probs_ref = (
        next(it) for _ in range(9)
    )
    if layer == 0:
        y_ref = next(it)
    else:
        probs0, h1_0, ctx_0 = (next(it) for _ in range(3))
    ret = [next(it) for _ in range(n_ret)]
    w = Weights([next(it) for _ in range(n_w)], plan, experts, slab, layer)
    dx_ref, ex_ref = (next(it) for _ in range(2))
    factors = [next(it) for _ in range(4)]
    if layer == 1:
        out_ref = next(it)
    rest = list(it)
    scr, sem, right, left, sums = rest[-5:]
    disp = rest[:-5]
    big = not plan
    w.start(meta, scr, sem)
    rows, width = h1_ref.shape
    z = meta[2]
    rc = rc_ref[:, layer:layer + 1]
    tc, _ = target_slots(rc, rr_ref[layer:layer + 1], z, experts, cap_pad, big)
    lines = small_lines(meta, small, layer, experts, slab)
    router = lines[:experts].astype(BF)
    g = g_ref[...].astype(F32)
    mid = mid_ref[...]
    probs = probs_ref[...]
    member = member_of(rc, experts)
    gate = jnp.sum(probs * member, axis=-1, keepdims=True)

    def blocks(part):
        if layer == 0:
            return [r[...] for r in ret] if n_ret > 1 else [ret[0][i] for i in range(experts)]
        return [r[part] for r in ret] if n_ret > 1 else [ret[0][i, part] for i in range(experts)]

    if layer == 0:
        y = y_ref[...]
        dh2 = take_rows(tc, blocks(0), cap_pad, rows)
    else:
        y = take_rows(tc, blocks(0), cap_pad, rows)
        dh2 = take_rows(tc, blocks(1), cap_pad, rows)
        out_ref[...] = mid + gate * y
    dgate = jnp.sum(g * y, axis=-1, keepdims=True)
    high, low = split_two(probs * (dgate * (member - gate)))
    dh2 = dh2 + mm(high, router) + mm(low, router)
    dmid, dgain1 = rms_back(mid, lines[experts + 1:experts + 2], dh2)
    dmid = dmid + g
    h2 = h2_ref[...]
    drouter = mm_tn(high, h2) + mm_tn(low, h2)
    da = dmid.astype(BF)
    right[3] = da
    w.wait(meta, scr, sem)
    dctx = mm_nt(da, scr[3]).astype(BF)
    sums[...] = jnp.zeros_like(sums)
    pairs = range(PAIRS)
    cols = [slice(pair * LANES, (pair + 1) * LANES) for pair in pairs]
    ds_heads = [stack_heads(dctx[:, c], rows) for c in cols]
    dp = [mm_nt(ds_heads[pair], qkv_ref[2, :, cols[pair]]) for pair in pairs]
    p = [p_ref[pair] for pair in pairs]
    dv = [mm_tn(p[pair].astype(BF), ds_heads[pair]) for pair in pairs]
    weighted = [jnp.sum(p[pair] * dp[pair], axis=-1, keepdims=True) for pair in pairs]
    ds = [(p[pair] * (dp[pair] - weighted[pair])).astype(BF) for pair in pairs]
    dq = [mm(ds[pair], qkv_ref[1, :, cols[pair]]) for pair in pairs]
    dq = [pick_heads(both, rows) * SCALE for both in dq]
    dk = [
        mm_tn(ds[pair], stack_heads(qkv_ref[0, :, cols[pair]], rows)) * SCALE for pair in pairs
    ]
    by_line = [offset_sums(ds[pair], flip[...]) for pair in pairs]
    for pair in pairs:
        for n, line in enumerate(by_line[pair]):
            sums[2 * pair + n:2 * pair + n + 1] = line
    grads = (dq, dk, dv)
    dh1 = None
    for j in range(3):
        dj = jnp.concatenate(grads[j], axis=1).astype(BF)
        right[j] = dj
        part = mm_nt(dj, scr[j])
        dh1 = part if dh1 is None else dh1 + part
    dx, dgain0 = rms_back(x_ref[...].astype(F32), lines[experts:experts + 1], dh1)
    dx = dx + dmid
    dx_ref[...] = dx
    high, low = split_two(sums[...])
    by_place = (mm(high, offset_of[...]) + mm(low, offset_of[...])) * head_of[...].astype(F32)
    ex_ref[...] = jnp.zeros_like(ex_ref)
    ex_ref[0:experts] = drouter
    ex_ref[experts:experts + 1] = dgain0
    ex_ref[experts + 1:experts + 2] = dgain1
    ex_ref[experts + 2:experts + 3] = jnp.sum(by_place, axis=0, keepdims=True)
    if layer == 1:
        rc0 = rc_ref[:, 0:1]
        _, tr0 = target_slots(rc0, rr_ref[0:1], z, experts, cap_pad, big)
        gate0 = jnp.sum(probs0[...] * member_of(rc0, experts), axis=-1, keepdims=True)
        dy0 = (gate0 * dx.astype(BF).astype(F32)).astype(BF)
        for i in range(experts):
            block = put_rows(tr0, i, cap_pad, dy0, rows).astype(BF)
            ref = disp[i] if len(disp) > 1 else disp[0].at[i]
            ref[...] = block
    if layer == 1:
        left[0] = h1_ref[...]
        left[1] = ctx_ref[...]
        left[2] = h1_0[...]
        left[3] = ctx_0[...]
    place = meta[4]
    for m in range(4):
        target = place ^ m
        factors[m][0:rows] = right[target]
        if layer == 1:
            which = jnp.where(target == 3, 1, 0)
            factors[m][rows:2 * rows] = left[which]
            factors[m][2 * rows:] = left[2 + which]


def pack_kernel(n, cap, parts, *refs):
    out = refs[-1]
    blocks = refs[:-1]
    packed = out.shape[-2]
    cap_pad = blocks[0].shape[-2]
    for part in range(parts):
        total = None
        for i in range(n):
            block = blocks[i][part] if len(blocks) > 1 else blocks[0][i, part]
            row = lax.broadcasted_iota(jnp.int32, (packed, cap_pad), 0)
            slot = lax.broadcasted_iota(jnp.int32, (packed, cap_pad), 1)
            pick = ((row == slot + i * cap) & (slot < cap)).astype(BF)
            moved = mm(pick, block)
            total = moved if total is None else total + moved
        out[part] = total.astype(BF)


def unpack_kernel(n, cap, parts, *refs):
    sums, outs = refs[:4], refs[4:]
    packed = sums[0].shape[-2]
    cap_pad = outs[0].shape[-2]
    for part in range(parts):
        total = (
            sums[0][part].astype(F32)
            + sums[1][part].astype(F32)
            + sums[2][part].astype(F32)
            + sums[3][part].astype(F32)
        ).astype(BF)
        for i in range(n):
            row = lax.broadcasted_iota(jnp.int32, (cap_pad, packed), 1)
            slot = lax.broadcasted_iota(jnp.int32, (cap_pad, packed), 0)
            pick = ((row == slot + i * cap) & (slot < cap)).astype(BF)
            block = mm(pick, total).astype(BF)
            if len(outs) > 1:
                outs[i][part] = block
            else:
                outs[0][i, part] = block


def expert_weights(layer, meta, own, other, scr, sem):
    for which in range(2):
        @pl.when(meta[0] == layer)
        def _():
            pltpu.make_async_copy(own[which], scr.at[which], sem.at[which]).start()

        @pl.when(meta[0] != layer)
        def _():
            pltpu.make_async_copy(other[which], scr.at[which], sem.at[which]).start()

    def wait(which):
        pltpu.make_async_copy(own[which], scr.at[which], sem.at[which]).wait()

    return wait


def expert_forward_kernel(layer, both, *refs):
    meta, c0, c1, c2, c3, in_own, in_other, out_own, out_other = refs[:9]
    outs = refs[9:13]
    count = (len(refs) - 16) // 2
    kept = refs[13:13 + count]
    scr, sem = refs[13 + count:15 + count]
    saved, keep_sem = refs[15 + count:-1], refs[-1]

    def save(n, values):
        saved[n][...] = values
        pltpu.make_async_copy(saved[n], kept[n], keep_sem.at[n]).start()

    wait = expert_weights(layer, meta, (in_own, out_own), (in_other, out_other), scr, sem)
    packed = c0.shape[-2]
    rows = jnp.concatenate([c[0] for c in (c0, c1, c2, c3)], axis=0)
    wait(0)
    pre = mm(rows, scr[0])
    act = gelu(pre).astype(BF)
    save(0, rows)
    save(1, act)
    wait(1)
    y = mm(act, scr[1])
    for m in range(4):
        outs[m][0] = y[m * packed:(m + 1) * packed].astype(BF)
    if both:
        grad_rows = jnp.concatenate([c[1] for c in (c0, c1, c2, c3)], axis=0)
        dpre = (mm_nt(grad_rows, scr[1]) * gelu_slope(pre)).astype(BF)
        save(2, grad_rows)
        save(3, dpre)
        dh = mm_nt(dpre, scr[0])
        for m in range(4):
            outs[m][1] = dh[m * packed:(m + 1) * packed].astype(BF)
    else:
        save(2, pre)
    for n in range(count):
        pltpu.make_async_copy(saved[n], kept[n], keep_sem.at[n]).wait()


def expert_backward_kernel(layer, *refs):
    meta, c0, c1, c2, c3, in_own, in_other, out_own, out_other, pre_ref = refs[:10]
    outs = refs[10:14]
    kept, scr, sem, saved, keep_sem = refs[14:16], refs[16], refs[17], refs[18:20], refs[20]

    def copy_out(n):
        return pltpu.make_async_copy(saved[n], kept[n], keep_sem.at[n])

    wait = expert_weights(layer, meta, (in_own, out_own), (in_other, out_other), scr, sem)
    packed = c0.shape[-2]
    grad_rows = jnp.concatenate([c[0] for c in (c0, c1, c2, c3)], axis=0)
    saved[0][...] = grad_rows
    copy_out(0).start()
    slope = gelu_slope(pre_ref[...])
    wait(1)
    dpre = (mm_nt(grad_rows, scr[1]) * slope).astype(BF)
    saved[1][...] = dpre
    copy_out(1).start()
    wait(0)
    dh = mm_nt(dpre, scr[0])
    for m in range(4):
        outs[m][0] = dh[m * packed:(m + 1) * packed].astype(BF)
    copy_out(0).wait()
    copy_out(1).wait()


def bring_layer(layer_is, sets, scr, sem):
    for layer in range(2):
        @pl.when(layer_is == layer)
        def _():
            for n in range(4):
                pltpu.make_async_copy(sets[layer][n], scr[n], sem.at[n]).start()

    def wait(n):
        pltpu.make_async_copy(sets[0][n], scr[n], sem.at[n]).wait()

    return wait


def expert_send_kernel(meta, *refs):
    sets, out, scr, sem = (refs[0:4], refs[4:8]), refs[8], refs[9:13], refs[13]
    wait = bring_layer(1 - meta[0], sets, scr, sem)
    wait(0)
    wait(1)
    out[0] = mm_tn(scr[0][...], scr[1][...]).astype(BF)
    wait(2)
    wait(3)
    out[1] = mm_tn(scr[2][...], scr[3][...]).astype(BF)


def expert_own_kernel(meta, *refs):
    sets, got, gin, gout, scr, sem = (
        (refs[0:4], refs[4:8]), refs[8], refs[9], refs[10], refs[11:15], refs[15],
    )
    wait = bring_layer(meta[0], sets, scr, sem)
    wait(0)
    wait(1)
    gin[...] = mm_tn(scr[0][...], scr[1][...]) + got[0].astype(F32)
    wait(2)
    wait(3)
    gout[...] = mm_tn(scr[2][...], scr[3][...]) + got[1].astype(F32)


def factor_kernel(experts, slab, rows, split, meta, *refs):
    rights, lefts, ex, keep, send = refs[0:4], refs[4:8], refs[8], refs[9], refs[10]
    right = jnp.concatenate([f[0:rows] for f in rights], axis=0)
    left = jnp.concatenate([f[split:split + rows] for f in lefts], axis=0)
    grad = mm_tn(left, right).astype(BF)
    s, z = meta[0], meta[2]
    extra = ex[...]
    pad = jnp.zeros((16, grad.shape[1] - LANES), F32)
    for shard in range(2 * experts):
        at = lax.rem(shard // 2 - z + experts, experts)
        wide = jnp.concatenate(
            [extra[:, shard * slab:(shard + 1) * slab], jnp.zeros((16, LANES - slab), F32)], axis=1
        )
        block = jnp.concatenate([wide, pad], axis=1).astype(BF)

        @pl.when(s == shard % 2)
        def _():
            keep[at, 0:slab] = grad[shard * slab:(shard + 1) * slab]
            keep[at, slab:] = block

        @pl.when(s != shard % 2)
        def _():
            send[at, 0:slab] = grad[shard * slab:(shard + 1) * slab]
            send[at, slab:] = block


def finish_kernel(experts, slab, table_slab, meta, *refs):
    arrived, (qkv, out, router, gains, table) = refs[:4], refs[4:]
    s, x = meta[0], meta[1]
    extra = None
    for a in range(2):
        for b in range(2):
            block = arrived[2 * a + b]
            matrix = 2 * (x ^ b) + (s ^ a)
            main = block[0:slab].astype(F32)

            @pl.when(matrix == 3)
            def _():
                out[0] = main

            @pl.when(matrix != 3)
            def _():
                qkv[0, matrix] = main

            small = block[slab:, 0:LANES].astype(F32)
            extra = small if extra is None else extra + small
    router[0] = extra[0:experts, 0:slab]
    gains[0] = extra[experts:experts + 2, 0:slab]
    table[...] = extra[experts + 2:experts + 3, 0:table_slab]


def call(
    kernel, out_shapes, args, specs, scratch=(), us=1, name=None, vmem=62, hbm=0
):
    return pl.pallas_call(
        kernel,
        out_shape=[jax.ShapeDtypeStruct(shape, dtype) for shape, dtype in out_shapes],
        in_specs=specs,
        out_specs=[VM] * (len(out_shapes) - hbm) + [HBM] * hbm,
        scratch_shapes=list(scratch),
        compiler_params=pltpu.CompilerParams(vmem_limit_bytes=vmem * 2**20),
        cost_estimate=pl.CostEstimate(
            flops=us * 10**9, bytes_accessed=us * 3 * 10**6, transcendentals=0
        ),
        name=name,
    )(*args)


def shift(v, axis, by):
    n = lax.axis_size(axis)
    return lax.ppermute(v, axis, [(i, (i + by) % n) for i in range(n)])


def after(values, *events):
    values = tuple(values)
    return list(lax.optimization_barrier(values + events)[: len(values)])


def swap_section(v):
    return lax.ppermute(v, "section", [(0, 1), (1, 0)])


def plane_swap(v, mask):
    return lax.ppermute(v, PLANE, [(i, i ^ mask) for i in range(4)])


def plane_gather(v):
    return [v] + [plane_swap(v, m) for m in (1, 2, 3)]


def local(
    experts,
    boundary,
    seq_lengths,
    routes,
    qkv_proj,
    out_proj,
    router,
    gains,
    rel_table,
    expert_in,
    expert_out,
):
    big = experts > 8
    s = lax.axis_index("section")
    x_at = lax.axis_index("rep")
    z_at = lax.axis_index("expert")
    y_at = lax.axis_index("half")
    shards = 2 * experts
    rows, width = boundary.shape[2:]
    slab = qkv_proj.shape[2]
    table_slab = rel_table.shape[1]
    cap = max(2, rows // experts + 1)
    cap_pad = up(cap, 8)
    packed = up(experts * cap, 16)
    ff = expert_in.shape[3]
    first = s == 0

    own = boundary[0]
    got = swap_section(own[1 - s])
    x0 = jnp.where(first, own[0], got)
    g1 = jnp.where(first, got, own[1])
    lengths = seq_lengths[s, 0]
    place = jnp.stack([s, x_at, z_at, y_at, 2 * x_at + y_at]).astype(jnp.int32)
    meta = jnp.concatenate([place, lengths])
    own_routes = routes[0, :, :, 0]
    got_routes = swap_section(own_routes[1 - s])
    route_list = [
        jnp.where(first, own_routes[0], got_routes),
        jnp.where(first, got_routes, own_routes[1]),
    ]

    early = ()
    if big:
        slabs = jnp.concatenate([qkv_proj[0], out_proj], axis=0)
        whole = lax.all_gather(slabs, ("expert", "half"), axis=1, tiled=True)
        layers = lax.all_gather(whole, "section", axis=0)
        attn_w = [[layers[0]], [layers[1]]]
        plan = []
    else:
        slabs = jnp.concatenate([qkv_proj[0], out_proj], axis=0)
        piece = lax.dynamic_slice_in_dim(slabs, 2 * x_at, 2, axis=0)
        along = {1: shift(piece, "expert", 1), 3: shift(piece, "expert", 3)}
        over_y0 = plane_swap(piece, 1)
        along[2] = shift(after([piece], along[1])[0], "expert", 2)
        early = (over_y0,)

    small_rows = up(experts + 3, 8)
    table_row = jnp.pad(rel_table, ((0, 0), (0, slab - table_slab)))
    small = jnp.concatenate(
        [
            router[0].T,
            gains[0],
            table_row,
            jnp.zeros((small_rows - experts - 3, slab), BF),
        ]
    )
    (small,) = after([small], *early)
    if big:
        small_all = lax.all_gather(
            lax.all_gather(small, ("expert", "half"), axis=0), "section", axis=0
        )
    else:
        lines = jnp.stack([small] + [shift(small, "expert", i) for i in range(1, experts)])
        lines = jnp.stack([lines, shift(lines, "half", 1)])
        small_all = jnp.stack([lines, swap_section(lines)])
    head_of, offset_of = table_places(shards, slab, table_slab)
    flip = jnp.asarray(np.eye(2 * rows)[::-1], BF)
    rr = jnp.stack(route_list)
    common = [meta, small_all, rr.T, rr, head_of, offset_of]

    if not big:
        pieces, plan = [slabs], [(0, 0, 0, 0, 4)]
        pieces += [over_y0, plane_swap(over_y0, 2)]
        plan += [(0, 1, 0, 0, 2), (0, 1, 1, 0, 2)]
        for i in (1, 3, 2):
            got = along[i]
            if i == 2:
                got, x0, g1, *common = after([got, x0, g1] + common)
            over_y, over_x = plane_swap(got, 1), plane_swap(got, 2)
            pieces += [got, over_y, over_x]
            plan += [(i, 0, 0, 0, 2), (i, 1, 0, 0, 2), (i, 0, 1, 0, 2)]
            if i == 1:
                pieces.append(plane_swap(over_y, 2))
                plan.append((i, 1, 1, 0, 2))
            elif i == 3:
                pieces.append(plane_swap(over_x, 1))
                plan.append((i, 1, 1, 0, 2))
            else:
                pieces += [plane_swap(over_y[:1], 2), plane_swap(over_x[1:], 1)]
                plan += [(i, 1, 1, 0, 1), (i, 1, 1, 1, 1)]
        copied = [swap_section(v) for v in pieces]
        attn_w = [pieces + copied] * 2
    other_in = swap_section(expert_in[0, 0])
    other_out = swap_section(expert_out[0, 0])
    expert_w = [expert_in[0, 0], other_in, expert_out[0, 0], other_out]

    n_w = len(attn_w[0])
    n_ret = 1 if big else experts

    def message_shapes(parts):
        if big:
            return [((experts,) + parts + (cap_pad, width), BF)]
        return [(parts + (cap_pad, width), BF)] * experts

    def dispatch(blocks, parts):
        if big:
            arrived = lax.all_to_all(blocks[0], "expert", 0, 0, tiled=True)
            arrived = [arrived if parts == 2 else arrived[:, None]]
        else:
            arrived = [blocks[0]] + [shift(blocks[i], "expert", i) for i in range(1, experts)]
            arrived = arrived if parts == 2 else [a[None] for a in arrived]
        (joined,) = call(
            functools.partial(pack_kernel, experts, cap, parts),
            [((parts, packed, width), BF)],
            arrived,
            [VM] * len(arrived),
            us=1,
            name="pack",
            vmem=8,
        )
        return plane_gather(joined)

    def come_back(partial, parts, events=()):
        sums = [partial[0]] + [plane_swap(partial[m], m) for m in (1, 2, 3)]
        if events:
            sums = after(sums, *events)
        shapes = (
            [((experts, parts, cap_pad, width), BF)]
            if big
            else [((parts, cap_pad, width), BF)] * experts
        )
        blocks = call(
            functools.partial(unpack_kernel, experts, cap, parts),
            shapes,
            sums,
            [VM] * 4,
            us=1,
            name="unpack",
            vmem=8,
        )
        if big:
            back = lax.all_to_all(blocks[0], "expert", 0, 0, tiled=True)
            return [back if parts == 2 else back[:, 0]]
        back = [blocks[0]] + [shift(blocks[i], "expert", -i) for i in range(1, experts)]
        return back if parts == 2 else [b[0] for b in back]

    def forward(layer, extra):
        args = common + extra
        specs = [SM] + [VM] * (len(args) - 1) + [ANY] * n_w
        shapes = [
            ((rows, width), BF),
            ((3, rows, width), BF),
            ((PAIRS, 2 * rows, rows), F32),
            ((rows, width), BF),
            ((rows, width), F32),
            ((rows, width), BF),
            ((rows, experts), F32),
        ]
        if layer == 1:
            shapes += [((rows, width), BF), ((rows, width), F32)]
        fixed = len(shapes)
        shapes += message_shapes((2,) if layer == 1 else ())
        outs = call(
            functools.partial(forward_kernel, layer, experts, slab, cap_pad, n_ret, n_w, plan),
            shapes,
            args + attn_w[layer],
            specs,
            Weights.scratch(plan, width),
            us=6,
            name="attention_forward",
        )
        names = ["h1", "qkv", "p", "ctx", "mid", "h2", "probs", "x1", "y0"][:fixed]
        return dict(zip(names, outs[:fixed])), outs[fixed:]

    def backward(layer, kept, x_in, g, returned, extra):
        args = common + [flip, g, x_in] + [
            kept[n] for n in ("h1", "qkv", "p", "ctx", "mid", "h2", "probs")
        ]
        args += extra + returned
        specs = [SM] + [VM] * (len(args) - 1) + [ANY] * n_w
        shapes = [
            ((rows, width), F32),
            ((up(experts + 3, 16), width), F32),
        ] + [(((3 if layer == 1 else 1) * rows, width), BF)] * 4
        if layer == 1:
            shapes += [((rows, width), F32)] + message_shapes(())
        return call(
            functools.partial(backward_kernel, layer, experts, slab, cap_pad, n_ret, n_w, plan),
            shapes,
            args + attn_w[layer],
            specs,
            Weights.scratch(plan, width)
            + [
                pltpu.VMEM((4, rows, width), BF),
                pltpu.VMEM((4, rows, width), BF),
                pltpu.VMEM((16, LANES), F32),
            ],
            us=8 if layer else 2,
            name="attention_backward",
        )

    expert_scratch = [pltpu.VMEM((2, width, ff), BF), pltpu.SemaphoreType.DMA((2,))]
    expert_specs = [SM] + [VM] * 4 + [ANY] * 4
    all_rows = 4 * packed

    def expert_forward(layer, joined, both):
        parts = 2 if both else 1
        shapes = [((parts, packed, width), BF)] * 4
        shapes += [((all_rows, width), BF), ((all_rows, ff), BF)]
        shapes += (
            [((all_rows, width), BF), ((all_rows, ff), BF)] if both else [((all_rows, ff), F32)]
        )
        outs = call(
            functools.partial(expert_forward_kernel, layer, both),
            shapes,
            [meta] + joined + expert_w,
            expert_specs,
            expert_scratch
            + [pltpu.VMEM(*shape) for shape in shapes[4:]]
            + [pltpu.SemaphoreType.DMA((len(shapes) - 4,))],
            hbm=len(shapes) - 4,
            us=4,
            name="expert_forward",
            vmem=20,
        )
        return outs[:4], outs[4:]

    def plane_factors(factors):
        return [factors[0]] + [plane_swap(factors[m], m) for m in (1, 2, 3)]

    def attention_grads(rights, lefts, split, ex):
        keep, send = call(
            functools.partial(factor_kernel, experts, slab, rows, split),
            [((experts, slab + 16, width), BF)] * 2,
            [meta] + rights + lefts + [ex],
            [SM] + [VM] * 9,
            us=4,
            name="attention_grads",
            vmem=20,
        )
        return keep, send

    def sum_cores(keep, send):
        both = keep.astype(F32) + swap_section(send).astype(F32)
        return [both[i].astype(BF) for i in range(experts)]

    def along_z(parts):
        return [parts[0]] + [shift(parts[i], "expert", i) for i in range(1, experts)]

    def add_up(parts):
        total = parts[0].astype(F32)
        for part in parts[1:]:
            total = total + part.astype(F32)
        return total.astype(BF)

    kept0, blocks = forward(0, [x0])
    joined = dispatch(blocks, 1)
    partial, (rows0, act0, pre0) = expert_forward(0, joined, False)
    returned = come_back(partial, 1)

    kept1, blocks = forward(1, [kept0["mid"], kept0["probs"], g1] + returned)
    joined = dispatch(blocks, 2)
    partial, (rows1, act1, grows1, dpre1) = expert_forward(1, joined, True)
    returned = come_back(partial, 2)

    outs = backward(
        1, kept1, kept1["x1"], g1, returned, [kept0["probs"], kept0["h1"], kept0["ctx"]]
    )
    dx1, ex1 = outs[:2]
    factors1, out1, blocks = outs[2:6], outs[6], outs[7:]

    joined = dispatch(blocks, 1)
    shapes = [((1, packed, width), BF)] * 4 + [((all_rows, width), BF), ((all_rows, ff), BF)]
    outs = call(
        functools.partial(expert_backward_kernel, 0),
        shapes,
        [meta] + joined + expert_w + [pre0],
        expert_specs + [VM],
        expert_scratch
        + [pltpu.VMEM(*shape) for shape in shapes[4:]]
        + [pltpu.SemaphoreType.DMA((2,))],
        hbm=2,
        us=4,
        name="expert_backward",
            vmem=20,
    )
    partial, (grows0, dpre0) = outs[:4], outs[4:]
    if not big:
        beside = plane_factors(factors1)
        beside = after(beside, partial[3])
        halves1 = attention_grads(beside, beside, rows, ex1)
        returned = come_back(partial, 1, halves1)
        moved1 = along_z(after(sum_cores(*halves1), returned[0]))
    else:
        returned = come_back(partial, 1)
    outs = backward(0, kept0, x0, dx1.astype(BF), returned, [kept1["y0"]])
    dx0, ex0 = outs[:2]
    factors0 = outs[2:6]
    if not big:
        factors0 = after(factors0, *moved1)
        rights0 = plane_factors(factors0)
        halves0 = attention_grads(rights0, beside, 2 * rows, ex0)
        parts0 = sum_cores(*halves0)
        moved0 = along_z(parts0)

    traded = swap_section(jnp.where(first, out1, dx0))
    result_rows = jnp.stack([jnp.where(first, dx0, traded), jnp.where(first, traded, out1)])

    sets = [rows0, dpre0, act0, grows0, rows1, dpre1, act1, grows1]
    if not big:
        sets = after(sets, rights0[1])
    bring_scratch = [
        pltpu.VMEM((all_rows, width), BF),
        pltpu.VMEM((all_rows, ff), BF),
        pltpu.VMEM((all_rows, ff), BF),
        pltpu.VMEM((all_rows, width), BF),
        pltpu.SemaphoreType.DMA((4,)),
    ]
    (sent,) = call(
        expert_send_kernel,
        [((2, width, ff), BF)],
        [meta] + sets,
        [SM] + [ANY] * 8,
        bring_scratch,
        us=5,
        name="expert_gradients_sent",
    )
    got = swap_section(sent)

    def own_experts(sets, got):
        return call(
            expert_own_kernel,
            [((width, ff), F32), ((ff, width), F32)],
            [meta] + sets + [got],
            [SM] + [ANY] * 8 + [VM],
            bring_scratch,
            us=6,
            name="expert_gradients_own",
        )

    traded = swap_section(jnp.where(first, out1, dx0))
    result_rows = jnp.stack([jnp.where(first, dx0, traded), jnp.where(first, traded, out1)])

    if big:
        own_factors = []
        for kept, ex, fac in ((kept0, ex0, factors0), (kept1, ex1, factors1)):
            spot = 2 * x_at + y_at
            right = jnp.stack([fac[m][:rows] for m in range(4)])
            pieces = [
                jnp.sum(
                    jnp.where(
                        (jnp.arange(4) ^ spot == j)[:, None, None], right, jnp.zeros_like(right)
                    ),
                    axis=0,
                )
                for j in range(4)
            ]
            lefts = [kept["h1"]] * 3 + [kept["ctx"]]
            grad = jnp.stack(
                [
                    lax.dot_general(
                        a, b, (((0,), (0,)), ((), ())), preferred_element_type=F32
                    )
                    for a, b in zip(lefts, pieces)
                ]
            )
            own_factors.append((grad, ex[:experts + 3]))
        grad = jnp.stack([own_factors[0][0], own_factors[1][0]]).astype(BF)
        lines = jnp.stack([own_factors[0][1], own_factors[1][1]])
        grad = lax.psum_scatter(grad, "section", scatter_dimension=0)
        lines = lax.psum_scatter(lines, "section", scatter_dimension=0)
        grad = lax.psum_scatter(grad, ("expert", "half"), scatter_dimension=1, tiled=True)
        grad = lax.psum(grad, "rep").astype(F32)
        lines = lax.psum(lines, ("rep", "expert", "half"))
        shard_at = z_at * 2 + y_at
        extra = lax.dynamic_slice_in_dim(lines, shard_at * slab, slab, axis=1)
        smalls = (
            grad[None, :3],
            grad[3][None],
            extra[:experts].T[None],
            extra[experts:experts + 2][None],
            extra[experts + 2, :table_slab][None],
        )
        final_in, final_out = own_experts(sets, got)
    else:
        blocks = [add_up(moved0), add_up(moved1)]
        arrived = []
        trade = ("section", "rep", "half")
        for a in range(2):
            message = jnp.where((y_at ^ a) == 0, blocks[0], blocks[1])
            for b in range(2):
                pairs = []
                for i in range(8):
                    si, xi, yi = i // 4, (i // 2) % 2, i % 2
                    pairs.append((i, (yi ^ a) * 4 + (xi ^ b) * 2 + si))
                arrived.append(lax.ppermute(message, trade, pairs))
        final_in, final_out = own_experts(after(sets, arrived[0]), got)
        arrived = after(arrived, final_in)
        smalls = list(call(
            functools.partial(finish_kernel, experts, slab, table_slab),
            [
                ((1, 3, slab, width), F32),
                ((1, slab, width), F32),
                ((1, experts, slab), F32),
                ((1, 2, slab), F32),
                ((1, table_slab), F32),
            ],
            [meta] + arrived,
            [SM] + [VM] * 4,
            us=2,
            name="finish",
            vmem=8,
        ))
        smalls[2] = smalls[2].transpose(0, 2, 1)
    return (result_rows[None], *smalls, final_in[None, None], final_out[None, None])


def solution(mesh):
    sections, reps, shards = (mesh.shape[n] for n in ("section", "rep", "shard"))
    experts = shards // 2
    split = Mesh(
        mesh.devices.reshape(sections, reps, experts, 2), ("section", "rep", "expert", "half")
    )
    shard = ("expert", "half")
    in_specs = (
        P("section", None, ("rep",) + shard, None),
        P(None, ("rep",) + shard, None),
        P("section", None, ("rep",) + shard, None),
        P("section", None, shard, None),
        P("section", shard, None),
        P("section", shard, None),
        P("section", None, shard),
        P("section", shard),
        P("section", shard, None, "rep"),
        P("section", shard, "rep", None),
    )
    out_specs = (
        P("section", None, ("rep",) + shard, None),
        P("section", None, shard, None),
        P("section", shard, None),
        P("section", shard, None),
        P("section", None, shard),
        P("section", shard),
        P("section", shard, None, "rep"),
        P("section", shard, "rep", None),
    )
    return jax.shard_map(
        functools.partial(local, experts),
        mesh=split,
        in_specs=in_specs,
        out_specs=out_specs,
        check_vma=False,
    )
```

```python
import functools
import math

import jax
import jax.numpy as jnp
import numpy as np
from jax import lax
from jax.experimental import pallas as pl
from jax.experimental.pallas import tpu as pltpu
from jax.sharding import Mesh, PartitionSpec as P

HEADS = 12
HEAD = 64
BUCKETS = 32
SPAN = 128
PAIRS = HEADS // 2
EPSILON = 1e-06
NEGATIVE = -1e30
SCALE = 1.0 / math.sqrt(HEAD)
LANES = 128
PLANE = ("rep", "half")
BF = jnp.bfloat16
F32 = jnp.float32
VM = pl.BlockSpec(memory_space=pltpu.VMEM)
SM = pl.BlockSpec(memory_space=pltpu.SMEM)
ANY = pl.BlockSpec(memory_space=pl.ANY)
HBM = pl.BlockSpec(memory_space=pltpu.HBM)


def up(n, m):
    return -(-n // m) * m


def bucket_of(offset):
    half_count = BUCKETS // 2
    exact_count = half_count // 2
    base = half_count if offset > 0 else 0
    distance = abs(offset)
    if distance < exact_count:
        return base + distance
    bucket = exact_count + int(
        math.log(distance / exact_count)
        / math.log(SPAN / exact_count)
        * (half_count - exact_count)
    )
    return base + min(bucket, half_count - 1)


def table_places(shards, slab, table_slab):
    head_of = np.zeros((16, shards * slab), np.float32)
    offset_of = np.zeros((LANES, shards * slab), np.float32)
    for lane in range(shards * slab):
        shard, place = divmod(lane, slab)
        if place >= table_slab:
            continue
        bucket, head = divmod(shard * table_slab + place, HEADS)
        head_of[head, lane] = 1.0
        for d in range(LANES):
            if bucket_of(d if d < HEAD else d - LANES) == bucket:
                offset_of[d, lane] = 1.0
    return jnp.asarray(head_of, BF), jnp.asarray(offset_of, BF)


def mm(a, b):
    return jnp.dot(a, b, preferred_element_type=F32)


def mm_nt(a, b):
    return lax.dot_general(a, b, (((1,), (1,)), ((), ())), preferred_element_type=F32)


def mm_tn(a, b):
    return lax.dot_general(a, b, (((0,), (0,)), ((), ())), preferred_element_type=F32)


def inv_rms(v):
    return lax.rsqrt(jnp.mean(v * v, axis=-1, keepdims=True) + EPSILON)


def rms_back(v, gain, grad):
    r = inv_rms(v)
    scaled = grad * gain
    dv = r * scaled - v * (r * r * r) * jnp.mean(v * scaled, axis=-1, keepdims=True)
    return dv, jnp.sum(grad * v * r, axis=0, keepdims=True)


def tanh_parts(v):
    c = math.sqrt(2.0 / math.pi)
    return c, jnp.tanh(c * (v + 0.044715 * (v * v * v)))


def gelu(v):
    _, t = tanh_parts(v)
    return 0.5 * v * (1.0 + t)


def gelu_slope(v):
    c, t = tanh_parts(v)
    return 0.5 * (1.0 + t) + 0.5 * v * (1.0 - t * t) * (c * (1.0 + 3.0 * 0.044715 * (v * v)))


def stack_heads(pair, rows):
    lane = lax.broadcasted_iota(jnp.int32, (rows, LANES), 1)
    zero = jnp.zeros_like(pair)
    return jnp.concatenate(
        [jnp.where(lane < HEAD, pair, zero), jnp.where(lane < HEAD, zero, pair)], axis=0
    )


def pick_heads(stacked, rows):
    lane = lax.broadcasted_iota(jnp.int32, (rows, LANES), 1)
    return jnp.where(lane < HEAD, stacked[:rows], stacked[rows:])


def member_of(rc, experts):
    lane = lax.broadcasted_iota(jnp.int32, (rc.shape[0], experts), 1)
    return (lane == rc).astype(F32)


def target_slots(rc, rr, z, experts, cap_pad, big):
    rows = rc.shape[0]
    i = lax.broadcasted_iota(jnp.int32, (rows, rows), 0)
    j = lax.broadcasted_iota(jnp.int32, (rows, rows), 1)
    same = rc == rr
    before = jnp.where(same & (j < i), 1.0, 0.0)
    after = jnp.where(same & (i < j), 1.0, 0.0)

    def place(route, slot):
        if not big:
            route = jnp.where(route < z, route - z + experts, route - z)
        return route * cap_pad + slot.astype(jnp.int32)

    return (
        place(rc, jnp.sum(before, axis=1, keepdims=True)),
        place(rr, jnp.sum(after, axis=0, keepdims=True)),
    )


def small_lines(meta, small, layer, experts, slab):
    pieces = []
    for shard in range(2 * experts):
        if small.shape[0] == 2 and len(small.shape) == 4:
            block = small[layer, shard]
        else:
            at_z = lax.rem(meta[2] - shard // 2 + experts, experts)
            block = small[meta[0] ^ layer, meta[3] ^ (shard % 2), at_z]
        pieces.append(block.astype(F32))
    return jnp.concatenate(pieces, axis=1)


def same_sequence(meta, rows):
    shape = (2 * rows, rows)
    i = lax.broadcasted_iota(jnp.int32, shape, 0)
    i = jnp.where(i < rows, i, i - rows)
    j = lax.broadcasted_iota(jnp.int32, shape, 1)
    seg_i, seg_j = jnp.zeros(shape, jnp.int32), jnp.zeros(shape, jnp.int32)
    end = 0
    for n in range(5, 9):
        end = end + meta[n]
        seg_i = seg_i + (i >= end).astype(jnp.int32)
        seg_j = seg_j + (j >= end).astype(jnp.int32)
    return seg_i == seg_j


def position_bias(by_offset, head, rows):
    line = jnp.broadcast_to(by_offset[head:head + 1], (rows, LANES))
    return pltpu.roll(line, 0, 1, stride=1, stride_axis=0)[:, :rows]


def offset_sums(ds, flip):
    turned = mm(flip, ds)
    wide = jnp.concatenate([turned, jnp.zeros_like(turned)], axis=1)
    rolled = pltpu.roll(wide, 0, 1, stride=1, stride_axis=0)
    rows = ds.shape[0] // 2
    first = jnp.sum(rolled[rows:], axis=0, keepdims=True)
    second = jnp.sum(rolled[:rows], axis=0, keepdims=True)
    return [pltpu.roll(first, 1, 1), pltpu.roll(second, 1 + rows, 1)]


def split_two(v):
    high = v.astype(BF)
    return high, (v - high.astype(F32)).astype(BF)


def put_rows(target_row, block, cap_pad, values, rows):
    slot = lax.broadcasted_iota(jnp.int32, (cap_pad, rows), 0) + block * cap_pad
    return mm((slot == target_row).astype(BF), values)


def take_rows(target_col, blocks, cap_pad, rows):
    total = None
    for i, block in enumerate(blocks):
        slot = lax.broadcasted_iota(jnp.int32, (rows, cap_pad), 1) + i * cap_pad
        part = mm((slot == target_col).astype(BF), block)
        total = part if total is None else total + part
    return total


class Weights:
    def __init__(self, refs, plan, experts, slab, layer):
        self.refs, self.plan, self.experts, self.slab, self.layer = (
            refs, plan, experts, slab, layer,
        )

    @staticmethod
    def scratch(plan, width):
        return [pltpu.VMEM((4, width, width), BF), pltpu.SemaphoreType.DMA((max(1, len(plan)),))]

    def copies(self, meta, scr, sem, which):
        if not self.plan:
            return [pltpu.make_async_copy(self.refs[0], scr, sem.at[0])]
        x, z, y = meta[1], meta[2], meta[3]
        count = len(self.plan)
        made = []
        for n, (i, flip_y, flip_x, offset, held) in enumerate(self.plan):
            at_z = lax.rem(z - i + self.experts, self.experts)
            row = pl.multiple_of((at_z * 2 + (y ^ flip_y)) * self.slab, self.slab)
            matrix = 0 if held == 4 else 2 * (x ^ flip_x) + offset
            made.append(
                pltpu.make_async_copy(
                    self.refs[which * count + n],
                    scr.at[pl.ds(matrix, held), pl.ds(row, self.slab)],
                    sem.at[n],
                )
            )
        return made

    def start(self, meta, scr, sem):
        if not self.plan:
            self.copies(meta, scr, sem, 0)[0].start()
            return

        @pl.when(meta[0] == self.layer)
        def _():
            for copy in self.copies(meta, scr, sem, 0):
                copy.start()

        @pl.when(meta[0] != self.layer)
        def _():
            for copy in self.copies(meta, scr, sem, 1):
                copy.start()

    def wait(self, meta, scr, sem):
        for copy in self.copies(meta, scr, sem, 0):
            copy.wait()


def forward_kernel(layer, experts, slab, cap_pad, n_ret, n_w, plan, *refs):
    it = iter(refs)
    meta, small, rc_ref, rr_ref, head_of, offset_of = (next(it) for _ in range(6))
    if layer == 0:
        x_ref = next(it)
    else:
        mid0, probs0, g_ref = (next(it) for _ in range(3))
        ret = [next(it) for _ in range(n_ret)]
    w = Weights([next(it) for _ in range(n_w)], plan, experts, slab, layer)
    h1_ref, qkv_ref, p_ref, ctx_ref, mid_ref, h2_ref, probs_ref = (next(it) for _ in range(7))
    if layer == 1:
        x1_ref, y0_ref = next(it), next(it)
    rest = list(it)
    scr, sem = rest[-2:]
    disp = rest[:-2]
    big = not plan
    w.start(meta, scr, sem)
    rows, width = h1_ref.shape
    z = meta[2]
    rc = rc_ref[:, layer:layer + 1]
    _, tr = target_slots(rc, rr_ref[layer:layer + 1], z, experts, cap_pad, big)
    lines = small_lines(meta, small, layer, experts, slab)
    router = lines[:experts].astype(BF)
    table = (head_of[...].astype(F32) * lines[experts + 2:experts + 3]).astype(BF)
    by_offset = mm_nt(table, offset_of[...])
    keep = same_sequence(meta, rows)
    if layer == 0:
        x = x_ref[...].astype(F32)
    else:
        blocks = [ret[i][...] for i in range(n_ret)] if n_ret > 1 else [
            ret[0][i] for i in range(experts)
        ]
        rc0 = rc_ref[:, 0:1]
        tc0, _ = target_slots(rc0, rr_ref[0:1], z, experts, cap_pad, big)
        y0 = take_rows(tc0, blocks, cap_pad, rows)
        y0_ref[...] = y0
        gate0 = jnp.sum(probs0[...] * member_of(rc0, experts), axis=-1, keepdims=True)
        x1 = (mid0[...] + gate0 * y0).astype(BF)
        x1_ref[...] = x1
        x = x1.astype(F32)
    h1 = (x * inv_rms(x) * lines[experts:experts + 1]).astype(BF)
    h1_ref[...] = h1
    w.wait(meta, scr, sem)
    q = mm(h1, scr[0]).astype(BF)
    k = mm(h1, scr[1]).astype(BF)
    v = mm(h1, scr[2]).astype(BF)
    qkv_ref[0] = q
    qkv_ref[1] = k
    qkv_ref[2] = v
    pairs = range(PAIRS)
    cols = [slice(pair * LANES, (pair + 1) * LANES) for pair in pairs]
    sc = [mm_nt(stack_heads(q[:, c], rows), k[:, c]) for c in cols]
    bias = [
        jnp.concatenate([position_bias(by_offset, 2 * pair + n, rows) for n in range(2)], axis=0)
        for pair in pairs
    ]
    sc = [jnp.where(keep, sc[pair] * SCALE + bias[pair], NEGATIVE) for pair in pairs]
    top = [jnp.max(v, axis=-1, keepdims=True) for v in sc]
    e = [jnp.exp(sc[pair] - top[pair]) for pair in pairs]
    total = [jnp.sum(v, axis=-1, keepdims=True) for v in e]
    p = [e[pair] / total[pair] for pair in pairs]
    for pair in pairs:
        p_ref[pair] = p[pair]
    contexts = [mm(p[pair].astype(BF), v[:, cols[pair]]) for pair in pairs]
    contexts = [pick_heads(both, rows) for both in contexts]
    ctx = jnp.concatenate(contexts, axis=1).astype(BF)
    ctx_ref[...] = ctx
    mid = x + mm(ctx, scr[3])
    mid_ref[...] = mid
    h2 = (mid * inv_rms(mid) * lines[experts + 1:experts + 2]).astype(BF)
    h2_ref[...] = h2
    logits = mm_nt(h2, router)
    e = jnp.exp(logits - jnp.max(logits, axis=-1, keepdims=True))
    probs = e / jnp.sum(e, axis=-1, keepdims=True)
    probs_ref[...] = probs
    sent = [h2]
    if layer == 1:
        gate = jnp.sum(probs * member_of(rc, experts), axis=-1, keepdims=True)
        sent.append((gate * g_ref[...].astype(F32)).astype(BF))
    for i in range(experts):
        for part, values in enumerate(sent):
            block = put_rows(tr, i, cap_pad, values, rows).astype(BF)
            ref = disp[i] if len(disp) > 1 else disp[0].at[i]
            if layer == 1:
                ref[part] = block
            else:
                ref[...] = block


def backward_kernel(layer, experts, slab, cap_pad, n_ret, n_w, plan, *refs):
    it = iter(refs)
    meta, small, rc_ref, rr_ref, head_of, offset_of, flip = (next(it) for _ in range(7))
    g_ref, x_ref, h1_ref, qkv_ref, p_ref, ctx_ref, mid_ref, h2_ref, probs_ref = (
        next(it) for _ in range(9)
    )
    if layer == 0:
        y_ref = next(it)
    else:
        probs0, h1_0, ctx_0 = (next(it) for _ in range(3))
    ret = [next(it) for _ in range(n_ret)]
    w = Weights([next(it) for _ in range(n_w)], plan, experts, slab, layer)
    dx_ref, ex_ref = (next(it) for _ in range(2))
    factors = [next(it) for _ in range(4)]
    if layer == 1:
        out_ref = next(it)
    rest = list(it)
    scr, sem, right, left, sums = rest[-5:]
    disp = rest[:-5]
    big = not plan
    w.start(meta, scr, sem)
    rows, width = h1_ref.shape
    z = meta[2]
    rc = rc_ref[:, layer:layer + 1]
    tc, _ = target_slots(rc, rr_ref[layer:layer + 1], z, experts, cap_pad, big)
    lines = small_lines(meta, small, layer, experts, slab)
    router = lines[:experts].astype(BF)
    g = g_ref[...].astype(F32)
    mid = mid_ref[...]
    probs = probs_ref[...]
    member = member_of(rc, experts)
    gate = jnp.sum(probs * member, axis=-1, keepdims=True)

    def blocks(part):
        if layer == 0:
            return [r[...] for r in ret] if n_ret > 1 else [ret[0][i] for i in range(experts)]
        return [r[part] for r in ret] if n_ret > 1 else [ret[0][i, part] for i in range(experts)]

    if layer == 0:
        y = y_ref[...]
        dh2 = take_rows(tc, blocks(0), cap_pad, rows)
    else:
        y = take_rows(tc, blocks(0), cap_pad, rows)
        dh2 = take_rows(tc, blocks(1), cap_pad, rows)
        out_ref[...] = mid + gate * y
    dgate = jnp.sum(g * y, axis=-1, keepdims=True)
    high, low = split_two(probs * (dgate * (member - gate)))
    dh2 = dh2 + mm(high, router) + mm(low, router)
    dmid, dgain1 = rms_back(mid, lines[experts + 1:experts + 2], dh2)
    dmid = dmid + g
    h2 = h2_ref[...]
    drouter = mm_tn(high, h2) + mm_tn(low, h2)
    da = dmid.astype(BF)
    right[3] = da
    w.wait(meta, scr, sem)
    dctx = mm_nt(da, scr[3]).astype(BF)
    sums[...] = jnp.zeros_like(sums)
    pairs = range(PAIRS)
    cols = [slice(pair * LANES, (pair + 1) * LANES) for pair in pairs]
    ds_heads = [stack_heads(dctx[:, c], rows) for c in cols]
    dp = [mm_nt(ds_heads[pair], qkv_ref[2, :, cols[pair]]) for pair in pairs]
    p = [p_ref[pair] for pair in pairs]
    dv = [mm_tn(p[pair].astype(BF), ds_heads[pair]) for pair in pairs]
    weighted = [jnp.sum(p[pair] * dp[pair], axis=-1, keepdims=True) for pair in pairs]
    ds = [(p[pair] * (dp[pair] - weighted[pair])).astype(BF) for pair in pairs]
    dq = [mm(ds[pair], qkv_ref[1, :, cols[pair]]) for pair in pairs]
    dq = [pick_heads(both, rows) * SCALE for both in dq]
    dk = [
        mm_tn(ds[pair], stack_heads(qkv_ref[0, :, cols[pair]], rows)) * SCALE for pair in pairs
    ]
    by_line = [offset_sums(ds[pair], flip[...]) for pair in pairs]
    for pair in pairs:
        for n, line in enumerate(by_line[pair]):
            sums[2 * pair + n:2 * pair + n + 1] = line
    grads = (dq, dk, dv)
    dh1 = None
    for j in range(3):
        dj = jnp.concatenate(grads[j], axis=1).astype(BF)
        right[j] = dj
        part = mm_nt(dj, scr[j])
        dh1 = part if dh1 is None else dh1 + part
    dx, dgain0 = rms_back(x_ref[...].astype(F32), lines[experts:experts + 1], dh1)
    dx = dx + dmid
    dx_ref[...] = dx
    high, low = split_two(sums[...])
    by_place = (mm(high, offset_of[...]) + mm(low, offset_of[...])) * head_of[...].astype(F32)
    ex_ref[...] = jnp.zeros_like(ex_ref)
    ex_ref[0:experts] = drouter
    ex_ref[experts:experts + 1] = dgain0
    ex_ref[experts + 1:experts + 2] = dgain1
    ex_ref[experts + 2:experts + 3] = jnp.sum(by_place, axis=0, keepdims=True)
    if layer == 1:
        rc0 = rc_ref[:, 0:1]
        _, tr0 = target_slots(rc0, rr_ref[0:1], z, experts, cap_pad, big)
        gate0 = jnp.sum(probs0[...] * member_of(rc0, experts), axis=-1, keepdims=True)
        dy0 = (gate0 * dx.astype(BF).astype(F32)).astype(BF)
        for i in range(experts):
            block = put_rows(tr0, i, cap_pad, dy0, rows).astype(BF)
            ref = disp[i] if len(disp) > 1 else disp[0].at[i]
            ref[...] = block
    if layer == 1:
        left[0] = h1_ref[...]
        left[1] = ctx_ref[...]
        left[2] = h1_0[...]
        left[3] = ctx_0[...]
    place = meta[4]
    for m in range(4):
        target = place ^ m
        factors[m][0:rows] = right[target]
        if layer == 1:
            which = jnp.where(target == 3, 1, 0)
            factors[m][rows:2 * rows] = left[which]
            factors[m][2 * rows:] = left[2 + which]


def pack_kernel(n, cap, parts, *refs):
    out = refs[-1]
    blocks = refs[:-1]
    packed = out.shape[-2]
    cap_pad = blocks[0].shape[-2]
    for part in range(parts):
        total = None
        for i in range(n):
            block = blocks[i][part] if len(blocks) > 1 else blocks[0][i, part]
            row = lax.broadcasted_iota(jnp.int32, (packed, cap_pad), 0)
            slot = lax.broadcasted_iota(jnp.int32, (packed, cap_pad), 1)
            pick = ((row == slot + i * cap) & (slot < cap)).astype(BF)
            moved = mm(pick, block)
            total = moved if total is None else total + moved
        out[part] = total.astype(BF)


def unpack_kernel(n, cap, parts, *refs):
    sums, outs = refs[:4], refs[4:]
    packed = sums[0].shape[-2]
    cap_pad = outs[0].shape[-2]
    for part in range(parts):
        total = (
            sums[0][part].astype(F32)
            + sums[1][part].astype(F32)
            + sums[2][part].astype(F32)
            + sums[3][part].astype(F32)
        ).astype(BF)
        for i in range(n):
            row = lax.broadcasted_iota(jnp.int32, (cap_pad, packed), 1)
            slot = lax.broadcasted_iota(jnp.int32, (cap_pad, packed), 0)
            pick = ((row == slot + i * cap) & (slot < cap)).astype(BF)
            block = mm(pick, total).astype(BF)
            if len(outs) > 1:
                outs[i][part] = block
            else:
                outs[0][i, part] = block


def expert_weights(layer, meta, own, other, scr, sem):
    for which in range(2):
        @pl.when(meta[0] == layer)
        def _():
            pltpu.make_async_copy(own[which], scr.at[which], sem.at[which]).start()

        @pl.when(meta[0] != layer)
        def _():
            pltpu.make_async_copy(other[which], scr.at[which], sem.at[which]).start()

    def wait(which):
        pltpu.make_async_copy(own[which], scr.at[which], sem.at[which]).wait()

    return wait


def expert_forward_kernel(layer, both, *refs):
    meta, c0, c1, c2, c3, in_own, in_other, out_own, out_other = refs[:9]
    outs = refs[9:13]
    count = (len(refs) - 16) // 2
    kept = refs[13:13 + count]
    scr, sem = refs[13 + count:15 + count]
    saved, keep_sem = refs[15 + count:-1], refs[-1]

    def save(n, values):
        saved[n][...] = values
        pltpu.make_async_copy(saved[n], kept[n], keep_sem.at[n]).start()

    wait = expert_weights(layer, meta, (in_own, out_own), (in_other, out_other), scr, sem)
    packed = c0.shape[-2]
    rows = jnp.concatenate([c[0] for c in (c0, c1, c2, c3)], axis=0)
    wait(0)
    pre = mm(rows, scr[0])
    act = gelu(pre).astype(BF)
    save(0, rows)
    save(1, act)
    wait(1)
    y = mm(act, scr[1])
    for m in range(4):
        outs[m][0] = y[m * packed:(m + 1) * packed].astype(BF)
    if both:
        grad_rows = jnp.concatenate([c[1] for c in (c0, c1, c2, c3)], axis=0)
        dpre = (mm_nt(grad_rows, scr[1]) * gelu_slope(pre)).astype(BF)
        save(2, grad_rows)
        save(3, dpre)
        dh = mm_nt(dpre, scr[0])
        for m in range(4):
            outs[m][1] = dh[m * packed:(m + 1) * packed].astype(BF)
    else:
        save(2, pre)
    for n in range(count):
        pltpu.make_async_copy(saved[n], kept[n], keep_sem.at[n]).wait()


def expert_backward_kernel(layer, *refs):
    meta, c0, c1, c2, c3, in_own, in_other, out_own, out_other, pre_ref = refs[:10]
    outs = refs[10:14]
    kept, scr, sem, saved, keep_sem = refs[14:16], refs[16], refs[17], refs[18:20], refs[20]

    def copy_out(n):
        return pltpu.make_async_copy(saved[n], kept[n], keep_sem.at[n])

    wait = expert_weights(layer, meta, (in_own, out_own), (in_other, out_other), scr, sem)
    packed = c0.shape[-2]
    grad_rows = jnp.concatenate([c[0] for c in (c0, c1, c2, c3)], axis=0)
    saved[0][...] = grad_rows
    copy_out(0).start()
    slope = gelu_slope(pre_ref[...])
    wait(1)
    dpre = (mm_nt(grad_rows, scr[1]) * slope).astype(BF)
    saved[1][...] = dpre
    copy_out(1).start()
    wait(0)
    dh = mm_nt(dpre, scr[0])
    for m in range(4):
        outs[m][0] = dh[m * packed:(m + 1) * packed].astype(BF)
    copy_out(0).wait()
    copy_out(1).wait()


def bring_layer(layer_is, sets, scr, sem):
    for layer in range(2):
        @pl.when(layer_is == layer)
        def _():
            for n in range(4):
                pltpu.make_async_copy(sets[layer][n], scr[n], sem.at[n]).start()

    def wait(n):
        pltpu.make_async_copy(sets[0][n], scr[n], sem.at[n]).wait()

    return wait


def expert_send_kernel(meta, *refs):
    sets, out, scr, sem = (refs[0:4], refs[4:8]), refs[8], refs[9:13], refs[13]
    wait = bring_layer(1 - meta[0], sets, scr, sem)
    wait(0)
    wait(1)
    out[0] = mm_tn(scr[0][...], scr[1][...]).astype(BF)
    wait(2)
    wait(3)
    out[1] = mm_tn(scr[2][...], scr[3][...]).astype(BF)


def expert_own_kernel(meta, *refs):
    sets, got, gin, gout, scr, sem = (
        (refs[0:4], refs[4:8]), refs[8], refs[9], refs[10], refs[11:15], refs[15],
    )
    wait = bring_layer(meta[0], sets, scr, sem)
    wait(0)
    wait(1)
    gin[...] = mm_tn(scr[0][...], scr[1][...]) + got[0].astype(F32)
    wait(2)
    wait(3)
    gout[...] = mm_tn(scr[2][...], scr[3][...]) + got[1].astype(F32)


def factor_kernel(experts, slab, rows, split, meta, *refs):
    rights, lefts, ex, keep, send = refs[0:4], refs[4:8], refs[8], refs[9], refs[10]
    right = jnp.concatenate([f[0:rows] for f in rights], axis=0)
    left = jnp.concatenate([f[split:split + rows] for f in lefts], axis=0)
    grad = mm_tn(left, right).astype(BF)
    s, z = meta[0], meta[2]
    extra = ex[...]
    pad = jnp.zeros((16, grad.shape[1] - LANES), F32)
    for shard in range(2 * experts):
        at = lax.rem(shard // 2 - z + experts, experts)
        wide = jnp.concatenate(
            [extra[:, shard * slab:(shard + 1) * slab], jnp.zeros((16, LANES - slab), F32)], axis=1
        )
        block = jnp.concatenate([wide, pad], axis=1).astype(BF)

        @pl.when(s == shard % 2)
        def _():
            keep[at, 0:slab] = grad[shard * slab:(shard + 1) * slab]
            keep[at, slab:] = block

        @pl.when(s != shard % 2)
        def _():
            send[at, 0:slab] = grad[shard * slab:(shard + 1) * slab]
            send[at, slab:] = block


def finish_kernel(experts, slab, table_slab, meta, *refs):
    arrived, (qkv, out, router, gains, table) = refs[:4], refs[4:]
    s, x = meta[0], meta[1]
    extra = None
    for a in range(2):
        for b in range(2):
            block = arrived[2 * a + b]
            matrix = 2 * (x ^ b) + (s ^ a)
            main = block[0:slab].astype(F32)

            @pl.when(matrix == 3)
            def _():
                out[0] = main

            @pl.when(matrix != 3)
            def _():
                qkv[0, matrix] = main

            small = block[slab:, 0:LANES].astype(F32)
            extra = small if extra is None else extra + small
    router[0] = extra[0:experts, 0:slab]
    gains[0] = extra[experts:experts + 2, 0:slab]
    table[...] = extra[experts + 2:experts + 3, 0:table_slab]


def call(
    kernel, out_shapes, args, specs, scratch=(), us=1, name=None, vmem=62, hbm=0
):
    return pl.pallas_call(
        kernel,
        out_shape=[jax.ShapeDtypeStruct(shape, dtype) for shape, dtype in out_shapes],
        in_specs=specs,
        out_specs=[VM] * (len(out_shapes) - hbm) + [HBM] * hbm,
        scratch_shapes=list(scratch),
        compiler_params=pltpu.CompilerParams(vmem_limit_bytes=vmem * 2**20),
        cost_estimate=pl.CostEstimate(
            flops=us * 10**9, bytes_accessed=us * 3 * 10**6, transcendentals=0
        ),
        name=name,
    )(*args)


def shift(v, axis, by):
    n = lax.axis_size(axis)
    return lax.ppermute(v, axis, [(i, (i + by) % n) for i in range(n)])


def after(values, *events):
    values = tuple(values)
    return list(lax.optimization_barrier(values + events)[: len(values)])


def swap_section(v):
    return lax.ppermute(v, "section", [(0, 1), (1, 0)])


def plane_swap(v, mask):
    return lax.ppermute(v, PLANE, [(i, i ^ mask) for i in range(4)])


def plane_gather(v):
    return [v] + [plane_swap(v, m) for m in (1, 2, 3)]


def local(
    experts,
    boundary,
    seq_lengths,
    routes,
    qkv_proj,
    out_proj,
    router,
    gains,
    rel_table,
    expert_in,
    expert_out,
):
    big = experts > 8
    s = lax.axis_index("section")
    x_at = lax.axis_index("rep")
    z_at = lax.axis_index("expert")
    y_at = lax.axis_index("half")
    shards = 2 * experts
    rows, width = boundary.shape[2:]
    slab = qkv_proj.shape[2]
    table_slab = rel_table.shape[1]
    cap = max(2, rows // experts + 1)
    cap_pad = up(cap, 8)
    packed = up(experts * cap, 16)
    ff = expert_in.shape[3]
    first = s == 0

    own = boundary[0]
    got = swap_section(own[1 - s])
    x0 = jnp.where(first, own[0], got)
    g1 = jnp.where(first, got, own[1])
    lengths = seq_lengths[s, 0]
    place = jnp.stack([s, x_at, z_at, y_at, 2 * x_at + y_at]).astype(jnp.int32)
    meta = jnp.concatenate([place, lengths])
    own_routes = routes[0, :, :, 0]
    got_routes = swap_section(own_routes[1 - s])
    route_list = [
        jnp.where(first, own_routes[0], got_routes),
        jnp.where(first, got_routes, own_routes[1]),
    ]

    early = ()
    if big:
        slabs = jnp.concatenate([qkv_proj[0], out_proj], axis=0)
        whole = lax.all_gather(slabs, ("expert", "half"), axis=1, tiled=True)
        layers = lax.all_gather(whole, "section", axis=0)
        attn_w = [[layers[0]], [layers[1]]]
        plan = []
    else:
        slabs = jnp.concatenate([qkv_proj[0], out_proj], axis=0)
        piece = lax.dynamic_slice_in_dim(slabs, 2 * x_at, 2, axis=0)
        along = {1: shift(piece, "expert", 1), 3: shift(piece, "expert", 3)}
        over_y0 = plane_swap(piece, 1)
        along[2] = shift(after([piece], along[1])[0], "expert", 2)
        over = {1: (plane_swap(along[1], 1), plane_swap(along[1], 2))}
        early = (over[1][0],)

    small_rows = up(experts + 3, 8)
    table_row = jnp.pad(rel_table, ((0, 0), (0, slab - table_slab)))
    small = jnp.concatenate(
        [
            router[0].T,
            gains[0],
            table_row,
            jnp.zeros((small_rows - experts - 3, slab), BF),
        ]
    )
    (small,) = after([small], *early)
    if big:
        small_all = lax.all_gather(
            lax.all_gather(small, ("expert", "half"), axis=0), "section", axis=0
        )
    else:
        lines = jnp.stack([small] + [shift(small, "expert", i) for i in range(1, experts)])
        lines = jnp.stack([lines, shift(lines, "half", 1)])
        small_all = jnp.stack([lines, swap_section(lines)])
    head_of, offset_of = table_places(shards, slab, table_slab)
    flip = jnp.asarray(np.eye(2 * rows)[::-1], BF)
    rr = jnp.stack(route_list)
    common = [meta, small_all, rr.T, rr, head_of, offset_of]

    if not big:
        pieces, plan = [slabs], [(0, 0, 0, 0, 4)]
        pieces += [over_y0, plane_swap(over_y0, 2)]
        plan += [(0, 1, 0, 0, 2), (0, 1, 1, 0, 2)]
        for i in (1, 3, 2):
            got = along[i]
            if i == 2:
                got, x0, g1, meta_, *common = after([got, x0, g1, common[0]] + common[2:])
                common = [meta_, small_all] + common
            over_y, over_x = over[i] if i in over else (plane_swap(got, 1), plane_swap(got, 2))
            pieces += [got, over_y, over_x]
            plan += [(i, 0, 0, 0, 2), (i, 1, 0, 0, 2), (i, 0, 1, 0, 2)]
            if i == 1:
                pieces.append(plane_swap(over_y, 2))
                plan.append((i, 1, 1, 0, 2))
            elif i == 3:
                pieces.append(plane_swap(over_x, 1))
                plan.append((i, 1, 1, 0, 2))
            else:
                pieces += [plane_swap(over_y[:1], 2), plane_swap(over_x[1:], 1)]
                plan += [(i, 1, 1, 0, 1), (i, 1, 1, 1, 1)]
        held_back = after(pieces[:7], pieces[9])
        copied = [swap_section(v) for v in held_back + pieces[7:]]
        attn_w = [pieces + copied] * 2

    n_w = len(attn_w[0])
    n_ret = 1 if big else experts

    def message_shapes(parts):
        if big:
            return [((experts,) + parts + (cap_pad, width), BF)]
        return [(parts + (cap_pad, width), BF)] * experts

    def dispatch(blocks, parts):
        if big:
            arrived = lax.all_to_all(blocks[0], "expert", 0, 0, tiled=True)
            arrived = [arrived if parts == 2 else arrived[:, None]]
        else:
            arrived = [blocks[0]] + [shift(blocks[i], "expert", i) for i in range(1, experts)]
            arrived = arrived if parts == 2 else [a[None] for a in arrived]
        (joined,) = call(
            functools.partial(pack_kernel, experts, cap, parts),
            [((parts, packed, width), BF)],
            arrived,
            [VM] * len(arrived),
            us=1,
            name="pack",
            vmem=8,
        )
        return plane_gather(joined)

    def come_back(partial, parts, events=()):
        sums = [partial[0]] + [plane_swap(partial[m], m) for m in (1, 2, 3)]
        if events:
            sums = after(sums, *events)
        shapes = (
            [((experts, parts, cap_pad, width), BF)]
            if big
            else [((parts, cap_pad, width), BF)] * experts
        )
        blocks = call(
            functools.partial(unpack_kernel, experts, cap, parts),
            shapes,
            sums,
            [VM] * 4,
            us=1,
            name="unpack",
            vmem=8,
        )
        if big:
            back = lax.all_to_all(blocks[0], "expert", 0, 0, tiled=True)
            return [back if parts == 2 else back[:, 0]]
        back = [blocks[0]] + [shift(blocks[i], "expert", -i) for i in range(1, experts)]
        return back if parts == 2 else [b[0] for b in back]

    def forward(layer, extra):
        args = common + extra
        specs = [SM] + [VM] * (len(args) - 1) + [ANY] * n_w
        shapes = [
            ((rows, width), BF),
            ((3, rows, width), BF),
            ((PAIRS, 2 * rows, rows), F32),
            ((rows, width), BF),
            ((rows, width), F32),
            ((rows, width), BF),
            ((rows, experts), F32),
        ]
        if layer == 1:
            shapes += [((rows, width), BF), ((rows, width), F32)]
        fixed = len(shapes)
        shapes += message_shapes((2,) if layer == 1 else ())
        outs = call(
            functools.partial(forward_kernel, layer, experts, slab, cap_pad, n_ret, n_w, plan),
            shapes,
            args + attn_w[layer],
            specs,
            Weights.scratch(plan, width),
            us=6,
            name="attention_forward",
        )
        names = ["h1", "qkv", "p", "ctx", "mid", "h2", "probs", "x1", "y0"][:fixed]
        return dict(zip(names, outs[:fixed])), outs[fixed:]

    def backward(layer, kept, x_in, g, returned, extra):
        args = common + [flip, g, x_in] + [
            kept[n] for n in ("h1", "qkv", "p", "ctx", "mid", "h2", "probs")
        ]
        args += extra + returned
        specs = [SM] + [VM] * (len(args) - 1) + [ANY] * n_w
        shapes = [
            ((rows, width), F32),
            ((up(experts + 3, 16), width), F32),
        ] + [(((3 if layer == 1 else 1) * rows, width), BF)] * 4
        if layer == 1:
            shapes += [((rows, width), F32)] + message_shapes(())
        return call(
            functools.partial(backward_kernel, layer, experts, slab, cap_pad, n_ret, n_w, plan),
            shapes,
            args + attn_w[layer],
            specs,
            Weights.scratch(plan, width)
            + [
                pltpu.VMEM((4, rows, width), BF),
                pltpu.VMEM((4, rows, width), BF),
                pltpu.VMEM((16, LANES), F32),
            ],
            us=8 if layer else 2,
            name="attention_backward",
        )

    expert_scratch = [pltpu.VMEM((2, width, ff), BF), pltpu.SemaphoreType.DMA((2,))]
    expert_specs = [SM] + [VM] * 4 + [ANY] * 4
    all_rows = 4 * packed

    def expert_forward(layer, joined, both):
        parts = 2 if both else 1
        shapes = [((parts, packed, width), BF)] * 4
        shapes += [((all_rows, width), BF), ((all_rows, ff), BF)]
        shapes += (
            [((all_rows, width), BF), ((all_rows, ff), BF)] if both else [((all_rows, ff), F32)]
        )
        outs = call(
            functools.partial(expert_forward_kernel, layer, both),
            shapes,
            [meta] + joined + expert_w,
            expert_specs,
            expert_scratch
            + [pltpu.VMEM(*shape) for shape in shapes[4:]]
            + [pltpu.SemaphoreType.DMA((len(shapes) - 4,))],
            hbm=len(shapes) - 4,
            us=4,
            name="expert_forward",
            vmem=20,
        )
        return outs[:4], outs[4:]

    def plane_factors(factors):
        return [factors[0]] + [plane_swap(factors[m], m) for m in (1, 2, 3)]

    def attention_grads(rights, lefts, split, ex):
        keep, send = call(
            functools.partial(factor_kernel, experts, slab, rows, split),
            [((experts, slab + 16, width), BF)] * 2,
            [meta] + rights + lefts + [ex],
            [SM] + [VM] * 9,
            us=4,
            name="attention_grads",
            vmem=20,
        )
        return keep, send

    def sum_cores(keep, send):
        both = keep.astype(F32) + swap_section(send).astype(F32)
        return [both[i].astype(BF) for i in range(experts)]

    def along_z(parts):
        return [parts[0]] + [shift(parts[i], "expert", i) for i in range(1, experts)]

    def add_up(parts):
        total = parts[0].astype(F32)
        for part in parts[1:]:
            total = total + part.astype(F32)
        return total.astype(BF)

    kept0, blocks = forward(0, [x0])
    w_in, w_out = after([expert_in[0, 0], expert_out[0, 0]], kept0["probs"])
    expert_w = [w_in, swap_section(w_in), w_out, swap_section(w_out)]
    joined = dispatch(blocks, 1)
    partial, (rows0, act0, pre0) = expert_forward(0, joined, False)
    returned = come_back(partial, 1)

    kept1, blocks = forward(1, [kept0["mid"], kept0["probs"], g1] + returned)
    joined = dispatch(blocks, 2)
    partial, (rows1, act1, grows1, dpre1) = expert_forward(1, joined, True)
    returned = come_back(partial, 2)

    outs = backward(
        1, kept1, kept1["x1"], g1, returned, [kept0["probs"], kept0["h1"], kept0["ctx"]]
    )
    dx1, ex1 = outs[:2]
    factors1, out1, blocks = outs[2:6], outs[6], outs[7:]

    joined = dispatch(blocks, 1)
    shapes = [((1, packed, width), BF)] * 4 + [((all_rows, width), BF), ((all_rows, ff), BF)]
    outs = call(
        functools.partial(expert_backward_kernel, 0),
        shapes,
        [meta] + joined + expert_w + [pre0],
        expert_specs + [VM],
        expert_scratch
        + [pltpu.VMEM(*shape) for shape in shapes[4:]]
        + [pltpu.SemaphoreType.DMA((2,))],
        hbm=2,
        us=4,
        name="expert_backward",
            vmem=20,
    )
    partial, (grows0, dpre0) = outs[:4], outs[4:]
    if not big:
        beside = plane_factors(factors1)
        beside = after(beside, partial[3])
        halves1 = attention_grads(beside, beside, rows, ex1)
        returned = come_back(partial, 1, halves1)
        moved1 = along_z(after(sum_cores(*halves1), returned[0]))
    else:
        returned = come_back(partial, 1)
    outs = backward(0, kept0, x0, dx1.astype(BF), returned, [kept1["y0"]])
    dx0, ex0 = outs[:2]
    factors0 = outs[2:6]
    if not big:
        factors0 = after(factors0, *moved1)
        rights0 = plane_factors(factors0)
        halves0 = attention_grads(rights0, beside, 2 * rows, ex0)
        parts0 = sum_cores(*halves0)
        moved0 = along_z(parts0)

    traded = swap_section(jnp.where(first, out1, dx0))
    result_rows = jnp.stack([jnp.where(first, dx0, traded), jnp.where(first, traded, out1)])

    sets = [rows0, dpre0, act0, grows0, rows1, dpre1, act1, grows1]
    if not big:
        sets = after(sets, dx0)
    bring_scratch = [
        pltpu.VMEM((all_rows, width), BF),
        pltpu.VMEM((all_rows, ff), BF),
        pltpu.VMEM((all_rows, ff), BF),
        pltpu.VMEM((all_rows, width), BF),
        pltpu.SemaphoreType.DMA((4,)),
    ]
    (sent,) = call(
        expert_send_kernel,
        [((2, width, ff), BF)],
        [meta] + sets,
        [SM] + [ANY] * 8,
        bring_scratch,
        us=5,
        name="expert_gradients_sent",
    )
    got = swap_section(sent)

    def own_experts(sets, got):
        return call(
            expert_own_kernel,
            [((width, ff), F32), ((ff, width), F32)],
            [meta] + sets + [got],
            [SM] + [ANY] * 8 + [VM],
            bring_scratch,
            us=6,
            name="expert_gradients_own",
        )

    traded = swap_section(jnp.where(first, out1, dx0))
    result_rows = jnp.stack([jnp.where(first, dx0, traded), jnp.where(first, traded, out1)])

    if big:
        own_factors = []
        for kept, ex, fac in ((kept0, ex0, factors0), (kept1, ex1, factors1)):
            spot = 2 * x_at + y_at
            right = jnp.stack([fac[m][:rows] for m in range(4)])
            pieces = [
                jnp.sum(
                    jnp.where(
                        (jnp.arange(4) ^ spot == j)[:, None, None], right, jnp.zeros_like(right)
                    ),
                    axis=0,
                )
                for j in range(4)
            ]
            lefts = [kept["h1"]] * 3 + [kept["ctx"]]
            grad = jnp.stack(
                [
                    lax.dot_general(
                        a, b, (((0,), (0,)), ((), ())), preferred_element_type=F32
                    )
                    for a, b in zip(lefts, pieces)
                ]
            )
            own_factors.append((grad, ex[:experts + 3]))
        grad = jnp.stack([own_factors[0][0], own_factors[1][0]]).astype(BF)
        lines = jnp.stack([own_factors[0][1], own_factors[1][1]])
        grad = lax.psum_scatter(grad, "section", scatter_dimension=0)
        lines = lax.psum_scatter(lines, "section", scatter_dimension=0)
        grad = lax.psum_scatter(grad, ("expert", "half"), scatter_dimension=1, tiled=True)
        grad = lax.psum(grad, "rep").astype(F32)
        lines = lax.psum(lines, ("rep", "expert", "half"))
        shard_at = z_at * 2 + y_at
        extra = lax.dynamic_slice_in_dim(lines, shard_at * slab, slab, axis=1)
        smalls = (
            grad[None, :3],
            grad[3][None],
            extra[:experts].T[None],
            extra[experts:experts + 2][None],
            extra[experts + 2, :table_slab][None],
        )
        final_in, final_out = own_experts(sets, got)
    else:
        blocks = [add_up(moved0), add_up(moved1)]
        arrived = []
        trade = ("section", "rep", "half")
        for a in range(2):
            message = jnp.where((y_at ^ a) == 0, blocks[0], blocks[1])
            for b in range(2):
                pairs = []
                for i in range(8):
                    si, xi, yi = i // 4, (i // 2) % 2, i % 2
                    pairs.append((i, (yi ^ a) * 4 + (xi ^ b) * 2 + si))
                arrived.append(lax.ppermute(message, trade, pairs))
        final_in, final_out = own_experts(after(sets, arrived[0]), got)
        arrived = after(arrived, final_in)
        smalls = list(call(
            functools.partial(finish_kernel, experts, slab, table_slab),
            [
                ((1, 3, slab, width), F32),
                ((1, slab, width), F32),
                ((1, experts, slab), F32),
                ((1, 2, slab), F32),
                ((1, table_slab), F32),
            ],
            [meta] + arrived,
            [SM] + [VM] * 4,
            us=2,
            name="finish",
            vmem=8,
        ))
        smalls[2] = smalls[2].transpose(0, 2, 1)
    return (result_rows[None], *smalls, final_in[None, None], final_out[None, None])


def solution(mesh):
    sections, reps, shards = (mesh.shape[n] for n in ("section", "rep", "shard"))
    experts = shards // 2
    split = Mesh(
        mesh.devices.reshape(sections, reps, experts, 2), ("section", "rep", "expert", "half")
    )
    shard = ("expert", "half")
    in_specs = (
        P("section", None, ("rep",) + shard, None),
        P(None, ("rep",) + shard, None),
        P("section", None, ("rep",) + shard, None),
        P("section", None, shard, None),
        P("section", shard, None),
        P("section", shard, None),
        P("section", None, shard),
        P("section", shard),
        P("section", shard, None, "rep"),
        P("section", shard, "rep", None),
    )
    out_specs = (
        P("section", None, ("rep",) + shard, None),
        P("section", None, shard, None),
        P("section", shard, None),
        P("section", shard, None),
        P("section", None, shard),
        P("section", shard),
        P("section", shard, None, "rep"),
        P("section", shard, "rep", None),
    )
    return jax.shard_map(
        functools.partial(local, experts),
        mesh=split,
        in_specs=in_specs,
        out_specs=out_specs,
        check_vma=False,
    )
```

```python
import functools
import math

import jax
import jax.numpy as jnp
import numpy as np
from jax import lax
from jax.experimental import pallas as pl
from jax.experimental.pallas import tpu as pltpu
from jax.sharding import Mesh, PartitionSpec as P

HEADS = 12
HEAD = 64
BUCKETS = 32
SPAN = 128
PAIRS = HEADS // 2
EPSILON = 1e-06
NEGATIVE = -1e30
SCALE = 1.0 / math.sqrt(HEAD)
LANES = 128
PLANE = ("rep", "half")
BF = jnp.bfloat16
F32 = jnp.float32
VM = pl.BlockSpec(memory_space=pltpu.VMEM)
SM = pl.BlockSpec(memory_space=pltpu.SMEM)
ANY = pl.BlockSpec(memory_space=pl.ANY)
HBM = pl.BlockSpec(memory_space=pltpu.HBM)


def up(n, m):
    return -(-n // m) * m


def bucket_of(offset):
    half_count = BUCKETS // 2
    exact_count = half_count // 2
    base = half_count if offset > 0 else 0
    distance = abs(offset)
    if distance < exact_count:
        return base + distance
    bucket = exact_count + int(
        math.log(distance / exact_count)
        / math.log(SPAN / exact_count)
        * (half_count - exact_count)
    )
    return base + min(bucket, half_count - 1)


def table_places(shards, slab, table_slab):
    head_of = np.zeros((16, shards * slab), np.float32)
    offset_of = np.zeros((LANES, shards * slab), np.float32)
    for lane in range(shards * slab):
        shard, place = divmod(lane, slab)
        if place >= table_slab:
            continue
        bucket, head = divmod(shard * table_slab + place, HEADS)
        head_of[head, lane] = 1.0
        for d in range(LANES):
            if bucket_of(d if d < HEAD else d - LANES) == bucket:
                offset_of[d, lane] = 1.0
    return jnp.asarray(head_of, BF), jnp.asarray(offset_of, BF)


def mm(a, b):
    return jnp.dot(a, b, preferred_element_type=F32)


def mm_nt(a, b):
    return lax.dot_general(a, b, (((1,), (1,)), ((), ())), preferred_element_type=F32)


def mm_tn(a, b):
    return lax.dot_general(a, b, (((0,), (0,)), ((), ())), preferred_element_type=F32)


def inv_rms(v):
    return lax.rsqrt(jnp.mean(v * v, axis=-1, keepdims=True) + EPSILON)


def rms_back(v, gain, grad):
    r = inv_rms(v)
    scaled = grad * gain
    dv = r * scaled - v * (r * r * r) * jnp.mean(v * scaled, axis=-1, keepdims=True)
    return dv, jnp.sum(grad * v * r, axis=0, keepdims=True)


def tanh_parts(v):
    c = math.sqrt(2.0 / math.pi)
    return c, jnp.tanh(c * (v + 0.044715 * (v * v * v)))


def gelu(v):
    _, t = tanh_parts(v)
    return 0.5 * v * (1.0 + t)


def gelu_slope(v):
    c, t = tanh_parts(v)
    return 0.5 * (1.0 + t) + 0.5 * v * (1.0 - t * t) * (c * (1.0 + 3.0 * 0.044715 * (v * v)))


def stack_heads(pair, rows):
    lane = lax.broadcasted_iota(jnp.int32, (rows, LANES), 1)
    zero = jnp.zeros_like(pair)
    return jnp.concatenate(
        [jnp.where(lane < HEAD, pair, zero), jnp.where(lane < HEAD, zero, pair)], axis=0
    )


def pick_heads(stacked, rows):
    lane = lax.broadcasted_iota(jnp.int32, (rows, LANES), 1)
    return jnp.where(lane < HEAD, stacked[:rows], stacked[rows:])


def member_of(rc, experts):
    lane = lax.broadcasted_iota(jnp.int32, (rc.shape[0], experts), 1)
    return (lane == rc).astype(F32)


def target_slots(rc, rr, z, experts, cap_pad, big):
    rows = rc.shape[0]
    i = lax.broadcasted_iota(jnp.int32, (rows, rows), 0)
    j = lax.broadcasted_iota(jnp.int32, (rows, rows), 1)
    same = rc == rr
    before = jnp.where(same & (j < i), 1.0, 0.0)
    after = jnp.where(same & (i < j), 1.0, 0.0)

    def place(route, slot):
        if not big:
            route = jnp.where(route < z, route - z + experts, route - z)
        return route * cap_pad + slot.astype(jnp.int32)

    return (
        place(rc, jnp.sum(before, axis=1, keepdims=True)),
        place(rr, jnp.sum(after, axis=0, keepdims=True)),
    )


def small_lines(meta, small, layer, experts, slab):
    pieces = []
    for shard in range(2 * experts):
        if small.shape[0] == 2 and len(small.shape) == 4:
            block = small[layer, shard]
        else:
            at_z = lax.rem(meta[2] - shard // 2 + experts, experts)
            block = small[meta[0] ^ layer, meta[3] ^ (shard % 2), at_z]
        pieces.append(block.astype(F32))
    return jnp.concatenate(pieces, axis=1)


def same_sequence(meta, rows):
    shape = (2 * rows, rows)
    i = lax.broadcasted_iota(jnp.int32, shape, 0)
    i = jnp.where(i < rows, i, i - rows)
    j = lax.broadcasted_iota(jnp.int32, shape, 1)
    seg_i, seg_j = jnp.zeros(shape, jnp.int32), jnp.zeros(shape, jnp.int32)
    end = 0
    for n in range(5, 9):
        end = end + meta[n]
        seg_i = seg_i + (i >= end).astype(jnp.int32)
        seg_j = seg_j + (j >= end).astype(jnp.int32)
    return seg_i == seg_j


def position_bias(by_offset, head, rows):
    line = jnp.broadcast_to(by_offset[head:head + 1], (rows, LANES))
    return pltpu.roll(line, 0, 1, stride=1, stride_axis=0)[:, :rows]


def offset_sums(ds, flip):
    turned = mm(flip, ds)
    wide = jnp.concatenate([turned, jnp.zeros_like(turned)], axis=1)
    rolled = pltpu.roll(wide, 0, 1, stride=1, stride_axis=0)
    rows = ds.shape[0] // 2
    first = jnp.sum(rolled[rows:], axis=0, keepdims=True)
    second = jnp.sum(rolled[:rows], axis=0, keepdims=True)
    return [pltpu.roll(first, 1, 1), pltpu.roll(second, 1 + rows, 1)]


def split_two(v):
    high = v.astype(BF)
    return high, (v - high.astype(F32)).astype(BF)


def put_rows(target_row, block, cap_pad, values, rows):
    slot = lax.broadcasted_iota(jnp.int32, (cap_pad, rows), 0) + block * cap_pad
    return mm((slot == target_row).astype(BF), values)


def take_rows(target_col, blocks, cap_pad, rows):
    total = None
    for i, block in enumerate(blocks):
        slot = lax.broadcasted_iota(jnp.int32, (rows, cap_pad), 1) + i * cap_pad
        part = mm((slot == target_col).astype(BF), block)
        total = part if total is None else total + part
    return total


class Weights:
    def __init__(self, refs, plan, experts, slab, layer):
        self.refs, self.plan, self.experts, self.slab, self.layer = (
            refs, plan, experts, slab, layer,
        )

    @staticmethod
    def scratch(plan, width):
        return [pltpu.VMEM((4, width, width), BF), pltpu.SemaphoreType.DMA((max(1, len(plan)),))]

    def copies(self, meta, scr, sem, which):
        if not self.plan:
            return [pltpu.make_async_copy(self.refs[0], scr, sem.at[0])]
        x, z, y = meta[1], meta[2], meta[3]
        count = len(self.plan)
        made = []
        for n, (i, flip_y, flip_x, offset, held) in enumerate(self.plan):
            at_z = lax.rem(z - i + self.experts, self.experts)
            row = pl.multiple_of((at_z * 2 + (y ^ flip_y)) * self.slab, self.slab)
            matrix = 0 if held == 4 else 2 * (x ^ flip_x) + offset
            made.append(
                pltpu.make_async_copy(
                    self.refs[which * count + n],
                    scr.at[pl.ds(matrix, held), pl.ds(row, self.slab)],
                    sem.at[n],
                )
            )
        return made

    def start(self, meta, scr, sem):
        if not self.plan:
            self.copies(meta, scr, sem, 0)[0].start()
            return

        @pl.when(meta[0] == self.layer)
        def _():
            for copy in self.copies(meta, scr, sem, 0):
                copy.start()

        @pl.when(meta[0] != self.layer)
        def _():
            for copy in self.copies(meta, scr, sem, 1):
                copy.start()

    def wait(self, meta, scr, sem):
        for copy in self.copies(meta, scr, sem, 0):
            copy.wait()


def forward_kernel(layer, experts, slab, cap_pad, n_ret, n_w, plan, *refs):
    it = iter(refs)
    meta, small, rc_ref, rr_ref, head_of, offset_of = (next(it) for _ in range(6))
    if layer == 0:
        x_ref = next(it)
    else:
        mid0, probs0, g_ref = (next(it) for _ in range(3))
        ret = [next(it) for _ in range(n_ret)]
    w = Weights([next(it) for _ in range(n_w)], plan, experts, slab, layer)
    h1_ref, qkv_ref, p_ref, ctx_ref, mid_ref, h2_ref, probs_ref = (next(it) for _ in range(7))
    if layer == 1:
        x1_ref, y0_ref = next(it), next(it)
    rest = list(it)
    scr, sem = rest[-2:]
    disp = rest[:-2]
    big = not plan
    w.start(meta, scr, sem)
    rows, width = h1_ref.shape
    z = meta[2]
    rc = rc_ref[:, layer:layer + 1]
    _, tr = target_slots(rc, rr_ref[layer:layer + 1], z, experts, cap_pad, big)
    lines = small_lines(meta, small, layer, experts, slab)
    router = lines[:experts].astype(BF)
    table = (head_of[...].astype(F32) * lines[experts + 2:experts + 3]).astype(BF)
    by_offset = mm_nt(table, offset_of[...])
    keep = same_sequence(meta, rows)
    if layer == 0:
        x = x_ref[...].astype(F32)
    else:
        blocks = [ret[i][...] for i in range(n_ret)] if n_ret > 1 else [
            ret[0][i] for i in range(experts)
        ]
        rc0 = rc_ref[:, 0:1]
        tc0, _ = target_slots(rc0, rr_ref[0:1], z, experts, cap_pad, big)
        y0 = take_rows(tc0, blocks, cap_pad, rows)
        y0_ref[...] = y0
        gate0 = jnp.sum(probs0[...] * member_of(rc0, experts), axis=-1, keepdims=True)
        x1 = (mid0[...] + gate0 * y0).astype(BF)
        x1_ref[...] = x1
        x = x1.astype(F32)
    h1 = (x * inv_rms(x) * lines[experts:experts + 1]).astype(BF)
    h1_ref[...] = h1
    w.wait(meta, scr, sem)
    q = mm(h1, scr[0]).astype(BF)
    k = mm(h1, scr[1]).astype(BF)
    v = mm(h1, scr[2]).astype(BF)
    qkv_ref[0] = q
    qkv_ref[1] = k
    qkv_ref[2] = v
    pairs = range(PAIRS)
    cols = [slice(pair * LANES, (pair + 1) * LANES) for pair in pairs]
    sc = [mm_nt(stack_heads(q[:, c], rows), k[:, c]) for c in cols]
    bias = [
        jnp.concatenate([position_bias(by_offset, 2 * pair + n, rows) for n in range(2)], axis=0)
        for pair in pairs
    ]
    sc = [jnp.where(keep, sc[pair] * SCALE + bias[pair], NEGATIVE) for pair in pairs]
    top = [jnp.max(v, axis=-1, keepdims=True) for v in sc]
    e = [jnp.exp(sc[pair] - top[pair]) for pair in pairs]
    total = [jnp.sum(v, axis=-1, keepdims=True) for v in e]
    p = [e[pair] / total[pair] for pair in pairs]
    for pair in pairs:
        p_ref[pair] = p[pair]
    contexts = [mm(p[pair].astype(BF), v[:, cols[pair]]) for pair in pairs]
    contexts = [pick_heads(both, rows) for both in contexts]
    ctx = jnp.concatenate(contexts, axis=1).astype(BF)
    ctx_ref[...] = ctx
    mid = x + mm(ctx, scr[3])
    mid_ref[...] = mid
    h2 = (mid * inv_rms(mid) * lines[experts + 1:experts + 2]).astype(BF)
    h2_ref[...] = h2
    logits = mm_nt(h2, router)
    e = jnp.exp(logits - jnp.max(logits, axis=-1, keepdims=True))
    probs = e / jnp.sum(e, axis=-1, keepdims=True)
    probs_ref[...] = probs
    sent = [h2]
    if layer == 1:
        gate = jnp.sum(probs * member_of(rc, experts), axis=-1, keepdims=True)
        sent.append((gate * g_ref[...].astype(F32)).astype(BF))
    for i in range(experts):
        for part, values in enumerate(sent):
            block = put_rows(tr, i, cap_pad, values, rows).astype(BF)
            ref = disp[i] if len(disp) > 1 else disp[0].at[i]
            if layer == 1:
                ref[part] = block
            else:
                ref[...] = block


def backward_kernel(layer, experts, slab, cap_pad, n_ret, n_w, plan, *refs):
    it = iter(refs)
    meta, small, rc_ref, rr_ref, head_of, offset_of, flip = (next(it) for _ in range(7))
    g_ref, x_ref, h1_ref, qkv_ref, p_ref, ctx_ref, mid_ref, h2_ref, probs_ref = (
        next(it) for _ in range(9)
    )
    if layer == 0:
        y_ref = next(it)
    else:
        probs0, h1_0, ctx_0 = (next(it) for _ in range(3))
    ret = [next(it) for _ in range(n_ret)]
    w = Weights([next(it) for _ in range(n_w)], plan, experts, slab, layer)
    dx_ref, ex_ref = (next(it) for _ in range(2))
    factors = [next(it) for _ in range(4)]
    if layer == 1:
        out_ref = next(it)
    rest = list(it)
    scr, sem, right, left, sums = rest[-5:]
    disp = rest[:-5]
    big = not plan
    w.start(meta, scr, sem)
    rows, width = h1_ref.shape
    z = meta[2]
    rc = rc_ref[:, layer:layer + 1]
    tc, _ = target_slots(rc, rr_ref[layer:layer + 1], z, experts, cap_pad, big)
    lines = small_lines(meta, small, layer, experts, slab)
    router = lines[:experts].astype(BF)
    g = g_ref[...].astype(F32)
    mid = mid_ref[...]
    probs = probs_ref[...]
    member = member_of(rc, experts)
    gate = jnp.sum(probs * member, axis=-1, keepdims=True)

    def blocks(part):
        if layer == 0:
            return [r[...] for r in ret] if n_ret > 1 else [ret[0][i] for i in range(experts)]
        return [r[part] for r in ret] if n_ret > 1 else [ret[0][i, part] for i in range(experts)]

    if layer == 0:
        y = y_ref[...]
        dh2 = take_rows(tc, blocks(0), cap_pad, rows)
    else:
        y = take_rows(tc, blocks(0), cap_pad, rows)
        dh2 = take_rows(tc, blocks(1), cap_pad, rows)
        out_ref[...] = mid + gate * y
    dgate = jnp.sum(g * y, axis=-1, keepdims=True)
    high, low = split_two(probs * (dgate * (member - gate)))
    dh2 = dh2 + mm(high, router) + mm(low, router)
    dmid, dgain1 = rms_back(mid, lines[experts + 1:experts + 2], dh2)
    dmid = dmid + g
    h2 = h2_ref[...]
    drouter = mm_tn(high, h2) + mm_tn(low, h2)
    da = dmid.astype(BF)
    right[3] = da
    w.wait(meta, scr, sem)
    dctx = mm_nt(da, scr[3]).astype(BF)
    sums[...] = jnp.zeros_like(sums)
    pairs = range(PAIRS)
    cols = [slice(pair * LANES, (pair + 1) * LANES) for pair in pairs]
    ds_heads = [stack_heads(dctx[:, c], rows) for c in cols]
    dp = [mm_nt(ds_heads[pair], qkv_ref[2, :, cols[pair]]) for pair in pairs]
    p = [p_ref[pair] for pair in pairs]
    dv = [mm_tn(p[pair].astype(BF), ds_heads[pair]) for pair in pairs]
    weighted = [jnp.sum(p[pair] * dp[pair], axis=-1, keepdims=True) for pair in pairs]
    ds = [(p[pair] * (dp[pair] - weighted[pair])).astype(BF) for pair in pairs]
    dq = [mm(ds[pair], qkv_ref[1, :, cols[pair]]) for pair in pairs]
    dq = [pick_heads(both, rows) * SCALE for both in dq]
    dk = [
        mm_tn(ds[pair], stack_heads(qkv_ref[0, :, cols[pair]], rows)) * SCALE for pair in pairs
    ]
    by_line = [offset_sums(ds[pair], flip[...]) for pair in pairs]
    for pair in pairs:
        for n, line in enumerate(by_line[pair]):
            sums[2 * pair + n:2 * pair + n + 1] = line
    grads = (dq, dk, dv)
    dh1 = None
    for j in range(3):
        dj = jnp.concatenate(grads[j], axis=1).astype(BF)
        right[j] = dj
        part = mm_nt(dj, scr[j])
        dh1 = part if dh1 is None else dh1 + part
    dx, dgain0 = rms_back(x_ref[...].astype(F32), lines[experts:experts + 1], dh1)
    dx = dx + dmid
    dx_ref[...] = dx
    high, low = split_two(sums[...])
    by_place = (mm(high, offset_of[...]) + mm(low, offset_of[...])) * head_of[...].astype(F32)
    ex_ref[...] = jnp.zeros_like(ex_ref)
    ex_ref[0:experts] = drouter
    ex_ref[experts:experts + 1] = dgain0
    ex_ref[experts + 1:experts + 2] = dgain1
    ex_ref[experts + 2:experts + 3] = jnp.sum(by_place, axis=0, keepdims=True)
    if layer == 1:
        rc0 = rc_ref[:, 0:1]
        _, tr0 = target_slots(rc0, rr_ref[0:1], z, experts, cap_pad, big)
        gate0 = jnp.sum(probs0[...] * member_of(rc0, experts), axis=-1, keepdims=True)
        dy0 = (gate0 * dx.astype(BF).astype(F32)).astype(BF)
        for i in range(experts):
            block = put_rows(tr0, i, cap_pad, dy0, rows).astype(BF)
            ref = disp[i] if len(disp) > 1 else disp[0].at[i]
            ref[...] = block
    if layer == 1:
        left[0] = h1_ref[...]
        left[1] = ctx_ref[...]
        left[2] = h1_0[...]
        left[3] = ctx_0[...]
    place = meta[4]
    for m in range(4):
        target = place ^ m
        factors[m][0:rows] = right[target]
        if layer == 1:
            which = jnp.where(target == 3, 1, 0)
            factors[m][rows:2 * rows] = left[which]
            factors[m][2 * rows:] = left[2 + which]


def pack_kernel(n, cap, parts, *refs):
    out = refs[-1]
    blocks = refs[:-1]
    packed = out.shape[-2]
    cap_pad = blocks[0].shape[-2]
    for part in range(parts):
        total = None
        for i in range(n):
            block = blocks[i][part] if len(blocks) > 1 else blocks[0][i, part]
            row = lax.broadcasted_iota(jnp.int32, (packed, cap_pad), 0)
            slot = lax.broadcasted_iota(jnp.int32, (packed, cap_pad), 1)
            pick = ((row == slot + i * cap) & (slot < cap)).astype(BF)
            moved = mm(pick, block)
            total = moved if total is None else total + moved
        out[part] = total.astype(BF)


def unpack_kernel(n, cap, parts, *refs):
    sums, outs = refs[:4], refs[4:]
    packed = sums[0].shape[-2]
    cap_pad = outs[0].shape[-2]
    for part in range(parts):
        total = (
            sums[0][part].astype(F32)
            + sums[1][part].astype(F32)
            + sums[2][part].astype(F32)
            + sums[3][part].astype(F32)
        ).astype(BF)
        for i in range(n):
            row = lax.broadcasted_iota(jnp.int32, (cap_pad, packed), 1)
            slot = lax.broadcasted_iota(jnp.int32, (cap_pad, packed), 0)
            pick = ((row == slot + i * cap) & (slot < cap)).astype(BF)
            block = mm(pick, total).astype(BF)
            if len(outs) > 1:
                outs[i][part] = block
            else:
                outs[0][i, part] = block


def expert_weights(layer, meta, own, other, scr, sem):
    for which in range(2):
        @pl.when(meta[0] == layer)
        def _():
            pltpu.make_async_copy(own[which], scr.at[which], sem.at[which]).start()

        @pl.when(meta[0] != layer)
        def _():
            pltpu.make_async_copy(other[which], scr.at[which], sem.at[which]).start()

    def wait(which):
        pltpu.make_async_copy(own[which], scr.at[which], sem.at[which]).wait()

    return wait


def expert_forward_kernel(layer, both, *refs):
    meta, c0, c1, c2, c3, in_own, in_other, out_own, out_other = refs[:9]
    outs = refs[9:13]
    count = (len(refs) - 16) // 2
    kept = refs[13:13 + count]
    scr, sem = refs[13 + count:15 + count]
    saved, keep_sem = refs[15 + count:-1], refs[-1]

    def save(n, values):
        saved[n][...] = values
        pltpu.make_async_copy(saved[n], kept[n], keep_sem.at[n]).start()

    wait = expert_weights(layer, meta, (in_own, out_own), (in_other, out_other), scr, sem)
    packed = c0.shape[-2]
    rows = jnp.concatenate([c[0] for c in (c0, c1, c2, c3)], axis=0)
    wait(0)
    pre = mm(rows, scr[0])
    act = gelu(pre).astype(BF)
    save(0, rows)
    save(1, act)
    wait(1)
    y = mm(act, scr[1])
    for m in range(4):
        outs[m][0] = y[m * packed:(m + 1) * packed].astype(BF)
    if both:
        grad_rows = jnp.concatenate([c[1] for c in (c0, c1, c2, c3)], axis=0)
        dpre = (mm_nt(grad_rows, scr[1]) * gelu_slope(pre)).astype(BF)
        save(2, grad_rows)
        save(3, dpre)
        dh = mm_nt(dpre, scr[0])
        for m in range(4):
            outs[m][1] = dh[m * packed:(m + 1) * packed].astype(BF)
    else:
        save(2, pre)
    for n in range(count):
        pltpu.make_async_copy(saved[n], kept[n], keep_sem.at[n]).wait()


def expert_backward_kernel(layer, *refs):
    meta, c0, c1, c2, c3, in_own, in_other, out_own, out_other, pre_ref = refs[:10]
    outs = refs[10:14]
    kept, scr, sem, saved, keep_sem = refs[14:16], refs[16], refs[17], refs[18:20], refs[20]

    def copy_out(n):
        return pltpu.make_async_copy(saved[n], kept[n], keep_sem.at[n])

    wait = expert_weights(layer, meta, (in_own, out_own), (in_other, out_other), scr, sem)
    packed = c0.shape[-2]
    grad_rows = jnp.concatenate([c[0] for c in (c0, c1, c2, c3)], axis=0)
    saved[0][...] = grad_rows
    copy_out(0).start()
    slope = gelu_slope(pre_ref[...])
    wait(1)
    dpre = (mm_nt(grad_rows, scr[1]) * slope).astype(BF)
    saved[1][...] = dpre
    copy_out(1).start()
    wait(0)
    dh = mm_nt(dpre, scr[0])
    for m in range(4):
        outs[m][0] = dh[m * packed:(m + 1) * packed].astype(BF)
    copy_out(0).wait()
    copy_out(1).wait()


def bring_layer(layer_is, sets, scr, sem):
    for layer in range(2):
        @pl.when(layer_is == layer)
        def _():
            for n in range(4):
                pltpu.make_async_copy(sets[layer][n], scr[n], sem.at[n]).start()

    def wait(n):
        pltpu.make_async_copy(sets[0][n], scr[n], sem.at[n]).wait()

    return wait


def expert_send_kernel(meta, *refs):
    sets, out, scr, sem = (refs[0:4], refs[4:8]), refs[8], refs[9:13], refs[13]
    wait = bring_layer(1 - meta[0], sets, scr, sem)
    wait(0)
    wait(1)
    out[0] = mm_tn(scr[0][...], scr[1][...]).astype(BF)
    wait(2)
    wait(3)
    out[1] = mm_tn(scr[2][...], scr[3][...]).astype(BF)


def expert_own_kernel(meta, *refs):
    sets, got, gin, gout, scr, sem = (
        (refs[0:4], refs[4:8]), refs[8], refs[9], refs[10], refs[11:15], refs[15],
    )
    wait = bring_layer(meta[0], sets, scr, sem)
    wait(0)
    wait(1)
    gin[...] = mm_tn(scr[0][...], scr[1][...]) + got[0].astype(F32)
    wait(2)
    wait(3)
    gout[...] = mm_tn(scr[2][...], scr[3][...]) + got[1].astype(F32)


def factor_kernel(experts, slab, rows, split, meta, *refs):
    rights, lefts, ex, keep, send = refs[0:4], refs[4:8], refs[8], refs[9], refs[10]
    right = jnp.concatenate([f[0:rows] for f in rights], axis=0)
    left = jnp.concatenate([f[split:split + rows] for f in lefts], axis=0)
    grad = mm_tn(left, right).astype(BF)
    s, z = meta[0], meta[2]
    extra = ex[...]
    pad = jnp.zeros((16, grad.shape[1] - LANES), F32)
    for shard in range(2 * experts):
        at = lax.rem(shard // 2 - z + experts, experts)
        wide = jnp.concatenate(
            [extra[:, shard * slab:(shard + 1) * slab], jnp.zeros((16, LANES - slab), F32)], axis=1
        )
        block = jnp.concatenate([wide, pad], axis=1).astype(BF)

        @pl.when(s == shard % 2)
        def _():
            keep[at, 0:slab] = grad[shard * slab:(shard + 1) * slab]
            keep[at, slab:] = block

        @pl.when(s != shard % 2)
        def _():
            send[at, 0:slab] = grad[shard * slab:(shard + 1) * slab]
            send[at, slab:] = block


def finish_kernel(experts, slab, table_slab, meta, *refs):
    arrived, (qkv, out, router, gains, table) = refs[:4], refs[4:]
    s, x = meta[0], meta[1]
    extra = None
    for a in range(2):
        for b in range(2):
            block = arrived[2 * a + b]
            matrix = 2 * (x ^ b) + (s ^ a)
            main = block[0:slab].astype(F32)

            @pl.when(matrix == 3)
            def _():
                out[0] = main

            @pl.when(matrix != 3)
            def _():
                qkv[0, matrix] = main

            small = block[slab:, 0:LANES].astype(F32)
            extra = small if extra is None else extra + small
    router[0] = extra[0:experts, 0:slab]
    gains[0] = extra[experts:experts + 2, 0:slab]
    table[...] = extra[experts + 2:experts + 3, 0:table_slab]


def call(
    kernel, out_shapes, args, specs, scratch=(), us=1, name=None, vmem=62, hbm=0
):
    return pl.pallas_call(
        kernel,
        out_shape=[jax.ShapeDtypeStruct(shape, dtype) for shape, dtype in out_shapes],
        in_specs=specs,
        out_specs=[VM] * (len(out_shapes) - hbm) + [HBM] * hbm,
        scratch_shapes=list(scratch),
        compiler_params=pltpu.CompilerParams(vmem_limit_bytes=vmem * 2**20),
        cost_estimate=pl.CostEstimate(
            flops=us * 10**9, bytes_accessed=us * 3 * 10**6, transcendentals=0
        ),
        name=name,
    )(*args)


def shift(v, axis, by):
    n = lax.axis_size(axis)
    return lax.ppermute(v, axis, [(i, (i + by) % n) for i in range(n)])


def after(values, *events):
    values = tuple(values)
    return list(lax.optimization_barrier(values + events)[: len(values)])


def swap_section(v):
    return lax.ppermute(v, "section", [(0, 1), (1, 0)])


def plane_swap(v, mask):
    return lax.ppermute(v, PLANE, [(i, i ^ mask) for i in range(4)])


def plane_gather(v):
    return [v] + [plane_swap(v, m) for m in (1, 2, 3)]


def local(
    experts,
    boundary,
    seq_lengths,
    routes,
    qkv_proj,
    out_proj,
    router,
    gains,
    rel_table,
    expert_in,
    expert_out,
):
    big = experts > 8
    s = lax.axis_index("section")
    x_at = lax.axis_index("rep")
    z_at = lax.axis_index("expert")
    y_at = lax.axis_index("half")
    shards = 2 * experts
    rows, width = boundary.shape[2:]
    slab = qkv_proj.shape[2]
    table_slab = rel_table.shape[1]
    cap = max(2, rows // experts + 1)
    cap_pad = up(cap, 8)
    packed = up(experts * cap, 8)
    ff = expert_in.shape[3]
    first = s == 0

    own = boundary[0]
    got = swap_section(own[1 - s])
    x0 = jnp.where(first, own[0], got)
    g1 = jnp.where(first, got, own[1])
    lengths = seq_lengths[s, 0]
    place = jnp.stack([s, x_at, z_at, y_at, 2 * x_at + y_at]).astype(jnp.int32)
    meta = jnp.concatenate([place, lengths])
    own_routes = routes[0, :, :, 0]
    got_routes = swap_section(own_routes[1 - s])
    route_list = [
        jnp.where(first, own_routes[0], got_routes),
        jnp.where(first, got_routes, own_routes[1]),
    ]

    early = ()
    if big:
        slabs = jnp.concatenate([qkv_proj[0], out_proj], axis=0)
        whole = lax.all_gather(slabs, ("expert", "half"), axis=1, tiled=True)
        layers = lax.all_gather(whole, "section", axis=0)
        attn_w = [[layers[0]], [layers[1]]]
        plan = []
    else:
        slabs = jnp.concatenate([qkv_proj[0], out_proj], axis=0)
        piece = lax.dynamic_slice_in_dim(slabs, 2 * x_at, 2, axis=0)
        along = {1: shift(piece, "expert", 1), 3: shift(piece, "expert", 3)}
        over_y0 = plane_swap(piece, 1)
        along[2] = shift(after([piece], along[1])[0], "expert", 2)
        over = {1: (plane_swap(along[1], 1), plane_swap(along[1], 2))}
        early = (over[1][0],)

    small_rows = up(experts + 3, 8)
    table_row = jnp.pad(rel_table, ((0, 0), (0, slab - table_slab)))
    small = jnp.concatenate(
        [
            router[0].T,
            gains[0],
            table_row,
            jnp.zeros((small_rows - experts - 3, slab), BF),
        ]
    )
    (small,) = after([small], *early)
    if big:
        small_all = lax.all_gather(
            lax.all_gather(small, ("expert", "half"), axis=0), "section", axis=0
        )
    else:
        lines = jnp.stack([small] + [shift(small, "expert", i) for i in range(1, experts)])
        lines = jnp.stack([lines, shift(lines, "half", 1)])
        small_all = jnp.stack([lines, swap_section(lines)])
    head_of, offset_of = table_places(shards, slab, table_slab)
    flip = jnp.asarray(np.eye(2 * rows)[::-1], BF)
    rr = jnp.stack(route_list)
    common = [meta, small_all, rr.T, rr, head_of, offset_of]

    if not big:
        pieces, plan = [slabs], [(0, 0, 0, 0, 4)]
        pieces += [over_y0, plane_swap(over_y0, 2)]
        plan += [(0, 1, 0, 0, 2), (0, 1, 1, 0, 2)]
        for i in (1, 3, 2):
            got = along[i]
            if i == 2:
                got, x0, g1, meta_, *common = after([got, x0, g1, common[0]] + common[2:])
                common = [meta_, small_all] + common
            over_y, over_x = over[i] if i in over else (plane_swap(got, 1), plane_swap(got, 2))
            pieces += [got, over_y, over_x]
            plan += [(i, 0, 0, 0, 2), (i, 1, 0, 0, 2), (i, 0, 1, 0, 2)]
            if i == 1:
                pieces.append(plane_swap(over_y, 2))
                plan.append((i, 1, 1, 0, 2))
            elif i == 3:
                pieces.append(plane_swap(over_x, 1))
                plan.append((i, 1, 1, 0, 2))
            else:
                pieces += [plane_swap(over_y[:1], 2), plane_swap(over_x[1:], 1)]
                plan += [(i, 1, 1, 0, 1), (i, 1, 1, 1, 1)]
        held_back = after(pieces[:7], pieces[9])
        copied = [swap_section(v) for v in held_back + pieces[7:]]
        attn_w = [pieces + copied] * 2

    n_w = len(attn_w[0])
    n_ret = 1 if big else experts

    def message_shapes(parts):
        if big:
            return [((experts,) + parts + (cap_pad, width), BF)]
        return [(parts + (cap_pad, width), BF)] * experts

    def dispatch(blocks, parts):
        if big:
            arrived = lax.all_to_all(blocks[0], "expert", 0, 0, tiled=True)
            arrived = [arrived if parts == 2 else arrived[:, None]]
        else:
            arrived = [blocks[0]] + [shift(blocks[i], "expert", i) for i in range(1, experts)]
            arrived = arrived if parts == 2 else [a[None] for a in arrived]
        (joined,) = call(
            functools.partial(pack_kernel, experts, cap, parts),
            [((parts, packed, width), BF)],
            arrived,
            [VM] * len(arrived),
            us=1,
            name="pack",
            vmem=8,
        )
        return plane_gather(joined)

    def come_back(partial, parts, events=()):
        sums = [partial[0]] + [plane_swap(partial[m], m) for m in (1, 2, 3)]
        if events:
            sums = after(sums, *events)
        shapes = (
            [((experts, parts, cap_pad, width), BF)]
            if big
            else [((parts, cap_pad, width), BF)] * experts
        )
        blocks = call(
            functools.partial(unpack_kernel, experts, cap, parts),
            shapes,
            sums,
            [VM] * 4,
            us=1,
            name="unpack",
            vmem=8,
        )
        if big:
            back = lax.all_to_all(blocks[0], "expert", 0, 0, tiled=True)
            return [back if parts == 2 else back[:, 0]]
        back = [blocks[0]] + [shift(blocks[i], "expert", -i) for i in range(1, experts)]
        return back if parts == 2 else [b[0] for b in back]

    def forward(layer, extra):
        args = common + extra
        specs = [SM] + [VM] * (len(args) - 1) + [ANY] * n_w
        shapes = [
            ((rows, width), BF),
            ((3, rows, width), BF),
            ((PAIRS, 2 * rows, rows), F32),
            ((rows, width), BF),
            ((rows, width), F32),
            ((rows, width), BF),
            ((rows, experts), F32),
        ]
        if layer == 1:
            shapes += [((rows, width), BF), ((rows, width), F32)]
        fixed = len(shapes)
        shapes += message_shapes((2,) if layer == 1 else ())
        outs = call(
            functools.partial(forward_kernel, layer, experts, slab, cap_pad, n_ret, n_w, plan),
            shapes,
            args + attn_w[layer],
            specs,
            Weights.scratch(plan, width),
            us=6,
            name="attention_forward",
        )
        names = ["h1", "qkv", "p", "ctx", "mid", "h2", "probs", "x1", "y0"][:fixed]
        return dict(zip(names, outs[:fixed])), outs[fixed:]

    def backward(layer, kept, x_in, g, returned, extra):
        args = common + [flip, g, x_in] + [
            kept[n] for n in ("h1", "qkv", "p", "ctx", "mid", "h2", "probs")
        ]
        args += extra + returned
        specs = [SM] + [VM] * (len(args) - 1) + [ANY] * n_w
        shapes = [
            ((rows, width), F32),
            ((up(experts + 3, 16), width), F32),
        ] + [(((3 if layer == 1 else 1) * rows, width), BF)] * 4
        if layer == 1:
            shapes += [((rows, width), F32)] + message_shapes(())
        return call(
            functools.partial(backward_kernel, layer, experts, slab, cap_pad, n_ret, n_w, plan),
            shapes,
            args + attn_w[layer],
            specs,
            Weights.scratch(plan, width)
            + [
                pltpu.VMEM((4, rows, width), BF),
                pltpu.VMEM((4, rows, width), BF),
                pltpu.VMEM((16, LANES), F32),
            ],
            us=8 if layer else 2,
            name="attention_backward",
        )

    expert_scratch = [pltpu.VMEM((2, width, ff), BF), pltpu.SemaphoreType.DMA((2,))]
    expert_specs = [SM] + [VM] * 4 + [ANY] * 4
    all_rows = 4 * packed

    def expert_forward(layer, joined, both):
        parts = 2 if both else 1
        shapes = [((parts, packed, width), BF)] * 4
        shapes += [((all_rows, width), BF), ((all_rows, ff), BF)]
        shapes += (
            [((all_rows, width), BF), ((all_rows, ff), BF)] if both else [((all_rows, ff), F32)]
        )
        outs = call(
            functools.partial(expert_forward_kernel, layer, both),
            shapes,
            [meta] + joined + expert_w,
            expert_specs,
            expert_scratch
            + [pltpu.VMEM(*shape) for shape in shapes[4:]]
            + [pltpu.SemaphoreType.DMA((len(shapes) - 4,))],
            hbm=len(shapes) - 4,
            us=4,
            name="expert_forward",
            vmem=20,
        )
        return outs[:4], outs[4:]

    def plane_factors(factors):
        return [factors[0]] + [plane_swap(factors[m], m) for m in (1, 2, 3)]

    def attention_grads(rights, lefts, split, ex):
        keep, send = call(
            functools.partial(factor_kernel, experts, slab, rows, split),
            [((experts, slab + 16, width), BF)] * 2,
            [meta] + rights + lefts + [ex],
            [SM] + [VM] * 9,
            us=4,
            name="attention_grads",
            vmem=20,
        )
        return keep, send

    def sum_cores(keep, send):
        both = keep.astype(F32) + swap_section(send).astype(F32)
        return [both[i].astype(BF) for i in range(experts)]

    def along_z(parts):
        return [parts[0]] + [shift(parts[i], "expert", i) for i in range(1, experts)]

    def add_up(parts):
        total = parts[0].astype(F32)
        for part in parts[1:]:
            total = total + part.astype(F32)
        return total.astype(BF)

    kept0, blocks = forward(0, [x0])
    w_in, w_out = after([expert_in[0, 0], expert_out[0, 0]], kept0["probs"])
    expert_w = [w_in, swap_section(w_in), w_out, swap_section(w_out)]
    joined = dispatch(blocks, 1)
    partial, (rows0, act0, pre0) = expert_forward(0, joined, False)
    returned = come_back(partial, 1)

    kept1, blocks = forward(1, [kept0["mid"], kept0["probs"], g1] + returned)
    joined = dispatch(blocks, 2)
    partial, (rows1, act1, grows1, dpre1) = expert_forward(1, joined, True)
    returned = come_back(partial, 2)

    outs = backward(
        1, kept1, kept1["x1"], g1, returned, [kept0["probs"], kept0["h1"], kept0["ctx"]]
    )
    dx1, ex1 = outs[:2]
    factors1, out1, blocks = outs[2:6], outs[6], outs[7:]

    joined = dispatch(blocks, 1)
    shapes = [((1, packed, width), BF)] * 4 + [((all_rows, width), BF), ((all_rows, ff), BF)]
    outs = call(
        functools.partial(expert_backward_kernel, 0),
        shapes,
        [meta] + joined + expert_w + [pre0],
        expert_specs + [VM],
        expert_scratch
        + [pltpu.VMEM(*shape) for shape in shapes[4:]]
        + [pltpu.SemaphoreType.DMA((2,))],
        hbm=2,
        us=4,
        name="expert_backward",
            vmem=20,
    )
    partial, (grows0, dpre0) = outs[:4], outs[4:]
    if not big:
        beside = plane_factors(factors1)
        beside = after(beside, partial[3])
        halves1 = attention_grads(beside, beside, rows, ex1)
        returned = come_back(partial, 1, halves1)
        moved1 = along_z(after(sum_cores(*halves1), returned[0]))
    else:
        returned = come_back(partial, 1)
    outs = backward(0, kept0, x0, dx1.astype(BF), returned, [kept1["y0"]])
    dx0, ex0 = outs[:2]
    factors0 = outs[2:6]
    if not big:
        factors0 = after(factors0, *moved1)
        rights0 = plane_factors(factors0)
        halves0 = attention_grads(rights0, beside, 2 * rows, ex0)
        parts0 = sum_cores(*halves0)
        moved0 = along_z(parts0)

    traded = swap_section(jnp.where(first, out1, dx0))
    result_rows = jnp.stack([jnp.where(first, dx0, traded), jnp.where(first, traded, out1)])

    sets = [rows0, dpre0, act0, grows0, rows1, dpre1, act1, grows1]
    if not big:
        sets = after(sets, dx0)
    bring_scratch = [
        pltpu.VMEM((all_rows, width), BF),
        pltpu.VMEM((all_rows, ff), BF),
        pltpu.VMEM((all_rows, ff), BF),
        pltpu.VMEM((all_rows, width), BF),
        pltpu.SemaphoreType.DMA((4,)),
    ]
    (sent,) = call(
        expert_send_kernel,
        [((2, width, ff), BF)],
        [meta] + sets,
        [SM] + [ANY] * 8,
        bring_scratch,
        us=5,
        name="expert_gradients_sent",
    )
    got = swap_section(sent)

    def own_experts(sets, got):
        return call(
            expert_own_kernel,
            [((width, ff), F32), ((ff, width), F32)],
            [meta] + sets + [got],
            [SM] + [ANY] * 8 + [VM],
            bring_scratch,
            us=6,
            name="expert_gradients_own",
        )

    traded = swap_section(jnp.where(first, out1, dx0))
    result_rows = jnp.stack([jnp.where(first, dx0, traded), jnp.where(first, traded, out1)])

    if big:
        own_factors = []
        for kept, ex, fac in ((kept0, ex0, factors0), (kept1, ex1, factors1)):
            spot = 2 * x_at + y_at
            right = jnp.stack([fac[m][:rows] for m in range(4)])
            pieces = [
                jnp.sum(
                    jnp.where(
                        (jnp.arange(4) ^ spot == j)[:, None, None], right, jnp.zeros_like(right)
                    ),
                    axis=0,
                )
                for j in range(4)
            ]
            lefts = [kept["h1"]] * 3 + [kept["ctx"]]
            grad = jnp.stack(
                [
                    lax.dot_general(
                        a, b, (((0,), (0,)), ((), ())), preferred_element_type=F32
                    )
                    for a, b in zip(lefts, pieces)
                ]
            )
            own_factors.append((grad, ex[:experts + 3]))
        grad = jnp.stack([own_factors[0][0], own_factors[1][0]]).astype(BF)
        lines = jnp.stack([own_factors[0][1], own_factors[1][1]])
        grad = lax.psum_scatter(grad, "section", scatter_dimension=0)
        lines = lax.psum_scatter(lines, "section", scatter_dimension=0)
        grad = lax.psum_scatter(grad, ("expert", "half"), scatter_dimension=1, tiled=True)
        grad = lax.psum(grad, "rep").astype(F32)
        lines = lax.psum(lines, ("rep", "expert", "half"))
        shard_at = z_at * 2 + y_at
        extra = lax.dynamic_slice_in_dim(lines, shard_at * slab, slab, axis=1)
        smalls = (
            grad[None, :3],
            grad[3][None],
            extra[:experts].T[None],
            extra[experts:experts + 2][None],
            extra[experts + 2, :table_slab][None],
        )
        final_in, final_out = own_experts(sets, got)
    else:
        blocks = [add_up(moved0), add_up(moved1)]
        arrived = []
        trade = ("section", "rep", "half")
        for a in range(2):
            message = jnp.where((y_at ^ a) == 0, blocks[0], blocks[1])
            for b in range(2):
                pairs = []
                for i in range(8):
                    si, xi, yi = i // 4, (i // 2) % 2, i % 2
                    pairs.append((i, (yi ^ a) * 4 + (xi ^ b) * 2 + si))
                arrived.append(lax.ppermute(message, trade, pairs))
        final_in, final_out = own_experts(after(sets, arrived[0]), got)
        arrived = after(arrived, final_in)
        smalls = list(call(
            functools.partial(finish_kernel, experts, slab, table_slab),
            [
                ((1, 3, slab, width), F32),
                ((1, slab, width), F32),
                ((1, experts, slab), F32),
                ((1, 2, slab), F32),
                ((1, table_slab), F32),
            ],
            [meta] + arrived,
            [SM] + [VM] * 4,
            us=2,
            name="finish",
            vmem=8,
        ))
        smalls[2] = smalls[2].transpose(0, 2, 1)
    return (result_rows[None], *smalls, final_in[None, None], final_out[None, None])


def solution(mesh):
    sections, reps, shards = (mesh.shape[n] for n in ("section", "rep", "shard"))
    experts = shards // 2
    split = Mesh(
        mesh.devices.reshape(sections, reps, experts, 2), ("section", "rep", "expert", "half")
    )
    shard = ("expert", "half")
    in_specs = (
        P("section", None, ("rep",) + shard, None),
        P(None, ("rep",) + shard, None),
        P("section", None, ("rep",) + shard, None),
        P("section", None, shard, None),
        P("section", shard, None),
        P("section", shard, None),
        P("section", None, shard),
        P("section", shard),
        P("section", shard, None, "rep"),
        P("section", shard, "rep", None),
    )
    out_specs = (
        P("section", None, ("rep",) + shard, None),
        P("section", None, shard, None),
        P("section", shard, None),
        P("section", shard, None),
        P("section", None, shard),
        P("section", shard),
        P("section", shard, None, "rep"),
        P("section", shard, "rep", None),
    )
    return jax.shard_map(
        functools.partial(local, experts),
        mesh=split,
        in_specs=in_specs,
        out_specs=out_specs,
        check_vma=False,
    )
```

```python
import functools
import math

import jax
import jax.numpy as jnp
import numpy as np
from jax import lax
from jax.experimental import pallas as pl
from jax.experimental.pallas import tpu as pltpu
from jax.sharding import Mesh, PartitionSpec as P

HEADS = 12
HEAD = 64
BUCKETS = 32
SPAN = 128
PAIRS = HEADS // 2
EPSILON = 1e-06
NEGATIVE = -1e30
SCALE = 1.0 / math.sqrt(HEAD)
LANES = 128
PLANE = ("rep", "half")
BF = jnp.bfloat16
F32 = jnp.float32
VM = pl.BlockSpec(memory_space=pltpu.VMEM)
SM = pl.BlockSpec(memory_space=pltpu.SMEM)
ANY = pl.BlockSpec(memory_space=pl.ANY)
HBM = pl.BlockSpec(memory_space=pltpu.HBM)


def up(n, m):
    return -(-n // m) * m


def bucket_of(offset):
    half_count = BUCKETS // 2
    exact_count = half_count // 2
    base = half_count if offset > 0 else 0
    distance = abs(offset)
    if distance < exact_count:
        return base + distance
    bucket = exact_count + int(
        math.log(distance / exact_count)
        / math.log(SPAN / exact_count)
        * (half_count - exact_count)
    )
    return base + min(bucket, half_count - 1)


def table_places(shards, slab, table_slab):
    head_of = np.zeros((16, shards * slab), np.float32)
    offset_of = np.zeros((LANES, shards * slab), np.float32)
    for lane in range(shards * slab):
        shard, place = divmod(lane, slab)
        if place >= table_slab:
            continue
        bucket, head = divmod(shard * table_slab + place, HEADS)
        head_of[head, lane] = 1.0
        for d in range(LANES):
            if bucket_of(d if d < HEAD else d - LANES) == bucket:
                offset_of[d, lane] = 1.0
    return jnp.asarray(head_of, BF), jnp.asarray(offset_of, BF)


def mm(a, b):
    return jnp.dot(a, b, preferred_element_type=F32)


def mm_nt(a, b):
    return lax.dot_general(a, b, (((1,), (1,)), ((), ())), preferred_element_type=F32)


def mm_tn(a, b):
    return lax.dot_general(a, b, (((0,), (0,)), ((), ())), preferred_element_type=F32)


def inv_rms(v):
    return lax.rsqrt(jnp.mean(v * v, axis=-1, keepdims=True) + EPSILON)


def rms_back(v, gain, grad):
    r = inv_rms(v)
    scaled = grad * gain
    dv = r * scaled - v * (r * r * r) * jnp.mean(v * scaled, axis=-1, keepdims=True)
    return dv, jnp.sum(grad * v * r, axis=0, keepdims=True)


def tanh_parts(v):
    c = math.sqrt(2.0 / math.pi)
    return c, jnp.tanh(c * (v + 0.044715 * (v * v * v)))


def gelu(v):
    _, t = tanh_parts(v)
    return 0.5 * v * (1.0 + t)


def gelu_slope(v):
    c, t = tanh_parts(v)
    return 0.5 * (1.0 + t) + 0.5 * v * (1.0 - t * t) * (c * (1.0 + 3.0 * 0.044715 * (v * v)))


def stack_heads(pair, rows):
    lane = lax.broadcasted_iota(jnp.int32, (rows, LANES), 1)
    zero = jnp.zeros_like(pair)
    return jnp.concatenate(
        [jnp.where(lane < HEAD, pair, zero), jnp.where(lane < HEAD, zero, pair)], axis=0
    )


def pick_heads(stacked, rows):
    lane = lax.broadcasted_iota(jnp.int32, (rows, LANES), 1)
    return jnp.where(lane < HEAD, stacked[:rows], stacked[rows:])


def member_of(rc, experts):
    lane = lax.broadcasted_iota(jnp.int32, (rc.shape[0], experts), 1)
    return (lane == rc).astype(F32)


def target_slots(rc, rr, z, experts, cap_pad, big):
    rows = rc.shape[0]
    i = lax.broadcasted_iota(jnp.int32, (rows, rows), 0)
    j = lax.broadcasted_iota(jnp.int32, (rows, rows), 1)
    same = rc == rr
    before = jnp.where(same & (j < i), 1.0, 0.0)
    after = jnp.where(same & (i < j), 1.0, 0.0)

    def place(route, slot):
        if not big:
            route = jnp.where(route < z, route - z + experts, route - z)
        return route * cap_pad + slot.astype(jnp.int32)

    return (
        place(rc, jnp.sum(before, axis=1, keepdims=True)),
        place(rr, jnp.sum(after, axis=0, keepdims=True)),
    )


def small_lines(meta, small, layer, experts, slab):
    pieces = []
    for shard in range(2 * experts):
        if small.shape[0] == 2 and len(small.shape) == 4:
            block = small[layer, shard]
        else:
            at_z = lax.rem(meta[2] - shard // 2 + experts, experts)
            block = small[meta[0] ^ layer, meta[3] ^ (shard % 2), at_z]
        pieces.append(block.astype(F32))
    return jnp.concatenate(pieces, axis=1)


def same_sequence(meta, rows):
    shape = (2 * rows, rows)
    i = lax.broadcasted_iota(jnp.int32, shape, 0)
    i = jnp.where(i < rows, i, i - rows)
    j = lax.broadcasted_iota(jnp.int32, shape, 1)
    seg_i, seg_j = jnp.zeros(shape, jnp.int32), jnp.zeros(shape, jnp.int32)
    end = 0
    for n in range(5, 9):
        end = end + meta[n]
        seg_i = seg_i + (i >= end).astype(jnp.int32)
        seg_j = seg_j + (j >= end).astype(jnp.int32)
    return seg_i == seg_j


def position_bias(by_offset, head, rows):
    line = jnp.broadcast_to(by_offset[head:head + 1], (rows, LANES))
    return pltpu.roll(line, 0, 1, stride=1, stride_axis=0)[:, :rows]


def offset_sums(ds, flip):
    turned = mm(flip, ds)
    wide = jnp.concatenate([turned, jnp.zeros_like(turned)], axis=1)
    rolled = pltpu.roll(wide, 0, 1, stride=1, stride_axis=0)
    rows = ds.shape[0] // 2
    first = jnp.sum(rolled[rows:], axis=0, keepdims=True)
    second = jnp.sum(rolled[:rows], axis=0, keepdims=True)
    return [pltpu.roll(first, 1, 1), pltpu.roll(second, 1 + rows, 1)]


def split_two(v):
    high = v.astype(BF)
    return high, (v - high.astype(F32)).astype(BF)


def put_rows(target_row, block, cap_pad, values, rows):
    slot = lax.broadcasted_iota(jnp.int32, (cap_pad, rows), 0) + block * cap_pad
    return mm((slot == target_row).astype(BF), values)


def take_rows(target_col, blocks, cap_pad, rows):
    total = None
    for i, block in enumerate(blocks):
        slot = lax.broadcasted_iota(jnp.int32, (rows, cap_pad), 1) + i * cap_pad
        part = mm((slot == target_col).astype(BF), block)
        total = part if total is None else total + part
    return total


class Weights:
    def __init__(self, refs, plan, experts, slab, layer):
        self.refs, self.plan, self.experts, self.slab, self.layer = (
            refs, plan, experts, slab, layer,
        )

    @staticmethod
    def scratch(plan, width):
        return [pltpu.VMEM((4, width, width), BF), pltpu.SemaphoreType.DMA((max(1, len(plan)),))]

    def copies(self, meta, scr, sem, which):
        if not self.plan:
            return [pltpu.make_async_copy(self.refs[0], scr, sem.at[0])]
        x, z, y = meta[1], meta[2], meta[3]
        count = len(self.plan)
        made = []
        for n, (i, flip_y, flip_x, offset, held) in enumerate(self.plan):
            at_z = lax.rem(z - i + self.experts, self.experts)
            row = pl.multiple_of((at_z * 2 + (y ^ flip_y)) * self.slab, self.slab)
            matrix = 0 if held == 4 else 2 * (x ^ flip_x) + offset
            made.append(
                pltpu.make_async_copy(
                    self.refs[which * count + n],
                    scr.at[pl.ds(matrix, held), pl.ds(row, self.slab)],
                    sem.at[n],
                )
            )
        return made

    def start(self, meta, scr, sem):
        if not self.plan:
            self.copies(meta, scr, sem, 0)[0].start()
            return

        @pl.when(meta[0] == self.layer)
        def _():
            for copy in self.copies(meta, scr, sem, 0):
                copy.start()

        @pl.when(meta[0] != self.layer)
        def _():
            for copy in self.copies(meta, scr, sem, 1):
                copy.start()

    def wait(self, meta, scr, sem):
        for copy in self.copies(meta, scr, sem, 0):
            copy.wait()


def forward_kernel(layer, experts, slab, cap_pad, n_ret, n_w, plan, *refs):
    it = iter(refs)
    meta, small, rc_ref, rr_ref, head_of, offset_of = (next(it) for _ in range(6))
    if layer == 0:
        x_ref = next(it)
    else:
        mid0, probs0, g_ref = (next(it) for _ in range(3))
        ret = [next(it) for _ in range(n_ret)]
    w = Weights([next(it) for _ in range(n_w)], plan, experts, slab, layer)
    h1_ref, qkv_ref, p_ref, ctx_ref, mid_ref, h2_ref, probs_ref = (next(it) for _ in range(7))
    if layer == 1:
        x1_ref, y0_ref = next(it), next(it)
    rest = list(it)
    scr, sem = rest[-2:]
    disp = rest[:-2]
    big = not plan
    w.start(meta, scr, sem)
    rows, width = h1_ref.shape
    z = meta[2]
    rc = rc_ref[:, layer:layer + 1]
    _, tr = target_slots(rc, rr_ref[layer:layer + 1], z, experts, cap_pad, big)
    lines = small_lines(meta, small, layer, experts, slab)
    router = lines[:experts].astype(BF)
    table = (head_of[...].astype(F32) * lines[experts + 2:experts + 3]).astype(BF)
    by_offset = mm_nt(table, offset_of[...])
    keep = same_sequence(meta, rows)
    if layer == 0:
        x = x_ref[...].astype(F32)
    else:
        blocks = [ret[i][...] for i in range(n_ret)] if n_ret > 1 else [
            ret[0][i] for i in range(experts)
        ]
        rc0 = rc_ref[:, 0:1]
        tc0, _ = target_slots(rc0, rr_ref[0:1], z, experts, cap_pad, big)
        y0 = take_rows(tc0, blocks, cap_pad, rows)
        y0_ref[...] = y0
        gate0 = jnp.sum(probs0[...] * member_of(rc0, experts), axis=-1, keepdims=True)
        x1 = (mid0[...] + gate0 * y0).astype(BF)
        x1_ref[...] = x1
        x = x1.astype(F32)
    h1 = (x * inv_rms(x) * lines[experts:experts + 1]).astype(BF)
    h1_ref[...] = h1
    w.wait(meta, scr, sem)
    q = mm(h1, scr[0]).astype(BF)
    k = mm(h1, scr[1]).astype(BF)
    v = mm(h1, scr[2]).astype(BF)
    qkv_ref[0] = q
    qkv_ref[1] = k
    qkv_ref[2] = v
    pairs = range(PAIRS)
    cols = [slice(pair * LANES, (pair + 1) * LANES) for pair in pairs]
    sc = [mm_nt(stack_heads(q[:, c], rows), k[:, c]) for c in cols]
    bias = [
        jnp.concatenate([position_bias(by_offset, 2 * pair + n, rows) for n in range(2)], axis=0)
        for pair in pairs
    ]
    sc = [jnp.where(keep, sc[pair] * SCALE + bias[pair], NEGATIVE) for pair in pairs]
    top = [jnp.max(v, axis=-1, keepdims=True) for v in sc]
    e = [jnp.exp(sc[pair] - top[pair]) for pair in pairs]
    total = [jnp.sum(v, axis=-1, keepdims=True) for v in e]
    p = [e[pair] / total[pair] for pair in pairs]
    for pair in pairs:
        p_ref[pair] = p[pair]
    contexts = [mm(p[pair].astype(BF), v[:, cols[pair]]) for pair in pairs]
    contexts = [pick_heads(both, rows) for both in contexts]
    ctx = jnp.concatenate(contexts, axis=1).astype(BF)
    ctx_ref[...] = ctx
    mid = x + mm(ctx, scr[3])
    mid_ref[...] = mid
    h2 = (mid * inv_rms(mid) * lines[experts + 1:experts + 2]).astype(BF)
    h2_ref[...] = h2
    logits = mm_nt(h2, router)
    e = jnp.exp(logits - jnp.max(logits, axis=-1, keepdims=True))
    probs = e / jnp.sum(e, axis=-1, keepdims=True)
    probs_ref[...] = probs
    sent = [h2]
    if layer == 1:
        gate = jnp.sum(probs * member_of(rc, experts), axis=-1, keepdims=True)
        sent.append((gate * g_ref[...].astype(F32)).astype(BF))
    for i in range(experts):
        for part, values in enumerate(sent):
            block = put_rows(tr, i, cap_pad, values, rows).astype(BF)
            ref = disp[i] if len(disp) > 1 else disp[0].at[i]
            if layer == 1:
                ref[part] = block
            else:
                ref[...] = block


def backward_kernel(layer, experts, slab, cap_pad, n_ret, n_w, plan, *refs):
    it = iter(refs)
    meta, small, rc_ref, rr_ref, head_of, offset_of, flip = (next(it) for _ in range(7))
    g_ref, x_ref, h1_ref, qkv_ref, p_ref, ctx_ref, mid_ref, h2_ref, probs_ref = (
        next(it) for _ in range(9)
    )
    if layer == 0:
        y_ref = next(it)
    else:
        probs0, h1_0, ctx_0 = (next(it) for _ in range(3))
    ret = [next(it) for _ in range(n_ret)]
    w = Weights([next(it) for _ in range(n_w)], plan, experts, slab, layer)
    dx_ref, ex_ref = (next(it) for _ in range(2))
    factors = [next(it) for _ in range(4)]
    if layer == 1:
        out_ref = next(it)
    rest = list(it)
    scr, sem, right, left, sums = rest[-5:]
    disp = rest[:-5]
    big = not plan
    w.start(meta, scr, sem)
    rows, width = h1_ref.shape
    z = meta[2]
    rc = rc_ref[:, layer:layer + 1]
    tc, _ = target_slots(rc, rr_ref[layer:layer + 1], z, experts, cap_pad, big)
    lines = small_lines(meta, small, layer, experts, slab)
    router = lines[:experts].astype(BF)
    g = g_ref[...].astype(F32)
    mid = mid_ref[...]
    probs = probs_ref[...]
    member = member_of(rc, experts)
    gate = jnp.sum(probs * member, axis=-1, keepdims=True)

    def blocks(part):
        if layer == 0:
            return [r[...] for r in ret] if n_ret > 1 else [ret[0][i] for i in range(experts)]
        return [r[part] for r in ret] if n_ret > 1 else [ret[0][i, part] for i in range(experts)]

    if layer == 0:
        y = y_ref[...]
        dh2 = take_rows(tc, blocks(0), cap_pad, rows)
    else:
        y = take_rows(tc, blocks(0), cap_pad, rows)
        dh2 = take_rows(tc, blocks(1), cap_pad, rows)
        out_ref[...] = mid + gate * y
    dgate = jnp.sum(g * y, axis=-1, keepdims=True)
    high, low = split_two(probs * (dgate * (member - gate)))
    dh2 = dh2 + mm(high, router) + mm(low, router)
    dmid, dgain1 = rms_back(mid, lines[experts + 1:experts + 2], dh2)
    dmid = dmid + g
    h2 = h2_ref[...]
    drouter = mm_tn(high, h2) + mm_tn(low, h2)
    da = dmid.astype(BF)
    right[3] = da
    w.wait(meta, scr, sem)
    dctx = mm_nt(da, scr[3]).astype(BF)
    sums[...] = jnp.zeros_like(sums)
    pairs = range(PAIRS)
    cols = [slice(pair * LANES, (pair + 1) * LANES) for pair in pairs]
    ds_heads = [stack_heads(dctx[:, c], rows) for c in cols]
    dp = [mm_nt(ds_heads[pair], qkv_ref[2, :, cols[pair]]) for pair in pairs]
    p = [p_ref[pair] for pair in pairs]
    dv = [mm_tn(p[pair].astype(BF), ds_heads[pair]) for pair in pairs]
    weighted = [jnp.sum(p[pair] * dp[pair], axis=-1, keepdims=True) for pair in pairs]
    ds = [(p[pair] * (dp[pair] - weighted[pair])).astype(BF) for pair in pairs]
    dq = [mm(ds[pair], qkv_ref[1, :, cols[pair]]) for pair in pairs]
    dq = [pick_heads(both, rows) * SCALE for both in dq]
    dk = [
        mm_tn(ds[pair], stack_heads(qkv_ref[0, :, cols[pair]], rows)) * SCALE for pair in pairs
    ]
    by_line = [offset_sums(ds[pair], flip[...]) for pair in pairs]
    for pair in pairs:
        for n, line in enumerate(by_line[pair]):
            sums[2 * pair + n:2 * pair + n + 1] = line
    grads = (dq, dk, dv)
    dh1 = None
    for j in range(3):
        dj = jnp.concatenate(grads[j], axis=1).astype(BF)
        right[j] = dj
        part = mm_nt(dj, scr[j])
        dh1 = part if dh1 is None else dh1 + part
    dx, dgain0 = rms_back(x_ref[...].astype(F32), lines[experts:experts + 1], dh1)
    dx = dx + dmid
    dx_ref[...] = dx
    high, low = split_two(sums[...])
    by_place = (mm(high, offset_of[...]) + mm(low, offset_of[...])) * head_of[...].astype(F32)
    ex_ref[...] = jnp.zeros_like(ex_ref)
    ex_ref[0:experts] = drouter
    ex_ref[experts:experts + 1] = dgain0
    ex_ref[experts + 1:experts + 2] = dgain1
    ex_ref[experts + 2:experts + 3] = jnp.sum(by_place, axis=0, keepdims=True)
    if layer == 1:
        rc0 = rc_ref[:, 0:1]
        _, tr0 = target_slots(rc0, rr_ref[0:1], z, experts, cap_pad, big)
        gate0 = jnp.sum(probs0[...] * member_of(rc0, experts), axis=-1, keepdims=True)
        dy0 = (gate0 * dx.astype(BF).astype(F32)).astype(BF)
        for i in range(experts):
            block = put_rows(tr0, i, cap_pad, dy0, rows).astype(BF)
            ref = disp[i] if len(disp) > 1 else disp[0].at[i]
            ref[...] = block
    if layer == 1:
        left[0] = h1_ref[...]
        left[1] = ctx_ref[...]
        left[2] = h1_0[...]
        left[3] = ctx_0[...]
    place = meta[4]
    for m in range(4):
        target = place ^ m
        factors[m][0:rows] = right[target]
        if layer == 1:
            which = jnp.where(target == 3, 1, 0)
            factors[m][rows:2 * rows] = left[which]
            factors[m][2 * rows:] = left[2 + which]


def pack_kernel(n, cap, parts, *refs):
    out = refs[-1]
    blocks = refs[:-1]
    packed = out.shape[-2]
    cap_pad = blocks[0].shape[-2]
    for part in range(parts):
        total = None
        for i in range(n):
            block = blocks[i][part] if len(blocks) > 1 else blocks[0][i, part]
            row = lax.broadcasted_iota(jnp.int32, (packed, cap_pad), 0)
            slot = lax.broadcasted_iota(jnp.int32, (packed, cap_pad), 1)
            pick = ((row == slot + i * cap) & (slot < cap)).astype(BF)
            moved = mm(pick, block)
            total = moved if total is None else total + moved
        out[part] = total.astype(BF)


def unpack_kernel(n, cap, parts, *refs):
    sums, outs = refs[:4], refs[4:]
    packed = sums[0].shape[-2]
    cap_pad = outs[0].shape[-2]
    for part in range(parts):
        total = (
            sums[0][part].astype(F32)
            + sums[1][part].astype(F32)
            + sums[2][part].astype(F32)
            + sums[3][part].astype(F32)
        ).astype(BF)
        for i in range(n):
            row = lax.broadcasted_iota(jnp.int32, (cap_pad, packed), 1)
            slot = lax.broadcasted_iota(jnp.int32, (cap_pad, packed), 0)
            pick = ((row == slot + i * cap) & (slot < cap)).astype(BF)
            block = mm(pick, total).astype(BF)
            if len(outs) > 1:
                outs[i][part] = block
            else:
                outs[0][i, part] = block


def expert_weights(layer, meta, own, other, scr, sem):
    for which in range(2):
        @pl.when(meta[0] == layer)
        def _():
            pltpu.make_async_copy(own[which], scr.at[which], sem.at[which]).start()

        @pl.when(meta[0] != layer)
        def _():
            pltpu.make_async_copy(other[which], scr.at[which], sem.at[which]).start()

    def wait(which):
        pltpu.make_async_copy(own[which], scr.at[which], sem.at[which]).wait()

    return wait


def expert_forward_kernel(layer, both, *refs):
    meta, c0, c1, c2, c3, in_own, in_other, out_own, out_other = refs[:9]
    outs = refs[9:13]
    count = (len(refs) - 16) // 2
    kept = refs[13:13 + count]
    scr, sem = refs[13 + count:15 + count]
    saved, keep_sem = refs[15 + count:-1], refs[-1]

    def save(n, values):
        saved[n][...] = values
        pltpu.make_async_copy(saved[n], kept[n], keep_sem.at[n]).start()

    wait = expert_weights(layer, meta, (in_own, out_own), (in_other, out_other), scr, sem)
    packed = c0.shape[-2]
    rows = jnp.concatenate([c[0] for c in (c0, c1, c2, c3)], axis=0)
    wait(0)
    pre = mm(rows, scr[0])
    act = gelu(pre).astype(BF)
    save(0, rows)
    save(1, act)
    wait(1)
    y = mm(act, scr[1])
    for m in range(4):
        outs[m][0] = y[m * packed:(m + 1) * packed].astype(BF)
    if both:
        grad_rows = jnp.concatenate([c[1] for c in (c0, c1, c2, c3)], axis=0)
        dpre = (mm_nt(grad_rows, scr[1]) * gelu_slope(pre)).astype(BF)
        save(2, grad_rows)
        save(3, dpre)
        dh = mm_nt(dpre, scr[0])
        for m in range(4):
            outs[m][1] = dh[m * packed:(m + 1) * packed].astype(BF)
    else:
        save(2, pre)
    for n in range(count):
        pltpu.make_async_copy(saved[n], kept[n], keep_sem.at[n]).wait()


def expert_backward_kernel(layer, *refs):
    meta, c0, c1, c2, c3, in_own, in_other, out_own, out_other, pre_ref = refs[:10]
    outs = refs[10:14]
    kept, scr, sem, saved, keep_sem = refs[14:16], refs[16], refs[17], refs[18:20], refs[20]

    def copy_out(n):
        return pltpu.make_async_copy(saved[n], kept[n], keep_sem.at[n])

    wait = expert_weights(layer, meta, (in_own, out_own), (in_other, out_other), scr, sem)
    packed = c0.shape[-2]
    grad_rows = jnp.concatenate([c[0] for c in (c0, c1, c2, c3)], axis=0)
    saved[0][...] = grad_rows
    copy_out(0).start()
    slope = gelu_slope(pre_ref[...])
    wait(1)
    dpre = (mm_nt(grad_rows, scr[1]) * slope).astype(BF)
    saved[1][...] = dpre
    copy_out(1).start()
    wait(0)
    dh = mm_nt(dpre, scr[0])
    for m in range(4):
        outs[m][0] = dh[m * packed:(m + 1) * packed].astype(BF)
    copy_out(0).wait()
    copy_out(1).wait()


def bring_layer(layer_is, sets, scr, sem):
    for layer in range(2):
        @pl.when(layer_is == layer)
        def _():
            for n in range(4):
                pltpu.make_async_copy(sets[layer][n], scr[n], sem.at[n]).start()

    def wait(n):
        pltpu.make_async_copy(sets[0][n], scr[n], sem.at[n]).wait()

    return wait


def expert_send_kernel(meta, *refs):
    sets, out, scr, sem = (refs[0:4], refs[4:8]), refs[8], refs[9:13], refs[13]
    wait = bring_layer(1 - meta[0], sets, scr, sem)
    wait(0)
    wait(1)
    out[0] = mm_tn(scr[0][...], scr[1][...]).astype(BF)
    wait(2)
    wait(3)
    out[1] = mm_tn(scr[2][...], scr[3][...]).astype(BF)


def expert_own_kernel(meta, *refs):
    sets, got, gin, gout, scr, sem = (
        (refs[0:4], refs[4:8]), refs[8], refs[9], refs[10], refs[11:15], refs[15],
    )
    wait = bring_layer(meta[0], sets, scr, sem)
    wait(0)
    wait(1)
    gin[...] = mm_tn(scr[0][...], scr[1][...]) + got[0].astype(F32)
    wait(2)
    wait(3)
    gout[...] = mm_tn(scr[2][...], scr[3][...]) + got[1].astype(F32)


def factor_kernel(experts, slab, rows, split, meta, *refs):
    rights, lefts, ex, keep, send = refs[0:4], refs[4:8], refs[8], refs[9], refs[10]
    right = jnp.concatenate([f[0:rows] for f in rights], axis=0)
    left = jnp.concatenate([f[split:split + rows] for f in lefts], axis=0)
    grad = mm_tn(left, right).astype(BF)
    s, z = meta[0], meta[2]
    extra = ex[...]
    pad = jnp.zeros((16, grad.shape[1] - LANES), F32)
    for shard in range(2 * experts):
        at = lax.rem(shard // 2 - z + experts, experts)
        wide = jnp.concatenate(
            [extra[:, shard * slab:(shard + 1) * slab], jnp.zeros((16, LANES - slab), F32)], axis=1
        )
        block = jnp.concatenate([wide, pad], axis=1).astype(BF)

        @pl.when(s == shard % 2)
        def _():
            keep[at, 0:slab] = grad[shard * slab:(shard + 1) * slab]
            keep[at, slab:] = block

        @pl.when(s != shard % 2)
        def _():
            send[at, 0:slab] = grad[shard * slab:(shard + 1) * slab]
            send[at, slab:] = block


def finish_kernel(experts, slab, table_slab, meta, *refs):
    arrived, (qkv, out, router, gains, table) = refs[:4], refs[4:]
    s, x = meta[0], meta[1]
    extra = None
    for a in range(2):
        for b in range(2):
            block = arrived[2 * a + b]
            matrix = 2 * (x ^ b) + (s ^ a)
            main = block[0:slab].astype(F32)

            @pl.when(matrix == 3)
            def _():
                out[0] = main

            @pl.when(matrix != 3)
            def _():
                qkv[0, matrix] = main

            small = block[slab:, 0:LANES].astype(F32)
            extra = small if extra is None else extra + small
    router[0] = extra[0:experts, 0:slab]
    gains[0] = extra[experts:experts + 2, 0:slab]
    table[...] = extra[experts + 2:experts + 3, 0:table_slab]


def call(
    kernel, out_shapes, args, specs, scratch=(), us=1, name=None, vmem=62, hbm=0
):
    return pl.pallas_call(
        kernel,
        out_shape=[jax.ShapeDtypeStruct(shape, dtype) for shape, dtype in out_shapes],
        in_specs=specs,
        out_specs=[VM] * (len(out_shapes) - hbm) + [HBM] * hbm,
        scratch_shapes=list(scratch),
        compiler_params=pltpu.CompilerParams(vmem_limit_bytes=vmem * 2**20),
        cost_estimate=pl.CostEstimate(
            flops=us * 10**9, bytes_accessed=us * 3 * 10**6, transcendentals=0
        ),
        name=name,
    )(*args)


def shift(v, axis, by):
    n = lax.axis_size(axis)
    return lax.ppermute(v, axis, [(i, (i + by) % n) for i in range(n)])


def after(values, *events):
    values = tuple(values)
    return list(lax.optimization_barrier(values + events)[: len(values)])


def swap_section(v):
    return lax.ppermute(v, "section", [(0, 1), (1, 0)])


def plane_swap(v, mask):
    return lax.ppermute(v, PLANE, [(i, i ^ mask) for i in range(4)])


def plane_gather(v):
    return [v] + [plane_swap(v, m) for m in (1, 2, 3)]


def local(
    experts,
    boundary,
    seq_lengths,
    routes,
    qkv_proj,
    out_proj,
    router,
    gains,
    rel_table,
    expert_in,
    expert_out,
):
    big = experts > 8
    s = lax.axis_index("section")
    x_at = lax.axis_index("rep")
    z_at = lax.axis_index("expert")
    y_at = lax.axis_index("half")
    shards = 2 * experts
    rows, width = boundary.shape[2:]
    slab = qkv_proj.shape[2]
    table_slab = rel_table.shape[1]
    cap = max(2, rows // experts + 1)
    cap_pad = up(cap, 8)
    packed = up(experts * cap, 16)
    ff = expert_in.shape[3]
    first = s == 0

    own = boundary[0]
    got = swap_section(own[1 - s])
    x0 = jnp.where(first, own[0], got)
    g1 = jnp.where(first, got, own[1])
    lengths = seq_lengths[s, 0]
    place = jnp.stack([s, x_at, z_at, y_at, 2 * x_at + y_at]).astype(jnp.int32)
    meta = jnp.concatenate([place, lengths])
    own_routes = routes[0, :, :, 0]
    got_routes = swap_section(own_routes[1 - s])
    route_list = [
        jnp.where(first, own_routes[0], got_routes),
        jnp.where(first, got_routes, own_routes[1]),
    ]

    early = ()
    if big:
        slabs = jnp.concatenate([qkv_proj[0], out_proj], axis=0)
        whole = lax.all_gather(slabs, ("expert", "half"), axis=1, tiled=True)
        layers = lax.all_gather(whole, "section", axis=0)
        attn_w = [[layers[0]], [layers[1]]]
        plan = []
    else:
        slabs = jnp.concatenate([qkv_proj[0], out_proj], axis=0)
        piece = lax.dynamic_slice_in_dim(slabs, 2 * x_at, 2, axis=0)
        along = {1: shift(piece, "expert", 1), 3: shift(piece, "expert", 3)}
        over_y0 = plane_swap(piece, 1)
        along[2] = shift(after([piece], along[1])[0], "expert", 2)
        over = {1: (plane_swap(along[1], 1), plane_swap(along[1], 2))}
        early = (over[1][0],)

    small_rows = up(experts + 3, 8)
    table_row = jnp.pad(rel_table, ((0, 0), (0, slab - table_slab)))
    small = jnp.concatenate(
        [
            router[0].T,
            gains[0],
            table_row,
            jnp.zeros((small_rows - experts - 3, slab), BF),
        ]
    )
    (small,) = after([small], *early)
    if big:
        small_all = lax.all_gather(
            lax.all_gather(small, ("expert", "half"), axis=0), "section", axis=0
        )
    else:
        lines = jnp.stack([small] + [shift(small, "expert", i) for i in range(1, experts)])
        lines = jnp.stack([lines, shift(lines, "half", 1)])
        small_all = jnp.stack([lines, swap_section(lines)])
    head_of, offset_of = table_places(shards, slab, table_slab)
    flip = jnp.asarray(np.eye(2 * rows)[::-1], BF)
    rr = jnp.stack(route_list)
    common = [meta, small_all, rr.T, rr, head_of, offset_of]

    if not big:
        pieces, plan = [slabs], [(0, 0, 0, 0, 4)]
        pieces += [over_y0, plane_swap(over_y0, 2)]
        plan += [(0, 1, 0, 0, 2), (0, 1, 1, 0, 2)]
        for i in (1, 3, 2):
            got = along[i]
            if i == 2:
                got, x0, g1, meta_, *common = after([got, x0, g1, common[0]] + common[2:])
                common = [meta_, small_all] + common
            over_y, over_x = over[i] if i in over else (plane_swap(got, 1), plane_swap(got, 2))
            pieces += [got, over_y, over_x]
            plan += [(i, 0, 0, 0, 2), (i, 1, 0, 0, 2), (i, 0, 1, 0, 2)]
            if i == 1:
                pieces.append(plane_swap(over_y, 2))
                plan.append((i, 1, 1, 0, 2))
            elif i == 3:
                pieces.append(plane_swap(over_x, 1))
                plan.append((i, 1, 1, 0, 2))
            else:
                pieces += [plane_swap(over_y[:1], 2), plane_swap(over_x[1:], 1)]
                plan += [(i, 1, 1, 0, 1), (i, 1, 1, 1, 1)]
        held_back = after(pieces[:7], pieces[9])
        copied = [swap_section(v) for v in held_back + pieces[7:]]
        attn_w = [pieces + copied] * 2

    n_w = len(attn_w[0])
    n_ret = 1 if big else experts

    def message_shapes(parts):
        if big:
            return [((experts,) + parts + (cap_pad, width), BF)]
        return [(parts + (cap_pad, width), BF)] * experts

    def dispatch(blocks, parts):
        if big:
            arrived = lax.all_to_all(blocks[0], "expert", 0, 0, tiled=True)
            arrived = [arrived if parts == 2 else arrived[:, None]]
        else:
            arrived = [blocks[0]] + [shift(blocks[i], "expert", i) for i in range(1, experts)]
            arrived = arrived if parts == 2 else [a[None] for a in arrived]
        (joined,) = call(
            functools.partial(pack_kernel, experts, cap, parts),
            [((parts, packed, width), BF)],
            arrived,
            [VM] * len(arrived),
            us=1,
            name="pack",
            vmem=8,
        )
        return plane_gather(joined)

    def come_back(partial, parts, events=()):
        sums = [partial[0]] + [plane_swap(partial[m], m) for m in (1, 2, 3)]
        if events:
            sums = after(sums, *events)
        shapes = (
            [((experts, parts, cap_pad, width), BF)]
            if big
            else [((parts, cap_pad, width), BF)] * experts
        )
        blocks = call(
            functools.partial(unpack_kernel, experts, cap, parts),
            shapes,
            sums,
            [VM] * 4,
            us=1,
            name="unpack",
            vmem=8,
        )
        if big:
            back = lax.all_to_all(blocks[0], "expert", 0, 0, tiled=True)
            return [back if parts == 2 else back[:, 0]]
        back = [blocks[0]] + [shift(blocks[i], "expert", -i) for i in range(1, experts)]
        return back if parts == 2 else [b[0] for b in back]

    def forward(layer, extra):
        args = common + extra
        specs = [SM] + [VM] * (len(args) - 1) + [ANY] * n_w
        shapes = [
            ((rows, width), BF),
            ((3, rows, width), BF),
            ((PAIRS, 2 * rows, rows), F32),
            ((rows, width), BF),
            ((rows, width), F32),
            ((rows, width), BF),
            ((rows, experts), F32),
        ]
        if layer == 1:
            shapes += [((rows, width), BF), ((rows, width), F32)]
        fixed = len(shapes)
        shapes += message_shapes((2,) if layer == 1 else ())
        outs = call(
            functools.partial(forward_kernel, layer, experts, slab, cap_pad, n_ret, n_w, plan),
            shapes,
            args + attn_w[layer],
            specs,
            Weights.scratch(plan, width),
            us=6,
            name="attention_forward",
        )
        names = ["h1", "qkv", "p", "ctx", "mid", "h2", "probs", "x1", "y0"][:fixed]
        return dict(zip(names, outs[:fixed])), outs[fixed:]

    def backward(layer, kept, x_in, g, returned, extra):
        args = common + [flip, g, x_in] + [
            kept[n] for n in ("h1", "qkv", "p", "ctx", "mid", "h2", "probs")
        ]
        args += extra + returned
        specs = [SM] + [VM] * (len(args) - 1) + [ANY] * n_w
        shapes = [
            ((rows, width), F32),
            ((up(experts + 3, 16), width), F32),
        ] + [(((3 if layer == 1 else 1) * rows, width), BF)] * 4
        if layer == 1:
            shapes += [((rows, width), F32)] + message_shapes(())
        return call(
            functools.partial(backward_kernel, layer, experts, slab, cap_pad, n_ret, n_w, plan),
            shapes,
            args + attn_w[layer],
            specs,
            Weights.scratch(plan, width)
            + [
                pltpu.VMEM((4, rows, width), BF),
                pltpu.VMEM((4, rows, width), BF),
                pltpu.VMEM((16, LANES), F32),
            ],
            us=8 if layer else 2,
            name="attention_backward",
        )

    expert_scratch = [pltpu.VMEM((2, width, ff), BF), pltpu.SemaphoreType.DMA((2,))]
    expert_specs = [SM] + [VM] * 4 + [ANY] * 4
    all_rows = 4 * packed

    def expert_forward(layer, joined, both):
        parts = 2 if both else 1
        shapes = [((parts, packed, width), BF)] * 4
        shapes += [((all_rows, width), BF), ((all_rows, ff), BF)]
        shapes += (
            [((all_rows, width), BF), ((all_rows, ff), BF)] if both else [((all_rows, ff), F32)]
        )
        outs = call(
            functools.partial(expert_forward_kernel, layer, both),
            shapes,
            [meta] + joined + expert_w,
            expert_specs,
            expert_scratch
            + [pltpu.VMEM(*shape) for shape in shapes[4:]]
            + [pltpu.SemaphoreType.DMA((len(shapes) - 4,))],
            hbm=len(shapes) - 4,
            us=4,
            name="expert_forward",
            vmem=20,
        )
        return outs[:4], outs[4:]

    def plane_factors(factors):
        return [factors[0]] + [plane_swap(factors[m], m) for m in (1, 2, 3)]

    def attention_grads(rights, lefts, split, ex):
        keep, send = call(
            functools.partial(factor_kernel, experts, slab, rows, split),
            [((experts, slab + 16, width), BF)] * 2,
            [meta] + rights + lefts + [ex],
            [SM] + [VM] * 9,
            us=4,
            name="attention_grads",
            vmem=20,
        )
        return keep, send

    def sum_cores(keep, send):
        both = keep.astype(F32) + swap_section(send).astype(F32)
        return [both[i].astype(BF) for i in range(experts)]

    def along_z(parts):
        return [parts[0]] + [shift(parts[i], "expert", i) for i in range(1, experts)]

    def add_up(parts):
        total = parts[0].astype(F32)
        for part in parts[1:]:
            total = total + part.astype(F32)
        return total.astype(BF)

    kept0, blocks = forward(0, [x0])
    w_in, w_out = after([expert_in[0, 0], expert_out[0, 0]], kept0["probs"])
    expert_w = [w_in, swap_section(w_in), w_out, swap_section(w_out)]
    joined = dispatch(blocks, 1)
    partial, (rows0, act0, pre0) = expert_forward(0, joined, False)
    returned = come_back(partial, 1)

    kept1, blocks = forward(1, [kept0["mid"], kept0["probs"], g1] + returned)
    joined = dispatch(blocks, 2)
    partial, (rows1, act1, grows1, dpre1) = expert_forward(1, joined, True)
    returned = come_back(partial, 2)

    outs = backward(
        1, kept1, kept1["x1"], g1, returned, [kept0["probs"], kept0["h1"], kept0["ctx"]]
    )
    dx1, ex1 = outs[:2]
    factors1, out1, blocks = outs[2:6], outs[6], outs[7:]

    joined = dispatch(blocks, 1)
    shapes = [((1, packed, width), BF)] * 4 + [((all_rows, width), BF), ((all_rows, ff), BF)]
    outs = call(
        functools.partial(expert_backward_kernel, 0),
        shapes,
        [meta] + joined + expert_w + [pre0],
        expert_specs + [VM],
        expert_scratch
        + [pltpu.VMEM(*shape) for shape in shapes[4:]]
        + [pltpu.SemaphoreType.DMA((2,))],
        hbm=2,
        us=4,
        name="expert_backward",
            vmem=20,
    )
    partial, (grows0, dpre0) = outs[:4], outs[4:]
    if not big:
        beside = plane_factors(factors1)
        beside = after(beside, partial[3])
        halves1 = attention_grads(beside, beside, rows, ex1)
        returned = come_back(partial, 1, halves1)
        moved1 = along_z(after(sum_cores(*halves1), returned[0]))
    else:
        returned = come_back(partial, 1)
    outs = backward(0, kept0, x0, dx1.astype(BF), returned, [kept1["y0"]])
    dx0, ex0 = outs[:2]
    factors0 = outs[2:6]
    if not big:
        factors0 = after(factors0, *moved1)
        rights0 = plane_factors(factors0)
        halves0 = attention_grads(rights0, beside, 2 * rows, ex0)
        parts0 = sum_cores(*halves0)
        moved0 = along_z(parts0)

    traded = swap_section(jnp.where(first, out1, dx0))
    result_rows = jnp.stack([jnp.where(first, dx0, traded), jnp.where(first, traded, out1)])

    sets = [rows0, dpre0, act0, grows0, rows1, dpre1, act1, grows1]
    if not big:
        sets = after(sets, dx0)
    bring_scratch = [
        pltpu.VMEM((all_rows, width), BF),
        pltpu.VMEM((all_rows, ff), BF),
        pltpu.VMEM((all_rows, ff), BF),
        pltpu.VMEM((all_rows, width), BF),
        pltpu.SemaphoreType.DMA((4,)),
    ]
    (sent,) = call(
        expert_send_kernel,
        [((2, width, ff), BF)],
        [meta] + sets,
        [SM] + [ANY] * 8,
        bring_scratch,
        us=5,
        name="expert_gradients_sent",
    )
    got = swap_section(sent)

    def own_experts(sets, got):
        return call(
            expert_own_kernel,
            [((width, ff), F32), ((ff, width), F32)],
            [meta] + sets + [got],
            [SM] + [ANY] * 8 + [VM],
            bring_scratch,
            us=6,
            name="expert_gradients_own",
        )

    traded = swap_section(jnp.where(first, out1, dx0))
    result_rows = jnp.stack([jnp.where(first, dx0, traded), jnp.where(first, traded, out1)])

    if big:
        own_factors = []
        for kept, ex, fac in ((kept0, ex0, factors0), (kept1, ex1, factors1)):
            spot = 2 * x_at + y_at
            right = jnp.stack([fac[m][:rows] for m in range(4)])
            pieces = [
                jnp.sum(
                    jnp.where(
                        (jnp.arange(4) ^ spot == j)[:, None, None], right, jnp.zeros_like(right)
                    ),
                    axis=0,
                )
                for j in range(4)
            ]
            lefts = [kept["h1"]] * 3 + [kept["ctx"]]
            grad = jnp.stack(
                [
                    lax.dot_general(
                        a, b, (((0,), (0,)), ((), ())), preferred_element_type=F32
                    )
                    for a, b in zip(lefts, pieces)
                ]
            )
            own_factors.append((grad, ex[:experts + 3]))
        grad = jnp.stack([own_factors[0][0], own_factors[1][0]]).astype(BF)
        lines = jnp.stack([own_factors[0][1], own_factors[1][1]])
        grad = lax.psum_scatter(grad, "section", scatter_dimension=0)
        lines = lax.psum_scatter(lines, "section", scatter_dimension=0)
        grad = lax.psum_scatter(grad, ("expert", "half"), scatter_dimension=1, tiled=True)
        grad = lax.psum(grad, "rep").astype(F32)
        lines = lax.psum(lines, ("rep", "expert", "half"))
        shard_at = z_at * 2 + y_at
        extra = lax.dynamic_slice_in_dim(lines, shard_at * slab, slab, axis=1)
        smalls = (
            grad[None, :3],
            grad[3][None],
            extra[:experts].T[None],
            extra[experts:experts + 2][None],
            extra[experts + 2, :table_slab][None],
        )
        final_in, final_out = own_experts(sets, got)
    else:
        final_in, final_out = own_experts(after(sets, *parts0), got)
        moved0 = after(moved0, final_in)
        blocks = [add_up(moved0), add_up(moved1)]
        arrived = []
        trade = ("section", "rep", "half")
        for a in range(2):
            message = jnp.where((y_at ^ a) == 0, blocks[0], blocks[1])
            for b in range(2):
                pairs = []
                for i in range(8):
                    si, xi, yi = i // 4, (i // 2) % 2, i % 2
                    pairs.append((i, (yi ^ a) * 4 + (xi ^ b) * 2 + si))
                arrived.append(lax.ppermute(message, trade, pairs))
        smalls = list(call(
            functools.partial(finish_kernel, experts, slab, table_slab),
            [
                ((1, 3, slab, width), F32),
                ((1, slab, width), F32),
                ((1, experts, slab), F32),
                ((1, 2, slab), F32),
                ((1, table_slab), F32),
            ],
            [meta] + arrived,
            [SM] + [VM] * 4,
            us=2,
            name="finish",
            vmem=8,
        ))
        smalls[2] = smalls[2].transpose(0, 2, 1)
    return (result_rows[None], *smalls, final_in[None, None], final_out[None, None])


def solution(mesh):
    sections, reps, shards = (mesh.shape[n] for n in ("section", "rep", "shard"))
    experts = shards // 2
    split = Mesh(
        mesh.devices.reshape(sections, reps, experts, 2), ("section", "rep", "expert", "half")
    )
    shard = ("expert", "half")
    in_specs = (
        P("section", None, ("rep",) + shard, None),
        P(None, ("rep",) + shard, None),
        P("section", None, ("rep",) + shard, None),
        P("section", None, shard, None),
        P("section", shard, None),
        P("section", shard, None),
        P("section", None, shard),
        P("section", shard),
        P("section", shard, None, "rep"),
        P("section", shard, "rep", None),
    )
    out_specs = (
        P("section", None, ("rep",) + shard, None),
        P("section", None, shard, None),
        P("section", shard, None),
        P("section", shard, None),
        P("section", None, shard),
        P("section", shard),
        P("section", shard, None, "rep"),
        P("section", shard, "rep", None),
    )
    return jax.shard_map(
        functools.partial(local, experts),
        mesh=split,
        in_specs=in_specs,
        out_specs=out_specs,
        check_vma=False,
    )
```
